32 devices in a mesh: fsdp: 4 (over x, core), ctx: 2 (over y), tp: 4 (over z).
Axes of the slice: x: 2, y: 2, z: 4, core: 2. Of those that a mesh axis runs over, the one named last changes fastest.
Arguments:
- tokens: bfloat16 [8192, 1024], P(('fsdp', 'ctx')), may hold values from -6 to 6
- cotangent: bfloat16 [8192, 1024], P(('fsdp', 'ctx')), may hold values from -6 to 6
- routes: int32 [8192, 2], P(('fsdp', 'ctx')), may hold values from 0 to 7, all different within a row; in each aligned block of 1024 rows (0 to 1023, 1024 to 2047, ...) at most 320 rows name the same one
- buckets: int32 [4095], replicated, may hold values from 0 to 31
- attention_in: float32 [3, 1024, 1024], P(None, ('fsdp', 'ctx'), 'tp'), may hold values from -0.1875 to 0.1875
- attention_out: float32 [1024, 1024], P('tp', ('fsdp', 'ctx')), may hold values from -3.5 to 3.5
- router: float32 [1024, 8], P(('fsdp', 'ctx')), may hold values from -0.125 to 0.125
- gains: float32 [2, 1024], P(None, ('fsdp', 'ctx')), may hold values from 0.5 to 1.5
- bias_table: float32 [32, 16], P(('fsdp', 'ctx'), 'tp'), may hold values from -6 to 6
- expert_in: float32 [8, 1024, 2, 2816], P(('fsdp', 'ctx'), None, None, 'tp'), may hold values from -0.1875 to 0.1875
- expert_out: float32 [8, 2816, 1024], P(('fsdp', 'ctx'), 'tp'), may hold values from -0.21875 to 0.21875
- attention_in_left: float32 [2, 3, 4096, 128], P(None, None, ('fsdp', 'ctx', 'tp')), as said below
- attention_in_right: float32 [2, 3, 8192, 256], P(None, None, ('fsdp', 'ctx', 'tp')), as said below
- attention_out_left: float32 [2, 8192, 256], P(None, ('fsdp', 'ctx', 'tp')), as said below
- attention_out_right: float32 [2, 4096, 128], P(None, ('fsdp', 'ctx', 'tp')), as said below
- expert_in_left: float32 [2, 32768, 1024], P(None, ('fsdp', 'ctx', 'tp')), as said below
- expert_in_right: float32 [2, 45056, 1408], P(None, ('fsdp', 'ctx', 'tp')), as said below
- expert_out_left: float32 [2, 22528, 704], P(None, ('fsdp', 'ctx', 'tp')), as said below
- expert_out_right: float32 [2, 32768, 1024], P(None, ('fsdp', 'ctx', 'tp')), as said below
- router_moment: float32 [1024, 8], P(('fsdp', 'ctx')), may hold values from 262144 to 1048576
- gains_moment: float32 [2, 1024], P(None, ('fsdp', 'ctx')), may hold values from 16384 to 65536
- table_moment: float32 [32, 16], P(('fsdp', 'ctx'), 'tp'), may hold values from 5461 to 21844
Outputs:
- output: bfloat16 [8192, 1024], P(('fsdp', 'ctx'))
- tokens_grad: float32 [8192, 1024], P(('fsdp', 'ctx'))
- attention_in_grad: float32 [3, 1024, 1024], P(None, ('fsdp', 'ctx'), 'tp')
- attention_in_new: float32 [3, 1024, 1024], P(None, ('fsdp', 'ctx'), 'tp')
- attention_in_left_new: float32 [3, 4096, 128], P(None, ('fsdp', 'ctx', 'tp'))
- attention_in_right_new: float32 [3, 8192, 256], P(None, ('fsdp', 'ctx', 'tp'))
- attention_out_grad: float32 [1024, 1024], P('tp', ('fsdp', 'ctx'))
- attention_out_new: float32 [1024, 1024], P('tp', ('fsdp', 'ctx'))
- attention_out_left_new: float32 [8192, 256], P(('fsdp', 'ctx', 'tp'))
- attention_out_right_new: float32 [4096, 128], P(('fsdp', 'ctx', 'tp'))
- expert_in_grad: float32 [8, 1024, 2, 2816], P(('fsdp', 'ctx'), None, None, 'tp')
- expert_in_new: float32 [8, 1024, 2, 2816], P(('fsdp', 'ctx'), None, None, 'tp')
- expert_in_left_new: float32 [32768, 1024], P(('fsdp', 'ctx', 'tp'))
- expert_in_right_new: float32 [45056, 1408], P(('fsdp', 'ctx', 'tp'))
- expert_out_grad: float32 [8, 2816, 1024], P(('fsdp', 'ctx'), 'tp')
- expert_out_new: float32 [8, 2816, 1024], P(('fsdp', 'ctx'), 'tp')
- expert_out_left_new: float32 [22528, 704], P(('fsdp', 'ctx', 'tp'))
- expert_out_right_new: float32 [32768, 1024], P(('fsdp', 'ctx', 'tp'))
- router_grad: float32 [1024, 8], P(('fsdp', 'ctx'))
- router_moment_new: float32 [1024, 8], P(('fsdp', 'ctx'))
- router_new: float32 [1024, 8], P(('fsdp', 'ctx'))
- gains_grad: float32 [2, 1024], P(None, ('fsdp', 'ctx'))
- gains_moment_new: float32 [2, 1024], P(None, ('fsdp', 'ctx'))
- gains_new: float32 [2, 1024], P(None, ('fsdp', 'ctx'))
- table_grad: float32 [32, 16], P(('fsdp', 'ctx'), 'tp')
- table_moment_new: float32 [32, 16], P(('fsdp', 'ctx'), 'tp')
- table_new: float32 [32, 16], P(('fsdp', 'ctx'), 'tp')
The draws below stay inside these ranges and needn't reach their ends.
Inputs may be any that keep to these rules, and one draw needn't show every extreme that they name: `routes`: in the rows of one device the two experts of a row differ, no expert is named by more than 320 rows, a bound that some block reaches. `attention_in_left`: index 0 of the first dimension holds each block's symmetric statistic with a positive diagonal, index 1 its given symmetric inverse root. `attention_in_right`: as for attention_in_left. `attention_out_left`: as for attention_in_left. `attention_out_right`: as for attention_in_left. `expert_in_left`: as for attention_in_left. `expert_in_right`: as for attention_in_left. `expert_out_left`: as for attention_in_left. `expert_out_right`: as for attention_in_left.
All inputs are finite; a program needn't handle non-finite values.
Results may differ from the reference program's by a relative error of at most 0.034.
Values may be sent and summed in bfloat16 or wider, within the bound.
A program may use at most 832 MiB of HBM per device.

```python
import math
import jax
import jax.numpy as jnp
import numpy as np
from jax import lax

D = 1024
H = 16
DH = 64
FF = 2816
NB = 32
TOPK = 2
SEQ_DEV = 1024
HD = 1024
SHARDS = 8
GROUPS = 32
EXPERTS = 8
SEQS = 4
LEN = 2048
TOKENS = 8192
CAPACITY = 320
DS = 128
HT = 256
FT = 704
N_TP = 4


def statistic_pair(key, count, width, scale):
    first_key, second_key, third_key = jax.random.split(key, 3)
    identity = jnp.eye(width, dtype=jnp.float32)
    diagonal = scale * jax.random.uniform(first_key, (count, width), jnp.float32, 1.0, 4.0)
    noise = jax.random.uniform(second_key, (count, width, width), jnp.float32, -1.0, 1.0)
    spread = jax.random.uniform(third_key, (count, width), jnp.float32, 0.5, 2.0)
    statistic = diagonal[:, :, None] * identity
    root = (noise + jnp.swapaxes(noise, 1, 2)) * (0.6 / width ** 0.5) + spread[:, :, None] * identity
    return jnp.stack([statistic, root])


def attention_square():
    return 0.01 * TOKENS


def expert_square():
    return 0.01 * TOKENS * TOPK / EXPERTS


def draw_attention_in_left(key, part):
    key = jax.random.fold_in(key, 11)
    return statistic_pair(key, 3 * GROUPS, DS, HT * attention_square()).reshape(2, 3, GROUPS * DS, DS)


def draw_attention_in_right(key, part):
    key = jax.random.fold_in(key, 12)
    return statistic_pair(key, 3 * GROUPS, HT, DS * attention_square()).reshape(2, 3, GROUPS * HT, HT)


def draw_attention_out_left(key, part):
    key = jax.random.fold_in(key, 13)
    return statistic_pair(key, GROUPS, HT, DS * attention_square()).reshape(2, GROUPS * HT, HT)


def draw_attention_out_right(key, part):
    key = jax.random.fold_in(key, 14)
    return statistic_pair(key, GROUPS, DS, HT * attention_square()).reshape(2, GROUPS * DS, DS)


def draw_expert_in_left(key, part):
    key = jax.random.fold_in(key, 15)
    return statistic_pair(key, GROUPS, D, 2 * FT * expert_square()).reshape(2, GROUPS * D, D)


def draw_expert_in_right(key, part):
    key = jax.random.fold_in(key, 16)
    return statistic_pair(key, GROUPS, 2 * FT, D * expert_square()).reshape(2, GROUPS * 2 * FT, 2 * FT)


def draw_expert_out_left(key, part):
    key = jax.random.fold_in(key, 17)
    return statistic_pair(key, GROUPS, FT, D * expert_square()).reshape(2, GROUPS * FT, FT)


def draw_expert_out_right(key, part):
    key = jax.random.fold_in(key, 18)
    return statistic_pair(key, GROUPS, D, FT * expert_square()).reshape(2, GROUPS * D, D)


def set_ends(entries, stream_key, smallest, high):
    longest = entries.shape.index(max(entries.shape))
    spots = []
    for shift in (0, 1):
        where = [jax.random.randint(jax.random.fold_in(stream_key, axis), (), 0, length) for axis, length in enumerate(entries.shape)]
        where[longest] = (where[longest] + shift) % entries.shape[longest]
        spots.append(tuple(where))
    return entries.at[spots[0]].set(smallest).at[spots[1]].set(high)


def levels(stream_key, shape, shards, low, top_value):
    factor_of = 1.0
    for position, shards_of in shards:
        steps = jax.random.uniform(jax.random.fold_in(jax.random.fold_in(stream_key, 6), position), (shards_of,), jnp.float32, low / len(shards), top_value / len(shards))
        factor_of = factor_of * jnp.repeat(jnp.exp(steps), shape[position] // shards_of).reshape((-1,) + (1,) * (len(shape) - 1 - position))
    return factor_of


def deal_out(stream_key, own, number, rows, count, top, most, slope):
    sequence = jax.random.permutation(stream_key, count)
    heavy_load, ordinary = portions_of(count, rows * top, most, slope, True), portions_of(count, rows * top, most, slope, False)
    places = jnp.arange(count)

    def named(tallies, offset_by):
        used = int((tallies > 0).sum())
        fixed = max(1, used // 4)
        moved = fixed + (places - fixed + offset_by * (used - fixed)) % max(1, count - fixed)
        return jnp.zeros((count,), jnp.int32).at[sequence[jnp.where(places < fixed, places, moved)]].set(jnp.asarray(tallies, jnp.int32))

    tallies = jnp.where(number % 4 == 0, named(heavy_load, number // 4), named(ordinary, number - number // 4 - 1))
    mixed = jax.random.permutation(jax.random.fold_in(own, 3), count)
    donor, taker = mixed[0:count // 2 * 2:2], mixed[1:count // 2 * 2:2]
    room = jnp.minimum(tallies[donor] - 1, most - tallies[taker]) // 2
    room = jnp.where((donor == sequence[0]) | (taker == sequence[0]) | (tallies[taker] == 0), 0, jnp.maximum(room, 0))
    moved = jax.random.randint(jax.random.fold_in(own, 4), (count // 2,), 0, 1 << 20) % (room + 1)
    tallies = tallies.at[donor].add(-moved).at[taker].add(moved)
    labels = jnp.searchsorted(jnp.cumsum(tallies), jnp.arange(rows * top), side="right").astype(jnp.int32)
    table = labels.reshape(top, rows).T
    table = table[jax.random.permutation(jax.random.fold_in(own, 1), rows)]
    offset_by = jax.random.randint(jax.random.fold_in(own, 2), (rows, 1), 0, top)
    return jnp.take_along_axis(table, (jnp.arange(top)[None, :] + offset_by) % top, axis=1)


def portions_of(number_of, total, bound, slope, full):
    loads = [(1 << 20) // math.isqrt(standing ** slope) + 1 for standing in range(1, number_of + 1)]
    largest = bound if full else min(bound, max(-(-total // number_of), total * loads[0] // sum(loads)))
    least = 1 if total - largest >= number_of - 1 else 0
    holding, surplus = [largest] + [least] * (number_of - 1), total - largest - least * (number_of - 1)
    while surplus > 0:
        candidates = [i for i in range(1, number_of) if holding[i] < largest] or [i for i in range(1, number_of) if holding[i] < bound]
        whole, remaining = sum([loads[i] for i in candidates]), surplus
        for i in candidates:
            extra = min(bound - holding[i], max(1, remaining * loads[i] // whole), surplus)
            holding[i] = holding[i] + extra
            surplus = surplus - extra
    return np.array(holding)


def normal_values(stream_key, dims, deviation, limit, shards=(), kind=jnp.bfloat16):
    values = jax.random.normal(stream_key, dims, jnp.float32) * deviation
    if len(shards) > 0:
        values = levels(stream_key, dims, shards, -0.22, 0.18) * values
    return jnp.clip(values, min=-limit, max=limit).astype(kind)


def setup_inputs(seed: int = 0) -> dict:
    seeds = jax.random.split(jax.random.key(seed), 23)
    tokens = normal_values(seeds[0], (TOKENS, D), 1.0, 6.0, ((0, 8),))
    cotangent = normal_values(seeds[1], (TOKENS, D), 1.0, 6.0, ((0, 8),))
    routes_keys = jax.random.split(jax.random.fold_in(seeds[2], 1), TOKENS // SEQ_DEV)
    routes_turns = jax.random.permutation(jax.random.fold_in(seeds[2], 3), TOKENS // SEQ_DEV)
    routes = jax.vmap(lambda own, number: deal_out(jax.random.fold_in(seeds[2], 2), own, number, SEQ_DEV, EXPERTS, TOPK, CAPACITY, 1))(routes_keys, routes_turns).reshape((TOKENS, TOPK))
    buckets = set_ends(jax.random.randint(seeds[3], (2 * LEN - 1,), 0, NB), jax.random.fold_in(seeds[3], 1), 0, NB - 1).astype(jnp.int32)
    attention_in = normal_values(seeds[4], (3, D, HD), D ** -0.5, 0.1875, ((1, 8), (2, 4)), jnp.float32)
    attention_out = normal_values(seeds[5], (HD, D), (max(1, 7 * HD // LEN)) ** -0.5, 3.5, ((0, 4), (1, 8)), jnp.float32)
    router = normal_values(seeds[6], (D, EXPERTS), (2 * D) ** -0.5, 0.125, ((0, 8),), jnp.float32)
    gains = jnp.clip(1.0 + 0.1 * jax.random.normal(seeds[7], (2, D), jnp.float32), 0.5, 1.5)
    bias_table = normal_values(seeds[8], (NB, H), 1.0, 6.0, ((0, 8), (1, 4)), jnp.float32)
    expert_in = normal_values(seeds[9], (EXPERTS, D, 2, FF), D ** -0.5, 0.1875, ((0, 8), (3, 4)), jnp.float32)
    expert_out = normal_values(seeds[10], (EXPERTS, FF, D), (FF // 4) ** -0.5, 0.21875, ((0, 8), (1, 4)), jnp.float32)
    attention_in_left = draw_attention_in_left(jax.random.fold_in(seeds[22], 71), 0)
    attention_in_right = draw_attention_in_right(jax.random.fold_in(seeds[22], 71), 0)
    attention_out_left = draw_attention_out_left(jax.random.fold_in(seeds[22], 71), 0)
    attention_out_right = draw_attention_out_right(jax.random.fold_in(seeds[22], 71), 0)
    expert_in_left = draw_expert_in_left(jax.random.fold_in(seeds[22], 71), 0)
    expert_in_right = draw_expert_in_right(jax.random.fold_in(seeds[22], 71), 0)
    expert_out_left = draw_expert_out_left(jax.random.fold_in(seeds[22], 71), 0)
    expert_out_right = draw_expert_out_right(jax.random.fold_in(seeds[22], 71), 0)
    router_moment = jnp.clip(jnp.exp(math.log(1048576) - 1.3862944 * jax.random.uniform(seeds[19], (D, EXPERTS), jnp.float32) ** levels(seeds[19], (D, EXPERTS), ((0, 8),), -0.2, 0.2)), 262144.0, 1048576)
    gains_moment = jnp.clip(jnp.exp(math.log(65536.0) - 1.3862944 * jax.random.uniform(seeds[20], (2, D), jnp.float32) ** levels(seeds[20], (2, D), ((1, 8),), -0.2, 0.2)), 16384.0, 65536.0)
    table_moment = jnp.clip(jnp.exp(math.log(21844.0) - 1.3862944 * jax.random.uniform(seeds[21], (NB, H), jnp.float32) ** levels(seeds[21], (NB, H), ((0, 8), (1, 4)), -0.2, 0.2)), 5461.0, 21844.0)
    return dict(tokens=tokens, cotangent=cotangent, routes=routes, buckets=buckets, attention_in=attention_in, attention_out=attention_out, router=router, gains=gains, bias_table=bias_table, expert_in=expert_in, expert_out=expert_out, attention_in_left=attention_in_left, attention_in_right=attention_in_right, attention_out_left=attention_out_left, attention_out_right=attention_out_right, expert_in_left=expert_in_left, expert_in_right=expert_in_right, expert_out_left=expert_out_left, expert_out_right=expert_out_right, router_moment=router_moment, gains_moment=gains_moment, table_moment=table_moment)


@jax.custom_vjp
def low(v):
    return lax.optimization_barrier(v.astype(jnp.bfloat16)).astype(jnp.float32)

@jax.custom_vjp
def low_back(v):
    return v

def low_keep(v):
    return (low(v), None)

def low_pass(kept, grad):
    return (grad,)

def back_keep(v):
    return (v, None)

def back_low(kept, grad):
    return (low(grad),)
low.defvjp(low_keep, low_pass)
low_back.defvjp(back_keep, back_low)
highest = lax.Precision.HIGHEST
norm_epsilon = 1e-06
step_epsilon = 1e-06
moment_epsilon = 1e-08
clip_level = 4.0
decay = 0.5
matrix_rate = 0.3
gain_rate = 0.25
router_rate = 0.01
table_rate = 0.3

def normalize(values, gain):
    return values * lax.rsqrt(lax.optimization_barrier(jnp.mean(values * values, -1, keepdims=True)) + norm_epsilon) * gain

def gated_gelu(both):
    return jax.nn.gelu(both[..., 0, :], approximate=True) * both[..., 1, :]

def attend(query, keys, values, table_rows):
    length = query.shape[0]
    block = min(512, length)
    scale = DH ** (-0.5)

    def one_block(start):
        block_query = lax.dynamic_slice_in_dim(query, start, block, 0)
        logit = jnp.einsum('qhd,khd->hqk', block_query, keys, precision=highest) * scale
        offsets = jnp.arange(length, dtype=jnp.int32)[None, :] - (start + jnp.arange(block, dtype=jnp.int32))[:, None] + (length - 1)
        scores = low_back(logit + jnp.take(table_rows, offsets, axis=1))
        top = lax.optimization_barrier(jnp.max(scores, -1, keepdims=True))
        powers = jnp.exp(scores - top)
        shares = low(powers / lax.optimization_barrier(jnp.sum(powers, -1, keepdims=True)))
        mixed = jnp.einsum('hqk,khd->qhd', shares, values, precision=highest)
        return (mixed, lax.optimization_barrier(jnp.max(logit, axis=(1, 2))))
    starts = jnp.arange(length // block, dtype=jnp.int32) * block
    mixed, peaks = lax.map(jax.checkpoint(one_block), starts)
    return (mixed.reshape(length, H * DH), lax.optimization_barrier(jnp.max(peaks, 0)))

def place(routes):
    grouped = routes.reshape(SHARDS, SEQ_DEV * TOPK)
    hits = (grouped[..., None] == jnp.arange(EXPERTS, dtype=jnp.int32)).astype(jnp.int32)
    slots = lax.optimization_barrier(jnp.sum(hits * (jnp.cumsum(hits, 1) - 1), -1))
    sources = jnp.arange(SHARDS, dtype=jnp.int32)[:, None]
    return ((sources * EXPERTS + grouped) * CAPACITY + slots).reshape(-1)

def layer(tokens, attention_in, attention_out, router, gains, bias_table, expert_in, expert_out, routes, buckets):
    attention_in = low(attention_in)
    attention_out = low(attention_out)
    router = low(router)
    gains = low(gains)
    bias_table = low(bias_table)
    expert_in = low(expert_in)
    expert_out = low(expert_out)
    first = low(normalize(tokens, gains[0]))
    projected = low(low_back(jnp.einsum('td,kde->kte', first, attention_in, precision=highest)))
    hits = (buckets[:, None] == jnp.arange(NB, dtype=jnp.int32)[None, :]).astype(jnp.float32)
    table_rows = jnp.dot(hits, bias_table, precision=highest).T
    shaped = projected.reshape(3, SEQS, LEN, H, DH)
    mixed, peaks = lax.map(lambda trio: attend(trio[0], trio[1], trio[2], table_rows), (shaped[0], shaped[1], shaped[2]))
    mixed = low(low_back(mixed.reshape(TOKENS, H * DH)))
    middle = tokens + low_back(jnp.dot(mixed, attention_out, precision=highest))
    second = low(normalize(middle, gains[1]))
    logits = low_back(jnp.dot(second, router, precision=highest))
    picked = jnp.take_along_axis(logits, routes, 1)
    top = lax.optimization_barrier(jnp.max(picked, -1, keepdims=True))
    powers = jnp.exp(picked - top)
    weights_gate = powers / lax.optimization_barrier(jnp.sum(powers, -1, keepdims=True))
    slot_rows = place(routes)
    buffer = jnp.zeros((SHARDS * EXPERTS * CAPACITY, D), jnp.float32).at[slot_rows].set(jnp.repeat(second, TOPK, axis=0))
    arrived = low_back(buffer.reshape(SHARDS, EXPERTS, CAPACITY, D).transpose(1, 0, 2, 3))
    mixed_up = low_back(jnp.einsum('escd,edgf->escgf', arrived, expert_in, precision=highest))
    hidden = low(gated_gelu(mixed_up))
    expert_rows = low(low_back(jnp.einsum('escf,efd->escd', hidden, expert_out, precision=highest)))
    returned = expert_rows.transpose(1, 0, 2, 3).reshape(SHARDS * EXPERTS * CAPACITY, D)[slot_rows].reshape(TOKENS, TOPK, D)
    return (middle + lax.optimization_barrier(jnp.sum(weights_gate[..., None] * returned, 1)), lax.optimization_barrier(jnp.max(peaks, 0)))

def precondition(grad, master, left, right):
    new_left = decay * left[0] + (1.0 - decay) * jnp.dot(grad, grad.T, precision=highest)
    new_right = decay * right[0] + (1.0 - decay) * jnp.dot(grad.T, grad, precision=highest)
    direction = jnp.dot(jnp.dot(left[1], grad, precision=highest), right[1], precision=highest)
    size = jnp.sqrt(jnp.mean(master * master) + step_epsilon)
    step = matrix_rate * size * direction * lax.rsqrt(jnp.mean(direction * direction) + step_epsilon)
    return (new_left, new_right, master - step)

def adapt(grad, moment, master, rate):
    new_moment = decay * moment + (1.0 - decay) * grad * grad
    return (new_moment, master - rate * grad * lax.rsqrt(new_moment + moment_epsilon))

def inner_blocks(array):
    return array.reshape(3, SHARDS, DS, N_TP, HT).transpose(1, 3, 0, 2, 4).reshape(GROUPS, 3, DS, HT)

def outer_blocks(array):
    return array.reshape(N_TP, HT, SHARDS, DS).transpose(2, 0, 1, 3).reshape(GROUPS, HT, DS)

def expand_blocks(array):
    return array.reshape(EXPERTS, D, 2, N_TP, FT).transpose(0, 3, 1, 2, 4).reshape(GROUPS, D, 2 * FT)

def pairs_of(array, width):
    return array.reshape(2, GROUPS, width, width).transpose(1, 0, 2, 3)

def reference(tokens, cotangent, routes, buckets, attention_in, attention_out, router, gains, bias_table, expert_in, expert_out, attention_in_left, attention_in_right, attention_out_left, attention_out_right, expert_in_left, expert_in_right, expert_out_left, expert_out_right, router_moment, gains_moment, table_moment):
    masters = (attention_in, attention_out, router, gains, bias_table, expert_in, expert_out)

    def forward(inputs, *weights):
        return layer(inputs, *weights, routes, buckets)
    result, pull, peaks = jax.vjp(forward, tokens.astype(jnp.float32), *masters, has_aux=True)
    grad_tokens, grad_in, grad_out, grad_router, grad_gains, grad_table, grad_expand, grad_shrink = pull(cotangent.astype(jnp.float32))
    in_left_pairs = attention_in_left.reshape(2, 3, GROUPS, DS, DS).transpose(2, 1, 0, 3, 4)
    in_right_pairs = attention_in_right.reshape(2, 3, GROUPS, HT, HT).transpose(2, 1, 0, 3, 4)
    in_left, in_right, in_new = jax.vmap(jax.vmap(precondition))(inner_blocks(grad_in), inner_blocks(attention_in), in_left_pairs, in_right_pairs)
    in_new = in_new.reshape(SHARDS, N_TP, 3, DS, HT).transpose(2, 0, 3, 1, 4).reshape(3, D, H * DH)
    column = jnp.sqrt(jnp.repeat(clip_level / jnp.maximum(peaks, clip_level), DH))
    in_new = in_new * jnp.stack([column, column, jnp.ones_like(column)])[:, None, :]
    in_left = in_left.transpose(1, 0, 2, 3).reshape(3, GROUPS * DS, DS)
    in_right = in_right.transpose(1, 0, 2, 3).reshape(3, GROUPS * HT, HT)
    out_left, out_right, out_new = jax.vmap(precondition)(outer_blocks(grad_out), outer_blocks(attention_out), pairs_of(attention_out_left, HT), pairs_of(attention_out_right, DS))
    out_new = out_new.reshape(SHARDS, N_TP, HT, DS).transpose(1, 2, 0, 3).reshape(H * DH, D)
    expand_left, expand_right, expand_new = jax.vmap(precondition)(expand_blocks(grad_expand), expand_blocks(expert_in), pairs_of(expert_in_left, D), pairs_of(expert_in_right, 2 * FT))
    expand_new = expand_new.reshape(EXPERTS, N_TP, D, 2, FT).transpose(0, 2, 3, 1, 4).reshape(EXPERTS, D, 2, FF)
    shrink_left, shrink_right, shrink_new = jax.vmap(precondition)(grad_shrink.reshape(GROUPS, FT, D), expert_out.reshape(GROUPS, FT, D), pairs_of(expert_out_left, FT), pairs_of(expert_out_right, D))
    shrink_new = shrink_new.reshape(EXPERTS, FF, D)
    router_moment_new, router_new = adapt(grad_router, router_moment, router, router_rate)
    gains_moment_new, gains_new = adapt(grad_gains, gains_moment, gains, gain_rate)
    table_moment_new, table_new = adapt(grad_table, table_moment, bias_table, table_rate)
    return (result.astype(jnp.bfloat16), grad_tokens, grad_in, in_new, in_left, in_right, grad_out, out_new, out_left.reshape(GROUPS * HT, HT), out_right.reshape(GROUPS * DS, DS), grad_expand, expand_new, expand_left.reshape(GROUPS * D, D), expand_right.reshape(GROUPS * 2 * FT, 2 * FT), grad_shrink, shrink_new, shrink_left.reshape(GROUPS * FT, FT), shrink_right.reshape(GROUPS * D, D), grad_router, router_moment_new, router_new, grad_gains, gains_moment_new, gains_new, grad_table, table_moment_new, table_new)
```

```python
import functools

import jax
import jax.numpy as jnp
from jax import lax
from jax.experimental import pallas as pl
from jax.experimental.pallas import tpu as pltpu

from jax.sharding import PartitionSpec as P

DH = 64
LANES = 128
MIB = 1024 * 1024


TOPK = 2

highest = lax.Precision.HIGHEST
norm_epsilon = 1e-06
step_epsilon = 1e-06
moment_epsilon = 1e-08
clip_level = 4.0
decay = 0.5
matrix_rate = 0.3
gain_rate = 0.25
router_rate = 0.01
table_rate = 0.3


def dot_nt(left, right):
    return lax.dot_general(left, right, (((1,), (1,)), ((), ())), preferred_element_type=jnp.float32)


def dot_nn(left, right):
    return lax.dot_general(left, right, (((1,), (0,)), ((), ())), preferred_element_type=jnp.float32)


def dot_tn(left, right):
    return lax.dot_general(left, right, (((0,), (0,)), ((), ())), preferred_element_type=jnp.float32)


def half_mask(shape, half):
    lane = lax.broadcasted_iota(jnp.int32, shape, 1)
    return (lane // DH) == half


def attend_kernel(length, rows, tile, q_ref, k_ref, v_ref, line_ref, mixed_ref, log_ref, peak_ref, strip, wide):
    step = pl.program_id(1)
    span = line_ref.shape[2]

    @pl.when(step == 0)
    def _():
        for half in range(2):
            line = jnp.broadcast_to(line_ref[0, half : half + 1, :], (LANES, span))
            strip[half] = pltpu.roll(line, span - (LANES - 1), 1, stride=1, stride_axis=0)
        wide[:, :LANES] = v_ref[...]
        wide[:, LANES:] = jnp.ones((length, LANES), jnp.bfloat16)
        peak_ref[...] = jnp.full(peak_ref.shape, -jnp.inf, jnp.float32)

    query = q_ref[...]
    groups = tile // LANES
    last = rows // LANES - 1
    mixed = jnp.zeros((tile, LANES), jnp.float32)
    for half in range(2):
        mine = half_mask((tile, LANES), half)
        own = jnp.where(mine, query, jnp.zeros_like(query))
        logit = dot_nt(own, k_ref[...])
        top = jnp.max(logit, 1, keepdims=True)
        bias = []
        for group in range(groups):
            start = pl.multiple_of((last - (step * groups + group)) * LANES, LANES)
            bias.append(strip[half, :, pl.ds(start, length)])
        bias = jnp.concatenate(bias, 0) if groups > 1 else bias[0]
        powers = jnp.exp(logit + bias - top)
        both = dot_nn(powers.astype(jnp.bfloat16), wide[...])
        total = both[:, LANES:]
        mixed = jnp.where(mine, both[:, :LANES] / total, mixed)
        log_total = top + jnp.log(total)
        log_ref[0, half : half + 1, :] = log_total.T[0:1, :]
        best = jnp.max(jnp.broadcast_to(top, (tile, LANES)), 0, keepdims=True)
        peak_ref[0, half : half + 1, :] = jnp.maximum(peak_ref[0, half : half + 1, :], best)
    mixed_ref[...] = mixed.astype(jnp.bfloat16)


def attend(query, keys, values, lines):
    rows, cols = query.shape
    length = keys.shape[0]
    pairs = cols // LANES
    tile = 256 if length <= 4096 else 128
    span = lines.shape[2]
    return pl.pallas_call(
        functools.partial(attend_kernel, length, rows, tile),
        grid=(pairs, rows // tile),
        in_specs=[
            pl.BlockSpec((tile, LANES), lambda p, t: (t, p)),
            pl.BlockSpec((length, LANES), lambda p, t: (0, p)),
            pl.BlockSpec((length, LANES), lambda p, t: (0, p)),
            pl.BlockSpec((1, 2, span), lambda p, t: (p, 0, 0)),
        ],
        out_specs=[
            pl.BlockSpec((tile, LANES), lambda p, t: (t, p)),
            pl.BlockSpec((1, 2, tile), lambda p, t: (p, 0, t)),
            pl.BlockSpec((1, 2, LANES), lambda p, t: (p, 0, 0)),
        ],
        out_shape=[
            jax.ShapeDtypeStruct((rows, cols), jnp.bfloat16),
            jax.ShapeDtypeStruct((pairs, 2, rows), jnp.float32),
            jax.ShapeDtypeStruct((pairs, 2, LANES), jnp.float32),
        ],
        scratch_shapes=[
            pltpu.VMEM((2, LANES, span), jnp.float32),
            pltpu.VMEM((length, 2 * LANES), jnp.bfloat16),
        ],
        compiler_params=pltpu.CompilerParams(vmem_limit_bytes=56 * MIB),
        cost_estimate=pl.CostEstimate(flops=16 * rows * length * cols, bytes_accessed=8 * length * cols, transcendentals=rows * length * cols // DH),
    )(query, keys, values, lines)


def attend_back_kernel(length, rows, tile, chunk, q_ref, k_ref, v_ref, g_ref, m_ref, log_ref, line_ref, dq_ref, dk_ref, dv_ref, sums_ref, strip, gather):
    step = pl.program_id(1)
    steps = pl.num_programs(1)
    span = line_ref.shape[2]
    last = length // LANES - 1

    @pl.when(step == 0)
    def _():
        for half in range(2):
            line = jnp.broadcast_to(line_ref[0, half : half + 1, :], (LANES, span))
            strip[half] = pltpu.roll(line, span - LANES, 1, stride=1, stride_axis=0)
        gather[...] = jnp.zeros_like(gather)
        dk_ref[...] = jnp.zeros_like(dk_ref)
        dv_ref[...] = jnp.zeros_like(dv_ref)

    query = q_ref[...]
    grad = g_ref[...]
    product = grad.astype(jnp.float32) * m_ref[...].astype(jnp.float32)
    owns, grads, deltas, logs = [], [], [], []
    for half in range(2):
        mine = half_mask((tile, LANES), half)
        owns.append(jnp.where(mine, query, jnp.zeros_like(query)))
        grads.append(jnp.where(mine, grad, jnp.zeros_like(grad)))
        picks = half_mask((8, LANES), half).astype(jnp.float32)
        deltas.append(
            lax.dot_general(picks, product, (((1,), (1,)), ((), ())), precision=lax.Precision.HIGHEST, preferred_element_type=jnp.float32)[0:1, :]
        )
        logs.append(log_ref[0, half : half + 1, :])

    def one_chunk(number, carry):
        outs = []
        base = pl.multiple_of(number * chunk, chunk)
        keys = k_ref[pl.ds(base, chunk), :]
        values = v_ref[pl.ds(base, chunk), :]
        new_key = dk_ref[pl.ds(base, chunk), :]
        new_value = dv_ref[pl.ds(base, chunk), :]
        for half in range(2):
            logit = dot_nt(keys, owns[half])
            places = []
            bias = []
            for group in range(chunk // LANES):
                row_group = number * (chunk // LANES) + group
                start = pl.multiple_of((last - row_group) * LANES + step * tile, LANES)
                places.append(start)
                bias.append(strip[half, :, pl.ds(start, tile)])
            bias = jnp.concatenate(bias, 0) if len(bias) > 1 else bias[0]
            shares = jnp.exp(logit + bias - logs[half])
            grad_shares = dot_nt(values, grads[half])
            scores = shares * (grad_shares - deltas[half])
            low_shares = shares.astype(jnp.bfloat16)
            low_scores = scores.astype(jnp.bfloat16)
            new_value = new_value + dot_nn(low_shares, grads[half])
            new_key = new_key + dot_nn(low_scores, owns[half])
            outs.append(carry[half] + dot_tn(low_scores, keys))
            for group, start in enumerate(places):
                gather[half, :, pl.ds(start, tile)] += scores[group * LANES : (group + 1) * LANES]
        dk_ref[pl.ds(base, chunk), :] = new_key
        dv_ref[pl.ds(base, chunk), :] = new_value
        return tuple(outs)

    zero = jnp.zeros((tile, LANES), jnp.float32)
    first, second = lax.fori_loop(0, length // chunk, one_chunk, (zero, zero))
    both = jnp.where(half_mask((tile, LANES), 0), first, second)
    dq_ref[...] = (both * (DH**-0.5)).astype(dq_ref.dtype)

    @pl.when(step == steps - 1)
    def _():
        for half in range(2):
            values = gather[half]
            size = LANES // 2
            while size >= 1:
                values = values[:size] + pltpu.roll(values[size : 2 * size], span - size, 1)
                size //= 2
            sums_ref[0, half : half + 1, :] = pltpu.roll(jnp.broadcast_to(values, (8, span)), LANES, 1)[0:1]


def attend_back(query, keys, values, grad, mixed, logs, lines):
    rows, cols = query.shape
    length = keys.shape[0]
    pairs = cols // LANES
    tile = 256
    chunk = 512
    span = lines.shape[2]
    return pl.pallas_call(
        functools.partial(attend_back_kernel, length, rows, tile, chunk),
        grid=(pairs, rows // tile),
        in_specs=[
            pl.BlockSpec((tile, LANES), lambda p, t: (t, p)),
            pl.BlockSpec((length, LANES), lambda p, t: (0, p)),
            pl.BlockSpec((length, LANES), lambda p, t: (0, p)),
            pl.BlockSpec((tile, LANES), lambda p, t: (t, p)),
            pl.BlockSpec((tile, LANES), lambda p, t: (t, p)),
            pl.BlockSpec((1, 2, tile), lambda p, t: (p, 0, t)),
            pl.BlockSpec((1, 2, span), lambda p, t: (p, 0, 0)),
        ],
        out_specs=[
            pl.BlockSpec((tile, LANES), lambda p, t: (t, p)),
            pl.BlockSpec((length, LANES), lambda p, t: (0, p)),
            pl.BlockSpec((length, LANES), lambda p, t: (0, p)),
            pl.BlockSpec((1, 2, span), lambda p, t: (p, 0, 0)),
        ],
        out_shape=[
            jax.ShapeDtypeStruct((rows, cols), jnp.bfloat16),
            jax.ShapeDtypeStruct((length, cols), jnp.float32),
            jax.ShapeDtypeStruct((length, cols), jnp.float32),
            jax.ShapeDtypeStruct((pairs, 2, span), jnp.float32),
        ],
        scratch_shapes=[
            pltpu.VMEM((2, LANES, span), jnp.float32),
            pltpu.VMEM((2, LANES, span), jnp.float32),
        ],
        compiler_params=pltpu.CompilerParams(vmem_limit_bytes=60 * MIB),
        cost_estimate=pl.CostEstimate(flops=40 * rows * length * cols, bytes_accessed=24 * length * cols, transcendentals=rows * length * cols // DH),
    )(query, keys, values, grad, mixed, logs, lines)


def normalize(values, gain):
    return values * lax.rsqrt(jnp.mean(values * values, -1, keepdims=True) + norm_epsilon) * gain


def gated_gelu(both):
    return jax.nn.gelu(both[..., 0, :], approximate=True) * both[..., 1, :]


def precondition(grad, master, left, right):
    low = grad.astype(jnp.bfloat16)
    new_left = decay * left[0] + (1.0 - decay) * dot_nt(low, low)
    new_right = decay * right[0] + (1.0 - decay) * dot_tn(low, low)
    turned = dot_nn(left[1].astype(jnp.bfloat16), low).astype(jnp.bfloat16)
    direction = dot_nn(turned, right[1].astype(jnp.bfloat16))
    size = jnp.sqrt(jnp.mean(master * master) + step_epsilon)
    step = (
        matrix_rate * size * direction * lax.rsqrt(jnp.mean(direction * direction) + step_epsilon)
    )
    return (new_left, new_right, master - step)


def adapt(grad, moment, master, rate):
    new_moment = decay * moment + (1.0 - decay) * grad * grad
    return (new_moment, master - rate * grad * lax.rsqrt(new_moment + moment_epsilon))


def barrier(*values):
    return lax.optimization_barrier(values)


def crossing(values):
    return lax.all_to_all(values, ("fsdp", "ctx"), split_axis=0, concat_axis=0, tiled=True)


def on_device(
    tokens,
    cotangent,
    routes,
    buckets,
    attention_in,
    attention_out,
    router,
    gains,
    bias_table,
    expert_in,
    expert_out,
    attention_in_left,
    attention_in_right,
    attention_out_left,
    attention_out_right,
    expert_in_left,
    expert_in_right,
    expert_out_left,
    expert_out_right,
    router_moment,
    gains_moment,
    table_moment,
):
    low = jnp.bfloat16
    rows = tokens.shape[0]
    width = tokens.shape[1]
    shards = lax.axis_size("fsdp") * lax.axis_size("ctx")
    n_ctx = lax.axis_size("ctx")
    n_tp = lax.axis_size("tp")
    here = lax.axis_index("fsdp") * n_ctx + lax.axis_index("ctx")
    tp_here = lax.axis_index("tp")
    length = rows * n_ctx
    depth = attention_in.shape[1]
    head_cols = attention_in.shape[2]
    local_heads = head_cols // DH
    head_pairs = head_cols // LANES
    table_size = bias_table.shape[0]
    experts = router.shape[1]
    capacity = rows * TOPK * 5 // (4 * experts)
    slots_all = experts * capacity
    span = length + rows

    sizes = (depth * experts, 2 * depth, table_size * local_heads)
    small = jnp.concatenate(
        [router.astype(low).reshape(-1), gains.astype(low).reshape(-1), bias_table.astype(low).reshape(-1)]
    )
    small = jnp.pad(small, (0, -small.shape[0] % (16 * head_cols))).reshape(-1, head_cols)
    gathered = lax.all_gather(
        jnp.concatenate([attention_in.astype(low).reshape(3 * depth, head_cols), small], 0),
        ("fsdp", "ctx"),
        axis=0,
        tiled=False,
    )
    entry_full = (
        gathered[:, : 3 * depth]
        .reshape(shards, 3, depth, head_cols)
        .transpose(1, 0, 2, 3)
        .reshape(3, width, head_cols)
    )
    small = gathered[:, 3 * depth :].reshape(shards, -1)
    router_full = small[:, : sizes[0]].reshape(width, experts)
    gains_full = (
        small[:, sizes[0] : sizes[0] + sizes[1]]
        .reshape(shards, 2, depth)
        .transpose(1, 0, 2)
        .reshape(2, width)
    )
    table_full = small[:, sizes[0] + sizes[1] : sum(sizes)].reshape(shards * table_size, local_heads)
    gain_first = gains_full[0].astype(jnp.float32)
    gain_second = gains_full[1].astype(jnp.float32)
    expand_in = expert_in[0].astype(low)
    expand_out = expert_out[0].astype(low)

    chosen = routes.reshape(-1)
    route_hits = (chosen[:, None] == jnp.arange(experts, dtype=jnp.int32)[None, :]).astype(
        jnp.int32
    )
    slots = jnp.sum(route_hits * (jnp.cumsum(route_hits, 0) - 1), 1)
    slot_rows = (chosen * capacity + slots).reshape(rows, TOPK)
    place = jnp.arange(slots_all, dtype=jnp.int32)
    first_hit = place[:, None] == slot_rows[None, :, 0]
    second_hit = place[:, None] == slot_rows[None, :, 1]
    picks = (first_hit | second_hit).astype(low)
    other = jnp.sum(
        jnp.where(first_hit, routes[None, :, 1], 0) + jnp.where(second_hit, routes[None, :, 0], 0),
        1,
    )
    grad_buffer = dot_nn(picks, cotangent).astype(low).reshape(experts, capacity, width)
    other_arrived = crossing(other.reshape(experts, capacity)).reshape(-1)
    grad_arrived = crossing(grad_buffer).reshape(slots_all, width)

    inputs = tokens.astype(jnp.float32)
    first = normalize(inputs, gain_first).astype(low)
    first, unused = barrier(first, grad_buffer)
    projected = jnp.einsum(
        "sd,kde->kse", first, entry_full, preferred_element_type=jnp.float32
    )
    query = (projected[0].astype(low) * (DH**-0.5)).astype(low)
    key_value = projected[1:].astype(low)
    low_end = length - rows - lax.axis_index("ctx") * rows
    near = lax.dynamic_slice_in_dim(jnp.pad(buckets, (0, 1)), low_end, span, 0)
    hits = (near[:, None] == jnp.arange(table_full.shape[0], dtype=jnp.int32)[None, :]).astype(low)
    lines = lax.dot_general(
        table_full, hits, (((0,), (1,)), ((), ())), preferred_element_type=jnp.float32
    ).reshape(head_pairs, 1, 2, span)
    back_lines = lines[..., ::-1]
    exit_own = lax.all_gather(attention_out.astype(low), ("fsdp", "ctx"), axis=1, tiled=True)
    exits = [exit_own]
    for shift in range(1, n_tp):
        exits.append(
            lax.ppermute(exit_own, "tp", [(i, (i + shift) % n_tp) for i in range(n_tp)])
        )
    turned = jnp.concatenate(exits[::-1] + exits[::-1], 0)
    exit_all = lax.dynamic_slice_in_dim(
        turned, (n_tp - 1 - tp_here) * head_cols, n_tp * head_cols, 0
    ).reshape(n_tp, head_pairs, LANES, width)
    queries, pairs, mixed_parts, logs, peak_parts = [], [], [], [], []
    value = jnp.zeros((), jnp.float32)
    for pair in range(head_pairs):
        columns = slice(pair * LANES, (pair + 1) * LANES)
        queries.append(query[:, columns])
        pairs.append(lax.all_gather(key_value[:, :, columns], "ctx", axis=1, tiled=True))
    for pair in range(head_pairs):
        mixed_part, log_part, peak_part = attend(
            queries[pair], pairs[pair][0], pairs[pair][1], lines[pair]
        )
        mixed_parts.append(mixed_part)
        logs.append(log_part)
        peak_parts.append(peak_part[0, :, 0])
        mixed_all = lax.all_gather(mixed_part, "tp", axis=1, tiled=True)
        value = value + dot_nn(mixed_all, exit_all[:, pair].reshape(n_tp * LANES, width))
    mixed = jnp.concatenate(mixed_parts, 1)
    middle = inputs + value
    second = normalize(middle, gain_second).astype(low)

    buffer = dot_nn(picks, second).astype(low).reshape(experts, capacity, width)
    buffer, grad_arrived, other_arrived = barrier(buffer, grad_arrived, other_arrived)
    arrived = crossing(buffer).reshape(slots_all, width)
    plain_grad = dot_nt(grad_arrived, expand_out)
    arrived, plain_grad = barrier(arrived, plain_grad)
    logits = dot_nn(arrived, router_full)
    names = jnp.arange(experts, dtype=jnp.int32)[None, :]
    contrast = (names == here).astype(jnp.float32) - (names == other_arrived[:, None]).astype(
        jnp.float32
    )
    gate = jax.nn.sigmoid(jnp.sum(logits * contrast, 1, keepdims=True))
    mixed_up = jnp.einsum("sd,dgf->sgf", arrived, expand_in, preferred_element_type=jnp.float32)
    hidden, pull = jax.vjp(gated_gelu, mixed_up)
    gated_hidden = (gate * hidden).astype(low)
    grad_gate = jnp.sum(plain_grad * hidden, 1, keepdims=True)
    grad_choice = (gate * (1.0 - gate) * grad_gate * contrast).astype(low)
    grad_mixed_up = pull(gate * plain_grad)[0].astype(low)
    sent_grads = (
        jnp.einsum("sgf,dgf->sd", grad_mixed_up, expand_in, preferred_element_type=jnp.float32)
        + dot_nt(grad_choice, router_full)
    ).astype(low)
    back_grads = crossing(sent_grads.reshape(experts, capacity, width)).reshape(slots_all, width)

    sent_rows = dot_nn(gated_hidden, expand_out).astype(low)
    grad_router = dot_tn(arrived, grad_choice)
    grad_expand_out = dot_tn(gated_hidden, grad_arrived)
    shrink_left, shrink_right, shrink_new = precondition(
        grad_expand_out, expert_out[0], expert_out_left, expert_out_right
    )
    grad_expand_in = jnp.einsum(
        "sd,sgf->dgf", arrived, grad_mixed_up, preferred_element_type=jnp.float32
    )
    back_grads, sent_rows, grad_router, grad_expand_out, grad_expand_in, shrink_left, shrink_right, shrink_new = barrier(
        back_grads, sent_rows, grad_router, grad_expand_out, grad_expand_in, shrink_left, shrink_right, shrink_new
    )
    grad_second = lax.psum(dot_tn(picks, back_grads).astype(low), "tp").astype(jnp.float32)

    back_rows = crossing(sent_rows.reshape(experts, capacity, width)).reshape(slots_all, width)
    expand_left, expand_right, expand_new = precondition(
        grad_expand_in.reshape(width, -1),
        expert_in.reshape(width, -1),
        expert_in_left,
        expert_in_right,
    )
    result_part = dot_tn(picks, back_rows).astype(low)
    grad_second, expand_left, expand_right, expand_new, result_part = barrier(
        grad_second, expand_left, expand_right, expand_new, result_part
    )
    result = (middle + lax.psum(result_part, "tp").astype(jnp.float32)).astype(low)

    unused, pull = jax.vjp(normalize, middle, gain_second)
    grad_middle_norm, grad_gain_second = pull(grad_second)
    grad_middle = cotangent.astype(jnp.float32) + grad_middle_norm
    grad_attention = grad_middle.astype(low)
    grad_mixed = dot_nt(grad_attention, exit_own).astype(low)
    grad_queries, key_value_grads, sums = [], [], []
    for pair in range(head_pairs):
        columns = slice(pair * LANES, (pair + 1) * LANES)
        grad_query, key_grad, value_grad, line_sums = attend_back(
            queries[pair],
            pairs[pair][0],
            pairs[pair][1],
            grad_mixed[:, columns],
            mixed_parts[pair],
            logs[pair],
            back_lines[pair],
        )
        grad_queries.append(grad_query)
        sums.append(line_sums)
        terms = jnp.concatenate([key_grad, value_grad], 1).astype(low)
        swapped = lax.all_to_all(
            terms.reshape(n_ctx, rows, 2 * LANES), "ctx", split_axis=0, concat_axis=0, tiled=True
        )
        key_value_grads.append(jnp.sum(swapped.astype(jnp.float32), 0).astype(low))
    grad_projected = jnp.stack(
        [
            jnp.concatenate(grad_queries, 1),
            jnp.concatenate([terms[:, :LANES] for terms in key_value_grads], 1),
            jnp.concatenate([terms[:, LANES:] for terms in key_value_grads], 1),
        ]
    )
    grad_exit = dot_tn(mixed, grad_attention).astype(low)
    grad_first_part = jnp.einsum(
        "kse,kde->sd", grad_projected, entry_full, preferred_element_type=jnp.float32
    )
    grad_first_part, result = barrier(grad_first_part.astype(low), result)
    grad_first = lax.psum(grad_first_part, "tp").astype(jnp.float32)
    grad_entry = jnp.einsum(
        "sd,kse->dke", first, grad_projected, preferred_element_type=jnp.float32
    ).astype(low)
    entry_terms = lax.all_to_all(
        grad_entry.reshape(shards, depth, 3 * head_cols),
        ("fsdp", "ctx"),
        split_axis=0,
        concat_axis=0,
        tiled=True,
    )
    owned_in = (
        jnp.sum(entry_terms.astype(jnp.float32), 0).reshape(depth, 3, head_cols).transpose(1, 0, 2)
    )
    exit_terms = lax.all_to_all(
        grad_exit.reshape(head_cols, shards, depth).transpose(1, 0, 2),
        ("fsdp", "ctx"),
        split_axis=0,
        concat_axis=0,
        tiled=True,
    )
    owned_out = jnp.sum(exit_terms.astype(jnp.float32), 0)
    unused, pull = jax.vjp(normalize, inputs, gain_first)
    grad_inputs, grad_gain_first = pull(grad_first)
    grad_tokens = grad_middle + grad_inputs

    table_grad = lax.dot_general(
        hits.astype(jnp.float32),
        jnp.concatenate(sums, 0).reshape(local_heads, span)[:, ::-1],
        (((0,), (1,)), ((), ())),
        precision=highest,
        preferred_element_type=jnp.float32,
    )
    own_tp = (jnp.arange(n_tp) == tp_here).astype(jnp.float32)
    own_shard = (jnp.arange(shards) == here).astype(jnp.float32)
    gain_sums = jnp.stack([grad_gain_first, grad_gain_second]) * own_tp[0]
    peak_own = jnp.concatenate(peak_parts)
    pieces = [
        grad_router,
        gain_sums,
        own_tp[:, None, None] * table_grad[None],
        own_shard[:, None, None] * own_tp[None, :, None] * peak_own[None, None, :],
    ]
    packed = jnp.concatenate([piece.reshape(-1) for piece in pieces])
    total = packed.shape[0]
    packed = lax.psum(
        jnp.pad(packed, (0, -total % 1024)).reshape(-1, LANES), ("fsdp", "ctx", "tp")
    ).reshape(-1)
    spots = [0]
    for piece in pieces:
        spots.append(spots[-1] + piece.size)
    router_sum = packed[spots[0] : spots[1]].reshape(shards, depth, experts)
    owned_router = lax.dynamic_index_in_dim(router_sum, here, 0, keepdims=False)
    gain_sum = packed[spots[1] : spots[2]].reshape(2, width)
    owned_gains = lax.dynamic_slice_in_dim(gain_sum, here * depth, depth, 1)
    table_sum = packed[spots[2] : spots[3]].reshape(n_tp, shards, table_size, local_heads)
    owned_table = jnp.einsum("t,s,tsbh->bh", own_tp, own_shard, table_sum, precision=highest)
    peak_sum = packed[spots[3] : spots[4]].reshape(shards, n_tp, local_heads)
    peaks = jnp.max(jnp.einsum("t,sth->sh", own_tp, peak_sum, precision=highest), 0)
    in_left, in_right, in_new = jax.vmap(precondition)(
        owned_in,
        attention_in,
        jnp.swapaxes(attention_in_left, 0, 1),
        jnp.swapaxes(attention_in_right, 0, 1),
    )
    column = jnp.sqrt(jnp.repeat(clip_level / jnp.maximum(peaks, clip_level), DH))
    in_new = in_new * jnp.stack([column, column, jnp.ones_like(column)])[:, None, :]
    out_left, out_right, out_new = precondition(
        owned_out, attention_out, attention_out_left, attention_out_right
    )
    router_moment_new, router_new = adapt(owned_router, router_moment, router, router_rate)
    gains_moment_new, gains_new = adapt(owned_gains, gains_moment, gains, gain_rate)
    table_moment_new, table_new = adapt(owned_table, table_moment, bias_table, table_rate)
    return (
        result,
        grad_tokens,
        owned_in,
        in_new,
        in_left,
        in_right,
        owned_out,
        out_new,
        out_left,
        out_right,
        grad_expand_in[None],
        expand_new.reshape(expert_in.shape),
        expand_left,
        expand_right,
        grad_expand_out[None],
        shrink_new[None],
        shrink_left,
        shrink_right,
        owned_router,
        router_moment_new,
        router_new,
        owned_gains,
        gains_moment_new,
        gains_new,
        owned_table,
        table_moment_new,
        table_new,
    )


def solution(mesh):
    placed = (
        P(("fsdp", "ctx"), None),
        P(("fsdp", "ctx"), None),
        P(("fsdp", "ctx"), None),
        P(),
        P(None, ("fsdp", "ctx"), "tp"),
        P("tp", ("fsdp", "ctx")),
        P(("fsdp", "ctx"), None),
        P(None, ("fsdp", "ctx")),
        P(("fsdp", "ctx"), "tp"),
        P(("fsdp", "ctx"), None, None, "tp"),
        P(("fsdp", "ctx"), "tp", None),
        P(None, None, ("fsdp", "ctx", "tp"), None),
        P(None, None, ("fsdp", "ctx", "tp"), None),
        P(None, ("fsdp", "ctx", "tp"), None),
        P(None, ("fsdp", "ctx", "tp"), None),
        P(None, ("fsdp", "ctx", "tp"), None),
        P(None, ("fsdp", "ctx", "tp"), None),
        P(None, ("fsdp", "ctx", "tp"), None),
        P(None, ("fsdp", "ctx", "tp"), None),
        P(("fsdp", "ctx"), None),
        P(None, ("fsdp", "ctx")),
        P(("fsdp", "ctx"), "tp"),
    )
    return jax.shard_map(
        on_device,
        mesh=mesh,
        in_specs=placed,
        out_specs=(
            P(("fsdp", "ctx"), None),
            P(("fsdp", "ctx"), None),
            P(None, ("fsdp", "ctx"), "tp"),
            P(None, ("fsdp", "ctx"), "tp"),
            P(None, ("fsdp", "ctx", "tp"), None),
            P(None, ("fsdp", "ctx", "tp"), None),
            P("tp", ("fsdp", "ctx")),
            P("tp", ("fsdp", "ctx")),
            P(("fsdp", "ctx", "tp"), None),
            P(("fsdp", "ctx", "tp"), None),
            P(("fsdp", "ctx"), None, None, "tp"),
            P(("fsdp", "ctx"), None, None, "tp"),
            P(("fsdp", "ctx", "tp"), None),
            P(("fsdp", "ctx", "tp"), None),
            P(("fsdp", "ctx"), "tp", None),
            P(("fsdp", "ctx"), "tp", None),
            P(("fsdp", "ctx", "tp"), None),
            P(("fsdp", "ctx", "tp"), None),
            P(("fsdp", "ctx"), None),
            P(("fsdp", "ctx"), None),
            P(("fsdp", "ctx"), None),
            P(None, ("fsdp", "ctx")),
            P(None, ("fsdp", "ctx")),
            P(None, ("fsdp", "ctx")),
            P(("fsdp", "ctx"), "tp"),
            P(("fsdp", "ctx"), "tp"),
            P(("fsdp", "ctx"), "tp"),
        ),
        check_vma=False,
    )
```

```python
import functools

import jax
import jax.numpy as jnp
from jax import lax
from jax.experimental import pallas as pl
from jax.experimental.pallas import tpu as pltpu

from jax.sharding import PartitionSpec as P

DH = 64
LANES = 128
MIB = 1024 * 1024


TOPK = 2

highest = lax.Precision.HIGHEST
norm_epsilon = 1e-06
step_epsilon = 1e-06
moment_epsilon = 1e-08
clip_level = 4.0
decay = 0.5
matrix_rate = 0.3
gain_rate = 0.25
router_rate = 0.01
table_rate = 0.3


def dot_nt(left, right):
    return lax.dot_general(left, right, (((1,), (1,)), ((), ())), preferred_element_type=jnp.float32)


def dot_nn(left, right):
    return lax.dot_general(left, right, (((1,), (0,)), ((), ())), preferred_element_type=jnp.float32)


def dot_tn(left, right):
    return lax.dot_general(left, right, (((0,), (0,)), ((), ())), preferred_element_type=jnp.float32)


def half_mask(shape, half):
    lane = lax.broadcasted_iota(jnp.int32, shape, 1)
    return (lane // DH) == half


def attend_kernel(length, rows, tile, q_ref, k_ref, v_ref, line_ref, mixed_ref, log_ref, peak_ref, strip, wide):
    step = pl.program_id(1)
    span = line_ref.shape[2]

    @pl.when(step == 0)
    def _():
        for half in range(2):
            line = jnp.broadcast_to(line_ref[0, half : half + 1, :], (LANES, span))
            strip[half] = pltpu.roll(line, span - (LANES - 1), 1, stride=1, stride_axis=0)
        wide[:, :LANES] = v_ref[...]
        wide[:, LANES:] = jnp.ones((length, LANES), jnp.bfloat16)
        peak_ref[...] = jnp.full(peak_ref.shape, -jnp.inf, jnp.float32)

    query = q_ref[...]
    groups = tile // LANES
    last = rows // LANES - 1
    mixed = jnp.zeros((tile, LANES), jnp.float32)
    for half in range(2):
        mine = half_mask((tile, LANES), half)
        own = jnp.where(mine, query, jnp.zeros_like(query))
        logit = dot_nt(own, k_ref[...])
        top = jnp.max(logit, 1, keepdims=True)
        bias = []
        for group in range(groups):
            start = pl.multiple_of((last - (step * groups + group)) * LANES, LANES)
            bias.append(strip[half, :, pl.ds(start, length)])
        bias = jnp.concatenate(bias, 0) if groups > 1 else bias[0]
        powers = jnp.exp(logit + bias - top)
        both = dot_nn(powers.astype(jnp.bfloat16), wide[...])
        total = both[:, LANES:]
        mixed = jnp.where(mine, both[:, :LANES] / total, mixed)
        log_total = top + jnp.log(total)
        log_ref[0, half : half + 1, :] = log_total.T[0:1, :]
        best = jnp.max(jnp.broadcast_to(top, (tile, LANES)), 0, keepdims=True)
        peak_ref[0, half : half + 1, :] = jnp.maximum(peak_ref[0, half : half + 1, :], best)
    mixed_ref[...] = mixed.astype(jnp.bfloat16)


def attend(query, keys, values, lines):
    rows, cols = query.shape
    length = keys.shape[0]
    pairs = cols // LANES
    tile = 256 if length <= 4096 else 128
    span = lines.shape[2]
    return pl.pallas_call(
        functools.partial(attend_kernel, length, rows, tile),
        grid=(pairs, rows // tile),
        in_specs=[
            pl.BlockSpec((tile, LANES), lambda p, t: (t, p)),
            pl.BlockSpec((length, LANES), lambda p, t: (0, p)),
            pl.BlockSpec((length, LANES), lambda p, t: (0, p)),
            pl.BlockSpec((1, 2, span), lambda p, t: (p, 0, 0)),
        ],
        out_specs=[
            pl.BlockSpec((tile, LANES), lambda p, t: (t, p)),
            pl.BlockSpec((1, 2, tile), lambda p, t: (p, 0, t)),
            pl.BlockSpec((1, 2, LANES), lambda p, t: (p, 0, 0)),
        ],
        out_shape=[
            jax.ShapeDtypeStruct((rows, cols), jnp.bfloat16),
            jax.ShapeDtypeStruct((pairs, 2, rows), jnp.float32),
            jax.ShapeDtypeStruct((pairs, 2, LANES), jnp.float32),
        ],
        scratch_shapes=[
            pltpu.VMEM((2, LANES, span), jnp.float32),
            pltpu.VMEM((length, 2 * LANES), jnp.bfloat16),
        ],
        compiler_params=pltpu.CompilerParams(vmem_limit_bytes=56 * MIB),
        cost_estimate=pl.CostEstimate(flops=16 * rows * length * cols, bytes_accessed=8 * length * cols, transcendentals=rows * length * cols // DH),
    )(query, keys, values, lines)


def remote(source, target, send, receive, where):
    return pltpu.make_async_remote_copy(
        src_ref=source,
        dst_ref=target,
        send_sem=send,
        recv_sem=receive,
        device_id=where,
        device_id_type=pl.DeviceIdType.MESH,
    )


class LineSum:
    lag = 3

    def __init__(self, axis, count, size, pairs, own, left, right, stage, total, sems):
        self.axis, self.count, self.size, self.pairs = axis, count, size, pairs
        self.own, self.left, self.right, self.stage, self.total = own, left, right, stage, total
        self.part_send, self.left_got, self.right_got, self.total_got, self.down_send, self.up_send = (
            sems.at[0], sems.at[1], sems.at[2], sems.at[3], sems.at[4], sems.at[5],
        )
        self.owners = ((count - 1) // 2, count // 2)
        self.reach = [max(owner, count - 1 - owner) for owner in self.owners]
        self.steps = pairs + self.lag * 2 * max(self.reach)

    @staticmethod
    def scratch(rows, width, size):
        return [pltpu.VMEM((rows, width), jnp.bfloat16)] * 4 + [
            pltpu.SemaphoreType.DMA((6, rows // size))
        ]

    def signal_neighbours(self, barrier):
        me = lax.axis_index(self.axis)
        for offset, there in ((-1, me > 0), (1, me < self.count - 1)):

            @pl.when(there)
            def _():
                pl.semaphore_signal(
                    barrier,
                    inc=1,
                    device_id={self.axis: me + offset},
                    device_id_type=pl.DeviceIdType.MESH,
                )

    def neighbours(self):
        me = lax.axis_index(self.axis)
        return jnp.where(me > 0, 1, 0) + jnp.where(me < self.count - 1, 1, 0)

    def place(self, side, pair):
        chunk = side * self.pairs + pair
        return chunk, pl.ds(pl.multiple_of(chunk * self.size, self.size), self.size)

    def part_up(self, chunk, rows):
        me = lax.axis_index(self.axis)
        return remote(
            self.stage.at[rows], self.left.at[rows], self.part_send.at[chunk], self.left_got.at[chunk], {self.axis: me + 1}
        )

    def part_down(self, chunk, rows):
        me = lax.axis_index(self.axis)
        return remote(
            self.stage.at[rows], self.right.at[rows], self.part_send.at[chunk], self.right_got.at[chunk], {self.axis: me - 1}
        )

    def total_up(self, chunk, rows):
        me = lax.axis_index(self.axis)
        return remote(
            self.total.at[rows], self.total.at[rows], self.up_send.at[chunk], self.total_got.at[chunk], {self.axis: me + 1}
        )

    def total_down(self, chunk, rows):
        me = lax.axis_index(self.axis)
        return remote(
            self.total.at[rows], self.total.at[rows], self.down_send.at[chunk], self.total_got.at[chunk], {self.axis: me - 1}
        )

    def arrived(self, target, rows, got):
        me = lax.axis_index(self.axis)
        peer = jnp.where(me < self.count - 1, me + 1, me - 1)
        remote(target.at[rows], target.at[rows], got, got, {self.axis: peer}).wait_recv()

    def step(self, number):
        me = lax.axis_index(self.axis)
        last = self.count - 1
        wide = jnp.float32
        for side, owner in enumerate(self.owners):
            reach = self.reach[side]
            from_end = jnp.where(me < owner, me, jnp.where(me > owner, last - me, reach))
            pair = number - self.lag * from_end
            chunk, rows = self.place(side, pair)
            inside = (pair >= 0) & (pair < self.pairs)

            @pl.when(inside & (me == 0) & (me < owner))
            def _():
                self.stage[rows, :] = self.own[rows, :]
                self.part_up(chunk, rows).start()

            @pl.when(inside & (me > 0) & (me < owner))
            def _():
                self.arrived(self.left, rows, self.left_got.at[chunk])
                self.stage[rows, :] = (self.own[rows, :].astype(wide) + self.left[rows, :].astype(wide)).astype(jnp.bfloat16)
                self.part_up(chunk, rows).start()

            @pl.when(inside & (me == last) & (me > owner))
            def _():
                self.stage[rows, :] = self.own[rows, :]
                self.part_down(chunk, rows).start()

            @pl.when(inside & (me < last) & (me > owner))
            def _():
                self.arrived(self.right, rows, self.right_got.at[chunk])
                self.stage[rows, :] = (self.own[rows, :].astype(wide) + self.right[rows, :].astype(wide)).astype(jnp.bfloat16)
                self.part_down(chunk, rows).start()

            @pl.when(inside & (me == owner))
            def _():
                value = self.own[rows, :].astype(wide)
                if owner > 0:
                    self.arrived(self.left, rows, self.left_got.at[chunk])
                    value = value + self.left[rows, :].astype(wide)
                if owner < last:
                    self.arrived(self.right, rows, self.right_got.at[chunk])
                    value = value + self.right[rows, :].astype(wide)
                self.total[rows, :] = value.astype(jnp.bfloat16)
                if owner > 0:
                    self.total_down(chunk, rows).start()
                if owner < last:
                    self.total_up(chunk, rows).start()

            away = jnp.where(me < owner, owner - me, me - owner)
            pair = number - self.lag * (reach + away)
            chunk, rows = self.place(side, pair)
            inside = (pair >= 0) & (pair < self.pairs) & (me != owner)

            @pl.when(inside)
            def _():
                self.arrived(self.total, rows, self.total_got.at[chunk])

            @pl.when(inside & (me < owner) & (me > 0))
            def _():
                self.total_down(chunk, rows).start()

            @pl.when(inside & (me > owner) & (me < last))
            def _():
                self.total_up(chunk, rows).start()

    def finish(self):
        me = lax.axis_index(self.axis)
        last = self.count - 1
        for side, owner in enumerate(self.owners):

            def one(pair, carry):
                chunk, rows = self.place(side, pair)

                @pl.when(me < owner)
                def _():
                    self.part_up(chunk, rows).wait_send()

                @pl.when(me > owner)
                def _():
                    self.part_down(chunk, rows).wait_send()

                @pl.when((me <= owner) & (me > 0))
                def _():
                    self.total_down(chunk, rows).wait_send()

                @pl.when((me >= owner) & (me < last))
                def _():
                    self.total_up(chunk, rows).wait_send()

                return carry

            lax.fori_loop(0, self.pairs, one, 0)


SUM_ROWS = 16


def combine_sum_kernel(count, slots_ref, back_ref, out_ref, own, left, right, stage, total, sems):
    rows, width = own.shape
    places = back_ref.shape[0]
    line = LineSum("tp", count, SUM_ROWS, rows // SUM_ROWS // 2, own, left, right, stage, total, sems)
    barrier = pltpu.get_barrier_semaphore()
    line.signal_neighbours(barrier)
    size, depth = 256, 512

    def one(number, carry):
        spot = pl.ds(pl.multiple_of(number * size, size), size)
        slots = slots_ref[spot, :]
        value = jnp.zeros((size, width), jnp.float32)
        for start in range(0, places, depth):
            lane = lax.broadcasted_iota(jnp.int32, (size, depth), 1) + start
            hit = (lane == slots[:, 0:1]) | (lane == slots[:, 1:2])
            value = value + dot_nn(
                jnp.where(hit, 1.0, 0.0).astype(jnp.bfloat16), back_ref[start : start + depth, :]
            )
        own[spot, :] = value.astype(jnp.bfloat16)
        return carry

    lax.fori_loop(0, rows // size, one, 0)
    pl.semaphore_wait(barrier, line.neighbours())

    def step(number, carry):
        line.step(number)
        return carry

    lax.fori_loop(0, line.steps, step, 0)
    out_ref[...] = total[...]
    line.finish()


def combine_sum(slots, back, rows):
    width = back.shape[1]
    vmem = pl.BlockSpec(memory_space=pltpu.VMEM)
    return pl.pallas_call(
        functools.partial(combine_sum_kernel, lax.axis_size("tp")),
        out_shape=jax.ShapeDtypeStruct((rows, width), jnp.bfloat16),
        in_specs=[vmem, vmem],
        out_specs=vmem,
        scratch_shapes=[pltpu.VMEM((rows, width), jnp.bfloat16)] + LineSum.scratch(rows, width, SUM_ROWS),
        compiler_params=pltpu.CompilerParams(
            collective_id=0, has_side_effects=True, vmem_limit_bytes=48 * MIB
        ),
        cost_estimate=pl.CostEstimate(
            flops=2 * rows * back.shape[0] * width, bytes_accessed=200 * rows * width, transcendentals=0
        ),
    )(slots, back)


def attend_back_kernel(length, rows, tile, chunk, n_pairs_all, n_ctx, n_tp, q_ref, k_ref, v_ref, g_ref, m_ref, log_ref, line_ref, part_ref, dq_ref, dkv_ref, sums_ref, total_ref, strip, gather, dk_ref, dv_ref, mine_ref, got_ref, swap_send, swap_got, left, right, stage, total, sems):
    pair = pl.program_id(0)
    step = pl.program_id(1)
    n_pairs = n_pairs_all
    steps = rows // tile
    span = line_ref.shape[2]
    last = length // LANES - 1
    here = lax.axis_index("ctx")
    turn = pair * steps + step
    line_sum = LineSum("tp", n_tp, SUM_ROWS, part_ref.shape[0] // SUM_ROWS // 2, part_ref, left, right, stage, total, sems)
    barrier = pltpu.get_barrier_semaphore()

    def swap(slot, peer):
        return remote(
            mine_ref.at[peer], got_ref.at[slot, here], swap_send.at[slot, peer], swap_got.at[slot, here], {"ctx": peer}
        )

    def arrival(slot, peer):
        return remote(
            mine_ref.at[peer], got_ref.at[slot, peer], swap_send.at[slot, peer], swap_got.at[slot, peer], {"ctx": peer}
        )

    @pl.when(turn == 0)
    def _():
        line_sum.signal_neighbours(barrier)
        for peer in range(n_ctx):

            @pl.when(peer != here)
            def _():
                pl.semaphore_signal(
                    barrier, inc=1, device_id={"ctx": peer}, device_id_type=pl.DeviceIdType.MESH
                )

        pl.semaphore_wait(barrier, line_sum.neighbours() + (n_ctx - 1))

    @pl.when(step == 0)
    def _():
        for half in range(2):
            line = jnp.broadcast_to(line_ref[0, half : half + 1, :], (LANES, span))
            strip[half] = pltpu.roll(line, span - LANES, 1, stride=1, stride_axis=0).astype(strip.dtype)
        gather[...] = jnp.zeros_like(gather)
        dk_ref[...] = jnp.zeros_like(dk_ref)
        dv_ref[...] = jnp.zeros_like(dv_ref)

    chunks = length // chunk
    turns = n_pairs_all * steps * chunks

    def sum_step(number, carry):
        line_sum.step(number)
        return carry

    query = q_ref[...]
    grad = g_ref[...]
    product = grad.astype(jnp.float32) * m_ref[...].astype(jnp.float32)
    owns, grads, deltas, logs = [], [], [], []
    for half in range(2):
        mine = half_mask((tile, LANES), half)
        owns.append(jnp.where(mine, query, jnp.zeros_like(query)))
        grads.append(jnp.where(mine, grad, jnp.zeros_like(grad)))
        picks = half_mask((8, LANES), half).astype(jnp.float32)
        deltas.append(
            lax.dot_general(picks, product, (((1,), (1,)), ((), ())), precision=lax.Precision.HIGHEST, preferred_element_type=jnp.float32)[0:1, :]
        )
        logs.append(log_ref[0, half : half + 1, :])

    def one_chunk(number, carry):
        outs = []
        now = turn * chunks + number
        lax.fori_loop(now * line_sum.steps // turns, (now + 1) * line_sum.steps // turns, sum_step, 0)
        base = pl.multiple_of(number * chunk, chunk)
        keys = k_ref[pl.ds(base, chunk), :]
        values = v_ref[pl.ds(base, chunk), :]
        new_key = dk_ref[pl.ds(base, chunk), :]
        new_value = dv_ref[pl.ds(base, chunk), :]
        for half in range(2):
            logit = dot_nt(keys, owns[half])
            places = []
            bias = []
            for group in range(chunk // LANES):
                row_group = number * (chunk // LANES) + group
                start = pl.multiple_of((last - row_group) * LANES + step * tile, LANES)
                places.append(start)
                bias.append(strip[half, :, pl.ds(start, tile)].astype(jnp.float32))
            bias = jnp.concatenate(bias, 0) if len(bias) > 1 else bias[0]
            shares = jnp.exp(logit + bias - logs[half])
            grad_shares = dot_nt(values, grads[half])
            scores = shares * (grad_shares - deltas[half])
            low_shares = shares.astype(jnp.bfloat16)
            low_scores = scores.astype(jnp.bfloat16)
            new_value = new_value + dot_nn(low_shares, grads[half])
            new_key = new_key + dot_nn(low_scores, owns[half])
            outs.append(carry[half] + dot_tn(low_scores, keys))
            for group, start in enumerate(places):
                gather[half, :, pl.ds(start, tile)] += scores[group * LANES : (group + 1) * LANES]
        dk_ref[pl.ds(base, chunk), :] = new_key
        dv_ref[pl.ds(base, chunk), :] = new_value
        return tuple(outs)

    zero = jnp.zeros((tile, LANES), jnp.float32)
    first, second = lax.fori_loop(0, length // chunk, one_chunk, (zero, zero))
    both = jnp.where(half_mask((tile, LANES), 0), first, second)
    dq_ref[...] = (both * (DH**-0.5)).astype(dq_ref.dtype)

    @pl.when(step == steps - 1)
    def _():
        for peer in range(n_ctx):
            spot = slice(peer * rows, (peer + 1) * rows)

            @pl.when((peer != here) & (pair > 0))
            def _():
                swap(pair - 1, peer).wait_send()

            mine_ref[peer, :, :LANES] = dk_ref[spot, :].astype(jnp.bfloat16)
            mine_ref[peer, :, LANES:] = dv_ref[spot, :].astype(jnp.bfloat16)

            @pl.when(peer != here)
            def _():
                swap(pair, peer).start()

        got_ref[pair, here] = mine_ref[here]
        for half in range(2):
            values = gather[half]
            size = LANES // 2
            while size >= 1:
                values = values[:size] + pltpu.roll(values[size : 2 * size], span - size, 1)
                size //= 2
            sums_ref[0, half : half + 1, :] = pltpu.roll(jnp.broadcast_to(values, (8, span)), LANES, 1)[0:1]

    @pl.when((step == steps - 1) & (pair == n_pairs - 1))
    def _():
        total_ref[...] = total[...]
        for slot in range(2):
            for peer in range(n_ctx):

                @pl.when(peer != here)
                def _():
                    arrival(slot, peer).wait_recv()

            value = got_ref[slot, 0].astype(jnp.float32)
            for peer in range(1, n_ctx):
                value = value + got_ref[slot, peer].astype(jnp.float32)
            dkv_ref[slot] = value.astype(jnp.bfloat16)
        for peer in range(n_ctx):

            @pl.when(peer != here)
            def _():
                swap(1, peer).wait_send()

        line_sum.finish()


def attend_back(query, key_value, grad, mixed, logs, lines, part):
    rows, cols = query.shape
    length = key_value.shape[2]
    pairs = cols // LANES
    depth = 2 if length <= 4096 else 1
    n_ctx = lax.axis_size("ctx")
    tile = 256
    chunk = 512
    span = lines.shape[2]
    width = part.shape[1]
    return pl.pallas_call(
        functools.partial(attend_back_kernel, length, rows, tile, chunk, pairs, n_ctx, lax.axis_size("tp")),
        grid=(pairs, rows // tile),
        in_specs=[
            pl.BlockSpec((tile, LANES), lambda p, t: (t, p)),
            pl.BlockSpec((None, None, length, LANES), lambda p, t: (p, 0, 0, 0), pipeline_mode=pl.Buffered(depth)),
            pl.BlockSpec((None, None, length, LANES), lambda p, t: (p, 1, 0, 0), pipeline_mode=pl.Buffered(depth)),
            pl.BlockSpec((tile, LANES), lambda p, t: (t, p)),
            pl.BlockSpec((tile, LANES), lambda p, t: (t, p)),
            pl.BlockSpec((1, 2, tile), lambda p, t: (p, 0, t)),
            pl.BlockSpec((1, 2, span), lambda p, t: (p, 0, 0)),
            pl.BlockSpec(memory_space=pltpu.VMEM),
        ],
        out_specs=[
            pl.BlockSpec((tile, LANES), lambda p, t: (t, p)),
            pl.BlockSpec(memory_space=pltpu.VMEM),
            pl.BlockSpec((1, 2, span), lambda p, t: (p, 0, 0)),
            pl.BlockSpec(memory_space=pltpu.VMEM),
        ],
        out_shape=[
            jax.ShapeDtypeStruct((rows, cols), jnp.bfloat16),
            jax.ShapeDtypeStruct((pairs, rows, 2 * LANES), jnp.bfloat16),
            jax.ShapeDtypeStruct((pairs, 2, span), jnp.float32),
            jax.ShapeDtypeStruct((rows, width), jnp.bfloat16),
        ],
        scratch_shapes=[
            pltpu.VMEM((2, LANES, span), jnp.float32 if length <= 4096 else jnp.bfloat16),
            pltpu.VMEM((2, LANES, span), jnp.float32),
            pltpu.VMEM((length, LANES), jnp.float32),
            pltpu.VMEM((length, LANES), jnp.float32),
            pltpu.VMEM((n_ctx, rows, 2 * LANES), jnp.bfloat16),
            pltpu.VMEM((pairs, n_ctx, rows, 2 * LANES), jnp.bfloat16),
            pltpu.SemaphoreType.DMA((pairs, n_ctx)),
            pltpu.SemaphoreType.DMA((pairs, n_ctx)),
        ]
        + LineSum.scratch(rows, width, SUM_ROWS),
        compiler_params=pltpu.CompilerParams(
            collective_id=1, has_side_effects=True, vmem_limit_bytes=60 * MIB
        ),
        cost_estimate=pl.CostEstimate(flops=40 * rows * length * cols, bytes_accessed=24 * length * cols, transcendentals=rows * length * cols // DH),
    )(query, key_value, key_value, grad, mixed, logs, lines, part)


def greet(barrier, me, peers):
    for number, where in peers:

        @pl.when(number != me)
        def _():
            pl.semaphore_signal(
                barrier, inc=1, device_id=where, device_id_type=pl.DeviceIdType.MESH
            )


def tail_kernel(
    n_fsdp,
    n_ctx,
    n_tp,
    blocks,
    sum_rows,
    part_ref,
    small_ref,
    grad_ref,
    scale_ref,
    s_right,
    p_right,
    s_left,
    p_left,
    w_ref,
    new_right,
    new_left,
    new_w,
    total_ref,
    small_out,
    turned,
    direction,
    squares,
    plane_got,
    line_got,
    line_own,
    plane_send,
    plane_sem,
    tp_send,
    tp_sem,
    left,
    right,
    stage,
    total,
    sems,
):
    turn = pl.program_id(0)
    turns = pl.num_programs(0)
    rights, lefts = blocks
    line = LineSum("tp", n_tp, SUM_ROWS, part_ref.shape[0] // SUM_ROWS // 2, part_ref, left, right, stage, total, sems)
    here = lax.axis_index("fsdp") * n_ctx + lax.axis_index("ctx")
    tp_here = lax.axis_index("tp")
    shards = n_fsdp * n_ctx
    plane = [(f * n_ctx + c, {"fsdp": f, "ctx": c}) for f in range(n_fsdp) for c in range(n_ctx)]
    column = [(t, {"tp": t}) for t in range(n_tp)]
    other = jnp.where(here == 0, 1, 0)
    other_where = {"fsdp": other // n_ctx, "ctx": other % n_ctx}
    other_tp = {"tp": jnp.where(tp_here == 0, 1, 0)}
    middle = rights + 2

    def plane_copy(number, where):
        return remote(small_ref.at[number], plane_got.at[here], plane_send.at[number], plane_sem.at[here], where)

    def tp_copy(number, where):
        return remote(line_own, line_got.at[tp_here], tp_send.at[number], tp_sem.at[tp_here], where)

    @pl.when(turn == 0)
    def _():
        barrier = pltpu.get_barrier_semaphore()
        greet(barrier, here, plane)
        greet(barrier, tp_here, column)
        squares[...] = jnp.zeros_like(squares)
        pl.semaphore_wait(barrier, shards - 1 + n_tp - 1)
        for number, where in plane:

            @pl.when(number != here)
            def _():
                plane_copy(number, where).start()

        plane_got[here] = small_ref[here]

    @pl.when(turn == middle)
    def _():
        for number, where in plane:

            @pl.when(number != here)
            def _():
                remote(plane_got.at[number], plane_got.at[number], plane_sem.at[number], plane_sem.at[number], other_where).wait_recv()

        added = plane_got[0]
        largest = plane_got[0]
        for number in range(1, shards):
            added = added + plane_got[number]
            largest = jnp.maximum(largest, plane_got[number])
        row = lax.broadcasted_iota(jnp.int32, added.shape, 0)
        line_own[...] = jnp.where(row == sum_rows + 1, largest, added)
        for number, where in column:

            @pl.when(number != tp_here)
            def _():
                tp_copy(number, where).start()

        line_got[tp_here] = line_own[...]

    def one(number, carry):
        line.step(number)
        return carry

    lax.fori_loop(turn * line.steps // turns, (turn + 1) * line.steps // turns, one, 0)

    @pl.when(turn < rights)
    def _():
        spot = pl.ds(pl.multiple_of(turn * LANES, LANES), LANES)
        grad = grad_ref[...]
        new_right[...] = decay * s_right[...] + (1.0 - decay) * dot_nt(grad_ref[spot, :], grad)
        turned[spot, :] = dot_nn(p_right[...].astype(jnp.bfloat16), grad).astype(jnp.bfloat16)

    @pl.when((turn >= rights) & (turn < rights + lefts))
    def _():
        spot = pl.ds(pl.multiple_of((turn - rights) * LANES, LANES), LANES)
        new_left[...] = decay * s_left[...] + (1.0 - decay) * dot_tn(grad_ref[:, spot], grad_ref[...])
        value = dot_nn(turned[...], p_left[...].astype(jnp.bfloat16))
        squares[...] = squares[...] + jnp.sum(value * value, 0, keepdims=True)
        direction[:, spot] = value.astype(jnp.bfloat16)

    @pl.when(turn >= rights + lefts)
    def _():
        spot = pl.ds(pl.multiple_of((turn - rights - lefts) * LANES, LANES), LANES)
        mean = jnp.sum(squares[0:1, :], 1, keepdims=True) / (grad_ref.shape[0] * grad_ref.shape[1])
        factor = scale_ref[0:1, 0:1] * lax.rsqrt(mean + step_epsilon)
        new_w[...] = w_ref[...] - factor * direction[spot, :].astype(jnp.float32)

    @pl.when(turn == turns - 1)
    def _():
        total_ref[...] = total[...]
        for number, where in column:

            @pl.when(number != tp_here)
            def _():
                remote(line_got.at[number], line_got.at[number], tp_sem.at[number], tp_sem.at[number], other_tp).wait_recv()

        added = line_got[0]
        for number in range(1, n_tp):
            added = added + line_got[number]
        row = lax.broadcasted_iota(jnp.int32, added.shape, 0)
        small_out[...] = jnp.where(row < sum_rows, added, line_own[...])
        for number, where in plane:

            @pl.when(number != here)
            def _():
                plane_copy(number, where).wait_send()

        for number, where in column:

            @pl.when(number != tp_here)
            def _():
                tp_copy(number, where).wait_send()

        line.finish()


def tail(part, small, sum_rows, grad, scale, left, right, weight):
    rows, width = part.shape
    deep, wide = grad.shape
    n_fsdp, n_ctx, n_tp = lax.axis_size("fsdp"), lax.axis_size("ctx"), lax.axis_size("tp")
    rights, lefts = deep // LANES, wide // LANES
    turns = 2 * rights + lefts
    small_rows = small.shape[1]
    vmem = pl.BlockSpec(memory_space=pltpu.VMEM)

    def at_right(turn):
        return jnp.minimum(turn, rights - 1)

    def at_left(turn):
        return jnp.clip(turn - rights, 0, lefts - 1)

    def at_weight(turn):
        return jnp.clip(turn - rights - lefts, 0, rights - 1)

    return pl.pallas_call(
        functools.partial(tail_kernel, n_fsdp, n_ctx, n_tp, (rights, lefts), sum_rows),
        grid=(turns,),
        in_specs=[
            vmem,
            vmem,
            vmem,
            vmem,
            pl.BlockSpec((None, LANES, deep), lambda t: (0, at_right(t), 0)),
            pl.BlockSpec((None, LANES, deep), lambda t: (1, at_right(t), 0)),
            pl.BlockSpec((None, LANES, wide), lambda t: (0, at_left(t), 0)),
            pl.BlockSpec((None, wide, LANES), lambda t: (1, 0, at_left(t))),
            pl.BlockSpec((LANES, wide), lambda t: (at_weight(t), 0)),
        ],
        out_specs=[
            pl.BlockSpec((LANES, deep), lambda t: (at_right(t), 0)),
            pl.BlockSpec((LANES, wide), lambda t: (at_left(t), 0)),
            pl.BlockSpec((LANES, wide), lambda t: (at_weight(t), 0)),
            vmem,
            vmem,
        ],
        out_shape=[
            jax.ShapeDtypeStruct((deep, deep), jnp.float32),
            jax.ShapeDtypeStruct((wide, wide), jnp.float32),
            jax.ShapeDtypeStruct((deep, wide), jnp.float32),
            jax.ShapeDtypeStruct((rows, width), jnp.bfloat16),
            jax.ShapeDtypeStruct((small_rows, LANES), jnp.float32),
        ],
        scratch_shapes=[
            pltpu.VMEM((deep, wide), jnp.bfloat16),
            pltpu.VMEM((deep, wide), jnp.bfloat16),
            pltpu.VMEM((1, LANES), jnp.float32),
            pltpu.VMEM((n_fsdp * n_ctx, small_rows, LANES), jnp.float32),
            pltpu.VMEM((n_tp, small_rows, LANES), jnp.float32),
            pltpu.VMEM((small_rows, LANES), jnp.float32),
            pltpu.SemaphoreType.DMA((n_fsdp * n_ctx,)),
            pltpu.SemaphoreType.DMA((n_fsdp * n_ctx,)),
            pltpu.SemaphoreType.DMA((n_tp,)),
            pltpu.SemaphoreType.DMA((n_tp,)),
        ]
        + LineSum.scratch(rows, width, SUM_ROWS),
        compiler_params=pltpu.CompilerParams(
            collective_id=2, has_side_effects=True, vmem_limit_bytes=56 * MIB
        ),
        cost_estimate=pl.CostEstimate(
            flops=8 * deep * wide * (deep + wide), bytes_accessed=240 * rows * width, transcendentals=0
        ),
    )(part, small, grad, scale, right, right, left, left, weight)


def normalize(values, gain):
    return values * lax.rsqrt(jnp.mean(values * values, -1, keepdims=True) + norm_epsilon) * gain


def gated_gelu(both):
    return jax.nn.gelu(both[..., 0, :], approximate=True) * both[..., 1, :]


def precondition(grad, master, left, right):
    low = grad.astype(jnp.bfloat16)
    new_left = decay * left[0] + (1.0 - decay) * dot_nt(low, low)
    new_right = decay * right[0] + (1.0 - decay) * dot_tn(low, low)
    turned = dot_nn(left[1].astype(jnp.bfloat16), low).astype(jnp.bfloat16)
    direction = dot_nn(turned, right[1].astype(jnp.bfloat16))
    size = jnp.sqrt(jnp.mean(master * master) + step_epsilon)
    step = (
        matrix_rate * size * direction * lax.rsqrt(jnp.mean(direction * direction) + step_epsilon)
    )
    return (new_left, new_right, master - step)


def adapt(grad, moment, master, rate):
    new_moment = decay * moment + (1.0 - decay) * grad * grad
    return (new_moment, master - rate * grad * lax.rsqrt(new_moment + moment_epsilon))


def barrier(*values):
    return lax.optimization_barrier(values)


def crossing(values):
    return lax.all_to_all(values, ("fsdp", "ctx"), split_axis=0, concat_axis=0, tiled=True)


def on_device(
    tokens,
    cotangent,
    routes,
    buckets,
    attention_in,
    attention_out,
    router,
    gains,
    bias_table,
    expert_in,
    expert_out,
    attention_in_left,
    attention_in_right,
    attention_out_left,
    attention_out_right,
    expert_in_left,
    expert_in_right,
    expert_out_left,
    expert_out_right,
    router_moment,
    gains_moment,
    table_moment,
):
    low = jnp.bfloat16
    rows = tokens.shape[0]
    width = tokens.shape[1]
    shards = lax.axis_size("fsdp") * lax.axis_size("ctx")
    n_ctx = lax.axis_size("ctx")
    n_tp = lax.axis_size("tp")
    here = lax.axis_index("fsdp") * n_ctx + lax.axis_index("ctx")
    tp_here = lax.axis_index("tp")
    length = rows * n_ctx
    depth = attention_in.shape[1]
    head_cols = attention_in.shape[2]
    local_heads = head_cols // DH
    head_pairs = head_cols // LANES
    table_size = bias_table.shape[0]
    experts = router.shape[1]
    capacity = rows * TOPK * 5 // (4 * experts)
    slots_all = experts * capacity
    span = length + rows

    sizes = (depth * experts, 2 * depth, table_size * local_heads)
    small = jnp.concatenate(
        [router.astype(low).reshape(-1), gains.astype(low).reshape(-1), bias_table.astype(low).reshape(-1)]
    )
    small = jnp.pad(small, (0, -small.shape[0] % (16 * head_cols))).reshape(-1, head_cols)
    gathered = lax.all_gather(
        jnp.concatenate([attention_in.astype(low).reshape(3 * depth, head_cols), small], 0),
        ("fsdp", "ctx"),
        axis=0,
        tiled=False,
    )
    entry_full = (
        gathered[:, : 3 * depth]
        .reshape(shards, 3, depth, head_cols)
        .transpose(1, 0, 2, 3)
        .reshape(3, width, head_cols)
    )
    small = gathered[:, 3 * depth :].reshape(shards, -1)
    router_full = small[:, : sizes[0]].reshape(width, experts)
    gains_full = (
        small[:, sizes[0] : sizes[0] + sizes[1]]
        .reshape(shards, 2, depth)
        .transpose(1, 0, 2)
        .reshape(2, width)
    )
    table_full = small[:, sizes[0] + sizes[1] : sum(sizes)].reshape(shards * table_size, local_heads)
    gain_first = gains_full[0].astype(jnp.float32)
    gain_second = gains_full[1].astype(jnp.float32)
    expand_in = expert_in[0].astype(low)
    expand_out = expert_out[0].astype(low)

    chosen = routes.reshape(-1)
    route_hits = (chosen[:, None] == jnp.arange(experts, dtype=jnp.int32)[None, :]).astype(
        jnp.int32
    )
    slots = jnp.sum(route_hits * (jnp.cumsum(route_hits, 0) - 1), 1)
    slot_rows = (chosen * capacity + slots).reshape(rows, TOPK)
    place = jnp.arange(slots_all, dtype=jnp.int32)
    first_hit = place[:, None] == slot_rows[None, :, 0]
    second_hit = place[:, None] == slot_rows[None, :, 1]
    picks = (first_hit | second_hit).astype(low)
    other = jnp.sum(
        jnp.where(first_hit, routes[None, :, 1], 0) + jnp.where(second_hit, routes[None, :, 0], 0),
        1,
    )
    grad_buffer = dot_nn(picks, cotangent).astype(low).reshape(experts, capacity, width)
    other_arrived = crossing(other.reshape(experts, capacity)).reshape(-1)
    grad_arrived = crossing(grad_buffer).reshape(slots_all, width)

    inputs = tokens.astype(jnp.float32)
    first = normalize(inputs, gain_first).astype(low)
    first, unused = barrier(first, grad_buffer)
    projected = jnp.einsum(
        "sd,kde->kse", first, entry_full, preferred_element_type=jnp.float32
    )
    query = (projected[0].astype(low) * (DH**-0.5)).astype(low)
    key_value = projected[1:].astype(low)
    low_end = length - rows - lax.axis_index("ctx") * rows
    near = lax.dynamic_slice_in_dim(jnp.pad(buckets, (0, 1)), low_end, span, 0)
    hits = (near[:, None] == jnp.arange(table_full.shape[0], dtype=jnp.int32)[None, :]).astype(low)
    lines = lax.dot_general(
        table_full, hits, (((0,), (1,)), ((), ())), preferred_element_type=jnp.float32
    ).reshape(head_pairs, 1, 2, span)
    hits_back = (near[::-1][:, None] == jnp.arange(table_full.shape[0], dtype=jnp.int32)[None, :]).astype(low)
    back_lines = lax.dot_general(
        table_full, hits_back, (((0,), (1,)), ((), ())), preferred_element_type=jnp.float32
    ).reshape(head_pairs, 2, span)
    exit_own = lax.all_gather(attention_out.astype(low), ("fsdp", "ctx"), axis=1, tiled=True)
    exits = [exit_own]
    for shift in range(1, n_tp):
        exits.append(
            lax.ppermute(exit_own, "tp", [(i, (i + shift) % n_tp) for i in range(n_tp)])
        )
    turned = jnp.concatenate(exits[::-1] + exits[::-1], 0)
    exit_all = lax.dynamic_slice_in_dim(
        turned, (n_tp - 1 - tp_here) * head_cols, n_tp * head_cols, 0
    ).reshape(n_tp, head_pairs, LANES, width)
    queries, pairs, mixed_parts, logs, peak_parts = [], [], [], [], []
    value = jnp.zeros((), jnp.float32)
    for pair in range(head_pairs):
        columns = slice(pair * LANES, (pair + 1) * LANES)
        queries.append(query[:, columns])
        pairs.append(lax.all_gather(key_value[:, :, columns], "ctx", axis=1, tiled=True))
    for pair in range(head_pairs):
        mixed_part, log_part, peak_part = attend(
            queries[pair], pairs[pair][0], pairs[pair][1], lines[pair]
        )
        mixed_parts.append(mixed_part)
        logs.append(log_part)
        peak_parts.append(peak_part[0, :, 0])
        mixed_all = lax.all_gather(mixed_part, "tp", axis=1, tiled=True)
        value = value + dot_nn(mixed_all, exit_all[:, pair].reshape(n_tp * LANES, width))
    mixed = jnp.concatenate(mixed_parts, 1)
    middle = inputs + value
    second = normalize(middle, gain_second).astype(low)

    buffer = dot_nn(picks, second).astype(low).reshape(experts, capacity, width)
    buffer, grad_arrived, other_arrived = barrier(buffer, grad_arrived, other_arrived)
    arrived = crossing(buffer).reshape(slots_all, width)
    plain_grad = dot_nt(grad_arrived, expand_out)
    arrived, plain_grad = barrier(arrived, plain_grad)
    logits = dot_nn(arrived, router_full)
    names = jnp.arange(experts, dtype=jnp.int32)[None, :]
    contrast = (names == here).astype(jnp.float32) - (names == other_arrived[:, None]).astype(
        jnp.float32
    )
    gate = jax.nn.sigmoid(jnp.sum(logits * contrast, 1, keepdims=True))
    mixed_up = jnp.einsum("sd,dgf->sgf", arrived, expand_in, preferred_element_type=jnp.float32)
    hidden, pull = jax.vjp(gated_gelu, mixed_up)
    gated_hidden = (gate * hidden).astype(low)
    grad_gate = jnp.sum(plain_grad * hidden, 1, keepdims=True)
    grad_choice = (gate * (1.0 - gate) * grad_gate * contrast).astype(low)
    grad_mixed_up = pull(gate * plain_grad)[0].astype(low)
    sent_grads = (
        jnp.einsum("sgf,dgf->sd", grad_mixed_up, expand_in, preferred_element_type=jnp.float32)
        + dot_nt(grad_choice, router_full)
    ).astype(low)
    back_grads = crossing(sent_grads.reshape(experts, capacity, width)).reshape(slots_all, width)

    sent_rows = dot_nn(gated_hidden, expand_out).astype(low)
    grad_router = dot_tn(arrived, grad_choice)
    grad_expand_out = dot_tn(gated_hidden, grad_arrived)
    shrink_left, shrink_right, shrink_new = precondition(
        grad_expand_out, expert_out[0], expert_out_left, expert_out_right
    )
    grad_expand_in = jnp.einsum(
        "sgf,sd->gfd", grad_mixed_up, arrived, preferred_element_type=jnp.float32
    )
    back_grads, sent_rows, grad_router, grad_expand_out, grad_expand_in, shrink_left, shrink_right, shrink_new = barrier(
        back_grads, sent_rows, grad_router, grad_expand_out, grad_expand_in, shrink_left, shrink_right, shrink_new
    )
    grad_second = combine_sum(slot_rows, back_grads, rows)

    back_rows = crossing(sent_rows.reshape(experts, capacity, width)).reshape(slots_all, width)
    grad_second, back_rows = barrier(grad_second, back_rows)
    result_part = dot_tn(picks, back_rows).astype(low)

    unused, pull = jax.vjp(normalize, middle, gain_second)
    grad_middle_norm, grad_gain_second = pull(grad_second.astype(jnp.float32))
    grad_middle = cotangent.astype(jnp.float32) + grad_middle_norm
    grad_attention = grad_middle.astype(low)
    grad_mixed = dot_nt(grad_attention, exit_own).astype(low)
    grad_query, key_value_grad, sums, result_sum = attend_back(
        query, jnp.stack(pairs), grad_mixed, mixed, jnp.concatenate(logs, 0), back_lines, result_part
    )
    result = (middle + result_sum.astype(jnp.float32)).astype(low)
    grad_projected = jnp.stack(
        [
            grad_query,
            jnp.concatenate([key_value_grad[pair, :, :LANES] for pair in range(head_pairs)], 1),
            jnp.concatenate([key_value_grad[pair, :, LANES:] for pair in range(head_pairs)], 1),
        ]
    )
    grad_exit = dot_tn(mixed, grad_attention).astype(low)
    grad_first_part = jnp.einsum(
        "kse,kde->sd", grad_projected, entry_full, preferred_element_type=jnp.float32
    )
    unused, pull = jax.vjp(normalize, inputs, gain_first)
    grad_gain_first = pull(grad_first_part)[1]
    grad_entry = jnp.einsum(
        "sd,kse->dke", first, grad_projected, preferred_element_type=jnp.float32
    ).astype(low)
    table_grad = lax.dot_general(
        hits_back.astype(jnp.float32),
        sums.reshape(local_heads, span),
        (((0,), (1,)), ((), ())),
        precision=highest,
        preferred_element_type=jnp.float32,
    )
    gain_sums = jnp.stack([grad_gain_first, jnp.where(tp_here == 0, grad_gain_second, 0.0)])
    peak_own = jnp.concatenate(peak_parts)
    pieces = [
        grad_router.reshape(shards, -1),
        gain_sums.reshape(2, shards, depth).transpose(1, 0, 2).reshape(shards, -1),
        table_grad.reshape(shards, -1),
        jnp.broadcast_to(peak_own[None], (shards, local_heads)),
    ]
    spots = [0]
    padded = []
    for piece in pieces:
        padded.append(jnp.pad(piece, ((0, 0), (0, -piece.shape[1] % LANES))))
        spots.append(spots[-1] + padded[-1].shape[1] // LANES)
    small = jnp.concatenate(padded, 1)
    small = jnp.pad(small, ((0, 0), (0, -small.shape[1] % (8 * LANES)))).reshape(shards, -1, LANES)
    columns = grad_expand_in.shape[0] * grad_expand_in.shape[1]
    flat_master = expert_in[0].transpose(1, 2, 0).reshape(columns, width)
    size = jnp.sqrt(jnp.mean(flat_master * flat_master) + step_epsilon)
    first_part, small, entry_terms, exit_terms = barrier(
        grad_first_part.astype(low), small, grad_entry, grad_exit
    )
    entry_terms = crossing(entry_terms.reshape(shards, depth, 3 * head_cols))
    exit_terms = crossing(exit_terms.reshape(head_cols, shards, depth).transpose(1, 0, 2))
    expand_right, expand_left, expand_new, grad_first, small_sum = tail(
        first_part,
        small,
        spots[2],
        grad_expand_in.reshape(columns, width).astype(low),
        jnp.full((8, LANES), matrix_rate * size, jnp.float32),
        expert_in_left,
        expert_in_right,
        flat_master,
    )
    grad_first, entry_terms, exit_terms = barrier(grad_first, entry_terms, exit_terms)
    owned_in = (
        jnp.sum(entry_terms.astype(jnp.float32), 0).reshape(depth, 3, head_cols).transpose(1, 0, 2)
    )
    owned_out = jnp.sum(exit_terms.astype(jnp.float32), 0)
    grad_tokens = grad_middle + pull(grad_first.astype(jnp.float32))[0]

    def small_piece(number, shape):
        count = 1
        for extent in shape:
            count *= extent
        return small_sum[spots[number] : spots[number + 1]].reshape(-1)[:count].reshape(shape)

    owned_router = small_piece(0, (depth, experts))
    owned_gains = small_piece(1, (2, depth))
    owned_table = small_piece(2, (table_size, local_heads))
    peaks = small_piece(3, (local_heads,))
    in_left, in_right, in_new = jax.vmap(precondition)(
        owned_in,
        attention_in,
        jnp.swapaxes(attention_in_left, 0, 1),
        jnp.swapaxes(attention_in_right, 0, 1),
    )
    column = jnp.sqrt(jnp.repeat(clip_level / jnp.maximum(peaks, clip_level), DH))
    in_new = in_new * jnp.stack([column, column, jnp.ones_like(column)])[:, None, :]
    out_left, out_right, out_new = precondition(
        owned_out, attention_out, attention_out_left, attention_out_right
    )
    router_moment_new, router_new = adapt(owned_router, router_moment, router, router_rate)
    gains_moment_new, gains_new = adapt(owned_gains, gains_moment, gains, gain_rate)
    table_moment_new, table_new = adapt(owned_table, table_moment, bias_table, table_rate)
    return (
        result,
        grad_tokens,
        owned_in,
        in_new,
        in_left,
        in_right,
        owned_out,
        out_new,
        out_left,
        out_right,
        grad_expand_in.transpose(2, 0, 1)[None],
        expand_new.reshape(2, -1, width).transpose(2, 0, 1)[None],
        expand_left,
        expand_right,
        grad_expand_out[None],
        shrink_new[None],
        shrink_left,
        shrink_right,
        owned_router,
        router_moment_new,
        router_new,
        owned_gains,
        gains_moment_new,
        gains_new,
        owned_table,
        table_moment_new,
        table_new,
    )


def solution(mesh):
    placed = (
        P(("fsdp", "ctx"), None),
        P(("fsdp", "ctx"), None),
        P(("fsdp", "ctx"), None),
        P(),
        P(None, ("fsdp", "ctx"), "tp"),
        P("tp", ("fsdp", "ctx")),
        P(("fsdp", "ctx"), None),
        P(None, ("fsdp", "ctx")),
        P(("fsdp", "ctx"), "tp"),
        P(("fsdp", "ctx"), None, None, "tp"),
        P(("fsdp", "ctx"), "tp", None),
        P(None, None, ("fsdp", "ctx", "tp"), None),
        P(None, None, ("fsdp", "ctx", "tp"), None),
        P(None, ("fsdp", "ctx", "tp"), None),
        P(None, ("fsdp", "ctx", "tp"), None),
        P(None, ("fsdp", "ctx", "tp"), None),
        P(None, ("fsdp", "ctx", "tp"), None),
        P(None, ("fsdp", "ctx", "tp"), None),
        P(None, ("fsdp", "ctx", "tp"), None),
        P(("fsdp", "ctx"), None),
        P(None, ("fsdp", "ctx")),
        P(("fsdp", "ctx"), "tp"),
    )
    return jax.shard_map(
        on_device,
        mesh=mesh,
        in_specs=placed,
        out_specs=(
            P(("fsdp", "ctx"), None),
            P(("fsdp", "ctx"), None),
            P(None, ("fsdp", "ctx"), "tp"),
            P(None, ("fsdp", "ctx"), "tp"),
            P(None, ("fsdp", "ctx", "tp"), None),
            P(None, ("fsdp", "ctx", "tp"), None),
            P("tp", ("fsdp", "ctx")),
            P("tp", ("fsdp", "ctx")),
            P(("fsdp", "ctx", "tp"), None),
            P(("fsdp", "ctx", "tp"), None),
            P(("fsdp", "ctx"), None, None, "tp"),
            P(("fsdp", "ctx"), None, None, "tp"),
            P(("fsdp", "ctx", "tp"), None),
            P(("fsdp", "ctx", "tp"), None),
            P(("fsdp", "ctx"), "tp", None),
            P(("fsdp", "ctx"), "tp", None),
            P(("fsdp", "ctx", "tp"), None),
            P(("fsdp", "ctx", "tp"), None),
            P(("fsdp", "ctx"), None),
            P(("fsdp", "ctx"), None),
            P(("fsdp", "ctx"), None),
            P(None, ("fsdp", "ctx")),
            P(None, ("fsdp", "ctx")),
            P(None, ("fsdp", "ctx")),
            P(("fsdp", "ctx"), "tp"),
            P(("fsdp", "ctx"), "tp"),
            P(("fsdp", "ctx"), "tp"),
        ),
        check_vma=False,
    )
```

```python
import functools

import jax
import jax.numpy as jnp
from jax import lax
from jax.experimental import pallas as pl
from jax.experimental.pallas import tpu as pltpu

from jax.sharding import PartitionSpec as P

DH = 64
LANES = 128
MIB = 1024 * 1024


TOPK = 2

highest = lax.Precision.HIGHEST
norm_epsilon = 1e-06
step_epsilon = 1e-06
moment_epsilon = 1e-08
clip_level = 4.0
decay = 0.5
matrix_rate = 0.3
gain_rate = 0.25
router_rate = 0.01
table_rate = 0.3


def dot_nt(left, right):
    return lax.dot_general(left, right, (((1,), (1,)), ((), ())), preferred_element_type=jnp.float32)


def dot_nn(left, right):
    return lax.dot_general(left, right, (((1,), (0,)), ((), ())), preferred_element_type=jnp.float32)


def dot_tn(left, right):
    return lax.dot_general(left, right, (((0,), (0,)), ((), ())), preferred_element_type=jnp.float32)


def half_mask(shape, half):
    lane = lax.broadcasted_iota(jnp.int32, shape, 1)
    return (lane // DH) == half


def attend_kernel(length, rows, tile, pairs, n_fsdp, n_ctx, n_tp, q_ref, own_ref, line_ref, cross_ref, mixed_ref, log_ref, peak_ref, kv_out, all_out, cross_out, strip, wide, kv_ref, all_ref, kv_send, kv_got, mix_send, mix_got, out_sem, cross_send, cross_got):
    pair = pl.program_id(0)
    step = pl.program_id(1)
    steps = rows // tile
    span = line_ref.shape[2]
    here = lax.axis_index("ctx")
    tp_here = lax.axis_index("tp")
    own_rows = pl.ds(pl.multiple_of(here * rows, rows), rows)
    ctx_peers = [(number, {"ctx": number}) for number in range(n_ctx)]
    tp_peers = [(number, {"tp": number}) for number in range(n_tp)]
    shard = lax.axis_index("fsdp") * n_ctx + here
    plane = [(f * n_ctx + c, {"fsdp": f, "ctx": c}) for f in range(n_fsdp) for c in range(n_ctx)]
    other = jnp.where(shard == 0, 1, 0)
    other_plane = {"fsdp": other // n_ctx, "ctx": other % n_ctx}
    other_ctx = {"ctx": jnp.where(here == 0, 1, 0)}
    other_tp = {"tp": jnp.where(tp_here == 0, 1, 0)}

    def kv_copy(slot, number, where):
        return remote(
            own_ref.at[slot], kv_ref.at[slot, :, own_rows, :], kv_send.at[slot, number], kv_got.at[slot, here], where
        )

    def kv_arrived(slot, number):
        spot = kv_ref.at[slot, :, pl.ds(number * rows, rows), :]
        remote(spot, spot, kv_got.at[slot, number], kv_got.at[slot, number], other_ctx).wait_recv()

    def cross_copy(number, where):
        return remote(
            cross_ref.at[number], cross_out.at[shard], cross_send.at[number], cross_got.at[shard], where
        )

    def cross_own():
        return pltpu.make_async_copy(cross_ref.at[shard], cross_out.at[shard], out_sem.at[2])

    def mix_spot(slot, turn, number):
        return (
            pl.ds(pl.multiple_of(turn * tile, tile), tile),
            pl.ds(pl.multiple_of((number * pairs + slot) * LANES, LANES), LANES),
        )

    def mix_copy(slot, turn, number, where):
        spot = all_ref.at[mix_spot(slot, turn, tp_here)]
        return remote(spot, spot, mix_send.at[slot, turn, number], mix_got.at[slot, turn, tp_here], where)

    @pl.when((pair == 0) & (step == 0))
    def _():
        barrier = pltpu.get_barrier_semaphore()
        greet(barrier, shard, plane)
        greet(barrier, tp_here, tp_peers)
        pl.semaphore_wait(barrier, n_fsdp * n_ctx - 1 + n_tp - 1)
        for slot in range(pairs):
            for number, where in ctx_peers:

                @pl.when(number != here)
                def _():
                    kv_copy(slot, number, where).start()

            kv_ref[slot, :, own_rows, :] = own_ref[slot]

    @pl.when(step == 0)
    def _():
        for half in range(2):
            line = jnp.broadcast_to(line_ref[0, half : half + 1, :], (LANES, span))
            strip[half] = pltpu.roll(line, span - (LANES - 1), 1, stride=1, stride_axis=0)
        wide[:, LANES:] = jnp.ones((length, LANES), jnp.bfloat16)
        peak_ref[...] = jnp.full(peak_ref.shape, -jnp.inf, jnp.float32)
        for number, where in ctx_peers:

            @pl.when(number != here)
            def _():
                kv_arrived(pair, number)

        wide[:, :LANES] = kv_ref[pair, 1]

    @pl.when((pair == 0) & (step == 2))
    def _():
        cross_own().start()
        for number, where in plane:

            @pl.when(number != shard)
            def _():
                cross_copy(number, where).start()

    query = q_ref[...]
    groups = tile // LANES
    last = rows // LANES - 1
    mixed = jnp.zeros((tile, LANES), jnp.float32)
    for half in range(2):
        mine = half_mask((tile, LANES), half)
        own = jnp.where(mine, query, jnp.zeros_like(query))
        logit = dot_nt(own, kv_ref[pair, 0])
        top = jnp.max(logit, 1, keepdims=True)
        bias = []
        for group in range(groups):
            start = pl.multiple_of((last - (step * groups + group)) * LANES, LANES)
            bias.append(strip[half, :, pl.ds(start, length)])
        bias = jnp.concatenate(bias, 0) if groups > 1 else bias[0]
        powers = jnp.exp(logit + bias - top)
        both = dot_nn(powers.astype(jnp.bfloat16), wide[...])
        total = both[:, LANES:]
        mixed = jnp.where(mine, both[:, :LANES] / total, mixed)
        log_total = top + jnp.log(total)
        log_ref[0, half : half + 1, :] = log_total.T[0:1, :]
        best = jnp.max(jnp.broadcast_to(top, (tile, LANES)), 0, keepdims=True)
        peak_ref[0, half : half + 1, :] = jnp.maximum(peak_ref[0, half : half + 1, :], best)
    low = mixed.astype(jnp.bfloat16)
    mixed_ref[...] = low
    all_ref[mix_spot(pair, step, tp_here)] = low
    for number, where in reversed(tp_peers):

        @pl.when(number != tp_here)
        def _():
            mix_copy(pair, step, number, where).start()

    @pl.when((pair == pairs - 1) & (step == steps - 1))
    def _():
        for slot in range(pairs):
            for number, where in ctx_peers:

                @pl.when(number != here)
                def _():
                    kv_copy(slot, number, where).wait_send()

        def one(index, carry):
            slot, turn = index // steps, index % steps
            for number, where in tp_peers:

                @pl.when(number != tp_here)
                def _():
                    spot = all_ref.at[mix_spot(slot, turn, number)]
                    got = mix_got.at[slot, turn, number]
                    remote(spot, spot, got, got, other_tp).wait_recv()
                    mix_copy(slot, turn, number, where).wait_send()

            return carry

        kept = pltpu.make_async_copy(kv_ref, kv_out, out_sem.at[0])
        kept.start()
        lax.fori_loop(0, pairs * steps, one, 0)
        gathered = pltpu.make_async_copy(all_ref, all_out, out_sem.at[1])
        gathered.start()
        kept.wait()
        gathered.wait()
        cross_own().wait()
        for number, where in plane:

            @pl.when(number != shard)
            def _():
                spot = cross_out.at[number]
                remote(spot, spot, cross_got.at[number], cross_got.at[number], other_plane).wait_recv()
                cross_copy(number, where).wait_send()


def attend(query, own, lines, cross):
    rows, cols = query.shape
    n_fsdp, n_ctx, n_tp = lax.axis_size("fsdp"), lax.axis_size("ctx"), lax.axis_size("tp")
    length = rows * n_ctx
    pairs = cols // LANES
    tile = 256 if length <= 4096 else 128
    span = lines.shape[2]
    vmem = pl.BlockSpec(memory_space=pltpu.VMEM)
    return pl.pallas_call(
        functools.partial(attend_kernel, length, rows, tile, pairs, n_fsdp, n_ctx, n_tp),
        grid=(pairs, rows // tile),
        in_specs=[
            pl.BlockSpec((tile, LANES), lambda p, t: (t, p)),
            vmem,
            pl.BlockSpec((1, 2, span), lambda p, t: (p, 0, 0)),
            pl.BlockSpec(memory_space=pl.ANY),
        ],
        out_specs=[
            pl.BlockSpec((tile, LANES), lambda p, t: (t, p)),
            pl.BlockSpec((1, 2, tile), lambda p, t: (p, 0, t)),
            pl.BlockSpec((1, 2, LANES), lambda p, t: (p, 0, 0)),
            pl.BlockSpec(memory_space=pl.ANY),
            pl.BlockSpec(memory_space=pl.ANY),
            pl.BlockSpec(memory_space=pl.ANY),
        ],
        out_shape=[
            jax.ShapeDtypeStruct((rows, cols), jnp.bfloat16),
            jax.ShapeDtypeStruct((pairs, 2, rows), jnp.float32),
            jax.ShapeDtypeStruct((pairs, 2, LANES), jnp.float32),
            jax.ShapeDtypeStruct((pairs, 2, length, LANES), jnp.bfloat16),
            jax.ShapeDtypeStruct((rows, n_tp * cols), jnp.bfloat16),
            jax.ShapeDtypeStruct(cross.shape, cross.dtype),
        ],
        scratch_shapes=[
            pltpu.VMEM((2, LANES, span), jnp.float32),
            pltpu.VMEM((length, 2 * LANES), jnp.bfloat16),
            pltpu.VMEM((pairs, 2, length, LANES), jnp.bfloat16),
            pltpu.VMEM((rows, n_tp * cols), jnp.bfloat16),
            pltpu.SemaphoreType.DMA((pairs, n_ctx)),
            pltpu.SemaphoreType.DMA((pairs, n_ctx)),
            pltpu.SemaphoreType.DMA((pairs, rows // tile, n_tp)),
            pltpu.SemaphoreType.DMA((pairs, rows // tile, n_tp)),
            pltpu.SemaphoreType.DMA((3,)),
            pltpu.SemaphoreType.DMA((n_fsdp * n_ctx,)),
            pltpu.SemaphoreType.DMA((n_fsdp * n_ctx,)),
        ],
        compiler_params=pltpu.CompilerParams(
            collective_id=3, has_side_effects=True, vmem_limit_bytes=60 * MIB
        ),
        cost_estimate=pl.CostEstimate(flops=100 * rows * length * cols, bytes_accessed=8 * length * cols, transcendentals=rows * length * cols // DH),
    )(query, own, lines, cross)


def remote(source, target, send, receive, where):
    return pltpu.make_async_remote_copy(
        src_ref=source,
        dst_ref=target,
        send_sem=send,
        recv_sem=receive,
        device_id=where,
        device_id_type=pl.DeviceIdType.MESH,
    )


def greet(barrier, me, peers):
    for number, where in peers:

        @pl.when(number != me)
        def _():
            pl.semaphore_signal(
                barrier, inc=1, device_id=where, device_id_type=pl.DeviceIdType.MESH
            )


class LineSum:
    lag = 3

    def __init__(self, axis, count, size, pairs, own, left, right, stage, total, sems):
        self.axis, self.count, self.size, self.pairs = axis, count, size, pairs
        self.own, self.left, self.right, self.stage, self.total = own, left, right, stage, total
        self.part_send, self.left_got, self.right_got, self.total_got, self.down_send, self.up_send = (
            sems.at[0], sems.at[1], sems.at[2], sems.at[3], sems.at[4], sems.at[5],
        )
        self.owners = ((count - 1) // 2, count // 2)
        self.reach = [max(owner, count - 1 - owner) for owner in self.owners]
        self.steps = pairs + self.lag * 2 * max(self.reach)

    @staticmethod
    def scratch(rows, width, size):
        return [pltpu.VMEM((rows, width), jnp.bfloat16)] * 4 + [
            pltpu.SemaphoreType.DMA((6, rows // size))
        ]

    def signal_neighbours(self, barrier):
        me = lax.axis_index(self.axis)
        for offset, there in ((-1, me > 0), (1, me < self.count - 1)):

            @pl.when(there)
            def _():
                pl.semaphore_signal(
                    barrier,
                    inc=1,
                    device_id={self.axis: me + offset},
                    device_id_type=pl.DeviceIdType.MESH,
                )

    def neighbours(self):
        me = lax.axis_index(self.axis)
        return jnp.where(me > 0, 1, 0) + jnp.where(me < self.count - 1, 1, 0)

    def place(self, side, pair):
        chunk = side * self.pairs + pair
        return chunk, pl.ds(pl.multiple_of(chunk * self.size, self.size), self.size)

    def part_up(self, chunk, rows):
        me = lax.axis_index(self.axis)
        return remote(
            self.stage.at[rows], self.left.at[rows], self.part_send.at[chunk], self.left_got.at[chunk], {self.axis: me + 1}
        )

    def part_down(self, chunk, rows):
        me = lax.axis_index(self.axis)
        return remote(
            self.stage.at[rows], self.right.at[rows], self.part_send.at[chunk], self.right_got.at[chunk], {self.axis: me - 1}
        )

    def total_up(self, chunk, rows):
        me = lax.axis_index(self.axis)
        return remote(
            self.total.at[rows], self.total.at[rows], self.up_send.at[chunk], self.total_got.at[chunk], {self.axis: me + 1}
        )

    def total_down(self, chunk, rows):
        me = lax.axis_index(self.axis)
        return remote(
            self.total.at[rows], self.total.at[rows], self.down_send.at[chunk], self.total_got.at[chunk], {self.axis: me - 1}
        )

    def arrived(self, target, rows, got):
        me = lax.axis_index(self.axis)
        peer = jnp.where(me < self.count - 1, me + 1, me - 1)
        remote(target.at[rows], target.at[rows], got, got, {self.axis: peer}).wait_recv()

    def step(self, number):
        me = lax.axis_index(self.axis)
        last = self.count - 1
        wide = jnp.float32
        for side, owner in enumerate(self.owners):
            reach = self.reach[side]
            from_end = jnp.where(me < owner, me, jnp.where(me > owner, last - me, reach))
            pair = number - self.lag * from_end
            chunk, rows = self.place(side, pair)
            inside = (pair >= 0) & (pair < self.pairs)

            @pl.when(inside & (me == 0) & (me < owner))
            def _():
                self.stage[rows, :] = self.own[rows, :]
                self.part_up(chunk, rows).start()

            @pl.when(inside & (me > 0) & (me < owner))
            def _():
                self.arrived(self.left, rows, self.left_got.at[chunk])
                self.stage[rows, :] = (self.own[rows, :].astype(wide) + self.left[rows, :].astype(wide)).astype(jnp.bfloat16)
                self.part_up(chunk, rows).start()

            @pl.when(inside & (me == last) & (me > owner))
            def _():
                self.stage[rows, :] = self.own[rows, :]
                self.part_down(chunk, rows).start()

            @pl.when(inside & (me < last) & (me > owner))
            def _():
                self.arrived(self.right, rows, self.right_got.at[chunk])
                self.stage[rows, :] = (self.own[rows, :].astype(wide) + self.right[rows, :].astype(wide)).astype(jnp.bfloat16)
                self.part_down(chunk, rows).start()

            @pl.when(inside & (me == owner))
            def _():
                value = self.own[rows, :].astype(wide)
                if owner > 0:
                    self.arrived(self.left, rows, self.left_got.at[chunk])
                    value = value + self.left[rows, :].astype(wide)
                if owner < last:
                    self.arrived(self.right, rows, self.right_got.at[chunk])
                    value = value + self.right[rows, :].astype(wide)
                self.total[rows, :] = value.astype(jnp.bfloat16)
                if owner > 0:
                    self.total_down(chunk, rows).start()
                if owner < last:
                    self.total_up(chunk, rows).start()

            away = jnp.where(me < owner, owner - me, me - owner)
            pair = number - self.lag * (reach + away)
            chunk, rows = self.place(side, pair)
            inside = (pair >= 0) & (pair < self.pairs) & (me != owner)

            @pl.when(inside)
            def _():
                self.arrived(self.total, rows, self.total_got.at[chunk])

            @pl.when(inside & (me < owner) & (me > 0))
            def _():
                self.total_down(chunk, rows).start()

            @pl.when(inside & (me > owner) & (me < last))
            def _():
                self.total_up(chunk, rows).start()

    def finish(self):
        me = lax.axis_index(self.axis)
        last = self.count - 1
        for side, owner in enumerate(self.owners):

            def one(pair, carry):
                chunk, rows = self.place(side, pair)

                @pl.when(me < owner)
                def _():
                    self.part_up(chunk, rows).wait_send()

                @pl.when(me > owner)
                def _():
                    self.part_down(chunk, rows).wait_send()

                @pl.when((me <= owner) & (me > 0))
                def _():
                    self.total_down(chunk, rows).wait_send()

                @pl.when((me >= owner) & (me < last))
                def _():
                    self.total_up(chunk, rows).wait_send()

                return carry

            lax.fori_loop(0, self.pairs, one, 0)


SUM_ROWS = 16


def combine_sum_kernel(count, slots_ref, back_ref, out_ref, own, left, right, stage, total, sems):
    rows, width = own.shape
    places = back_ref.shape[0]
    line = LineSum("tp", count, SUM_ROWS, rows // SUM_ROWS // 2, own, left, right, stage, total, sems)
    barrier = pltpu.get_barrier_semaphore()
    line.signal_neighbours(barrier)
    size, depth = 256, 512

    def one(number, carry):
        spot = pl.ds(pl.multiple_of(number * size, size), size)
        slots = slots_ref[spot, :]
        value = jnp.zeros((size, width), jnp.float32)
        for start in range(0, places, depth):
            lane = lax.broadcasted_iota(jnp.int32, (size, depth), 1) + start
            hit = (lane == slots[:, 0:1]) | (lane == slots[:, 1:2])
            value = value + dot_nn(
                jnp.where(hit, 1.0, 0.0).astype(jnp.bfloat16), back_ref[start : start + depth, :]
            )
        own[spot, :] = value.astype(jnp.bfloat16)
        return carry

    lax.fori_loop(0, rows // size, one, 0)
    pl.semaphore_wait(barrier, line.neighbours())

    def step(number, carry):
        line.step(number)
        return carry

    lax.fori_loop(0, line.steps, step, 0)
    out_ref[...] = total[...]
    line.finish()


def combine_sum(slots, back, rows):
    width = back.shape[1]
    vmem = pl.BlockSpec(memory_space=pltpu.VMEM)
    return pl.pallas_call(
        functools.partial(combine_sum_kernel, lax.axis_size("tp")),
        out_shape=jax.ShapeDtypeStruct((rows, width), jnp.bfloat16),
        in_specs=[vmem, vmem],
        out_specs=vmem,
        scratch_shapes=[pltpu.VMEM((rows, width), jnp.bfloat16)] + LineSum.scratch(rows, width, SUM_ROWS),
        compiler_params=pltpu.CompilerParams(
            collective_id=0, has_side_effects=True, vmem_limit_bytes=48 * MIB
        ),
        cost_estimate=pl.CostEstimate(
            flops=2 * rows * back.shape[0] * width, bytes_accessed=200 * rows * width, transcendentals=0
        ),
    )(slots, back)


def attend_back_kernel(length, rows, tile, chunk, n_pairs_all, n_ctx, n_tp, q_ref, k_ref, v_ref, g_ref, m_ref, log_ref, line_ref, part_ref, dq_ref, dkv_ref, sums_ref, total_ref, strip, gather, dk_ref, dv_ref, mine_ref, got_ref, swap_send, swap_got, left, right, stage, total, sems):
    pair = pl.program_id(0)
    step = pl.program_id(1)
    n_pairs = n_pairs_all
    steps = rows // tile
    span = line_ref.shape[2]
    last = length // LANES - 1
    here = lax.axis_index("ctx")
    turn = pair * steps + step
    line_sum = LineSum("tp", n_tp, SUM_ROWS, part_ref.shape[0] // SUM_ROWS // 2, part_ref, left, right, stage, total, sems)
    barrier = pltpu.get_barrier_semaphore()

    def swap(slot, peer):
        return remote(
            mine_ref.at[peer], got_ref.at[slot, here], swap_send.at[slot, peer], swap_got.at[slot, here], {"ctx": peer}
        )

    def arrival(slot, peer):
        return remote(
            mine_ref.at[peer], got_ref.at[slot, peer], swap_send.at[slot, peer], swap_got.at[slot, peer], {"ctx": peer}
        )

    @pl.when(turn == 0)
    def _():
        line_sum.signal_neighbours(barrier)
        for peer in range(n_ctx):

            @pl.when(peer != here)
            def _():
                pl.semaphore_signal(
                    barrier, inc=1, device_id={"ctx": peer}, device_id_type=pl.DeviceIdType.MESH
                )

        pl.semaphore_wait(barrier, line_sum.neighbours() + (n_ctx - 1))

    @pl.when(step == 0)
    def _():
        for half in range(2):
            line = jnp.broadcast_to(line_ref[0, half : half + 1, :], (LANES, span))
            strip[half] = pltpu.roll(line, span - LANES, 1, stride=1, stride_axis=0).astype(strip.dtype)
        gather[...] = jnp.zeros_like(gather)
        dk_ref[...] = jnp.zeros_like(dk_ref)
        dv_ref[...] = jnp.zeros_like(dv_ref)

    chunks = length // chunk
    turns = n_pairs_all * steps * chunks

    def sum_step(number, carry):
        line_sum.step(number)
        return carry

    query = q_ref[...]
    grad = g_ref[...]
    product = grad.astype(jnp.float32) * m_ref[...].astype(jnp.float32)
    owns, grads, deltas, logs = [], [], [], []
    for half in range(2):
        mine = half_mask((tile, LANES), half)
        owns.append(jnp.where(mine, query, jnp.zeros_like(query)))
        grads.append(jnp.where(mine, grad, jnp.zeros_like(grad)))
        picks = half_mask((8, LANES), half).astype(jnp.float32)
        deltas.append(
            lax.dot_general(picks, product, (((1,), (1,)), ((), ())), precision=lax.Precision.HIGHEST, preferred_element_type=jnp.float32)[0:1, :]
        )
        logs.append(log_ref[0, half : half + 1, :])

    def one_chunk(number, carry):
        outs = []
        now = turn * chunks + number
        lax.fori_loop(now * line_sum.steps // turns, (now + 1) * line_sum.steps // turns, sum_step, 0)
        base = pl.multiple_of(number * chunk, chunk)
        keys = k_ref[pl.ds(base, chunk), :]
        values = v_ref[pl.ds(base, chunk), :]
        new_key = dk_ref[pl.ds(base, chunk), :]
        new_value = dv_ref[pl.ds(base, chunk), :]
        for half in range(2):
            logit = dot_nt(keys, owns[half])
            places = []
            bias = []
            for group in range(chunk // LANES):
                row_group = number * (chunk // LANES) + group
                start = pl.multiple_of((last - row_group) * LANES + step * tile, LANES)
                places.append(start)
                bias.append(strip[half, :, pl.ds(start, tile)].astype(jnp.float32))
            bias = jnp.concatenate(bias, 0) if len(bias) > 1 else bias[0]
            shares = jnp.exp(logit + bias - logs[half])
            grad_shares = dot_nt(values, grads[half])
            scores = shares * (grad_shares - deltas[half])
            low_shares = shares.astype(jnp.bfloat16)
            low_scores = scores.astype(jnp.bfloat16)
            new_value = new_value + dot_nn(low_shares, grads[half])
            new_key = new_key + dot_nn(low_scores, owns[half])
            outs.append(carry[half] + dot_tn(low_scores, keys))
            for group, start in enumerate(places):
                gather[half, :, pl.ds(start, tile)] += scores[group * LANES : (group + 1) * LANES]
        dk_ref[pl.ds(base, chunk), :] = new_key
        dv_ref[pl.ds(base, chunk), :] = new_value
        return tuple(outs)

    zero = jnp.zeros((tile, LANES), jnp.float32)
    first, second = lax.fori_loop(0, length // chunk, one_chunk, (zero, zero))
    both = jnp.where(half_mask((tile, LANES), 0), first, second)
    dq_ref[...] = (both * (DH**-0.5)).astype(dq_ref.dtype)

    @pl.when(step == steps - 1)
    def _():
        for peer in range(n_ctx):
            spot = slice(peer * rows, (peer + 1) * rows)

            @pl.when((peer != here) & (pair > 0))
            def _():
                swap(pair - 1, peer).wait_send()

            mine_ref[peer, :, :LANES] = dk_ref[spot, :].astype(jnp.bfloat16)
            mine_ref[peer, :, LANES:] = dv_ref[spot, :].astype(jnp.bfloat16)

            @pl.when(peer != here)
            def _():
                swap(pair, peer).start()

        got_ref[pair, here] = mine_ref[here]
        for half in range(2):
            values = gather[half]
            size = LANES // 2
            while size >= 1:
                values = values[:size] + pltpu.roll(values[size : 2 * size], span - size, 1)
                size //= 2
            sums_ref[0, half : half + 1, :] = pltpu.roll(jnp.broadcast_to(values, (8, span)), LANES, 1)[0:1]

    @pl.when((step == steps - 1) & (pair == n_pairs - 1))
    def _():
        total_ref[...] = total[...]
        for slot in range(2):
            for peer in range(n_ctx):

                @pl.when(peer != here)
                def _():
                    arrival(slot, peer).wait_recv()

            value = got_ref[slot, 0].astype(jnp.float32)
            for peer in range(1, n_ctx):
                value = value + got_ref[slot, peer].astype(jnp.float32)
            dkv_ref[slot] = value.astype(jnp.bfloat16)
        for peer in range(n_ctx):

            @pl.when(peer != here)
            def _():
                swap(1, peer).wait_send()

        line_sum.finish()


def attend_back(query, key_value, grad, mixed, logs, lines, part):
    rows, cols = query.shape
    length = key_value.shape[2]
    pairs = cols // LANES
    depth = 2 if length <= 4096 else 1
    n_ctx = lax.axis_size("ctx")
    tile = 256
    chunk = 512
    span = lines.shape[2]
    width = part.shape[1]
    return pl.pallas_call(
        functools.partial(attend_back_kernel, length, rows, tile, chunk, pairs, n_ctx, lax.axis_size("tp")),
        grid=(pairs, rows // tile),
        in_specs=[
            pl.BlockSpec((tile, LANES), lambda p, t: (t, p)),
            pl.BlockSpec((None, None, length, LANES), lambda p, t: (p, 0, 0, 0), pipeline_mode=pl.Buffered(depth)),
            pl.BlockSpec((None, None, length, LANES), lambda p, t: (p, 1, 0, 0), pipeline_mode=pl.Buffered(depth)),
            pl.BlockSpec((tile, LANES), lambda p, t: (t, p)),
            pl.BlockSpec((tile, LANES), lambda p, t: (t, p)),
            pl.BlockSpec((1, 2, tile), lambda p, t: (p, 0, t)),
            pl.BlockSpec((1, 2, span), lambda p, t: (p, 0, 0)),
            pl.BlockSpec(memory_space=pltpu.VMEM),
        ],
        out_specs=[
            pl.BlockSpec((tile, LANES), lambda p, t: (t, p)),
            pl.BlockSpec(memory_space=pltpu.VMEM),
            pl.BlockSpec((1, 2, span), lambda p, t: (p, 0, 0)),
            pl.BlockSpec(memory_space=pltpu.VMEM),
        ],
        out_shape=[
            jax.ShapeDtypeStruct((rows, cols), jnp.bfloat16),
            jax.ShapeDtypeStruct((pairs, rows, 2 * LANES), jnp.bfloat16),
            jax.ShapeDtypeStruct((pairs, 2, span), jnp.float32),
            jax.ShapeDtypeStruct((rows, width), jnp.bfloat16),
        ],
        scratch_shapes=[
            pltpu.VMEM((2, LANES, span), jnp.float32 if length <= 4096 else jnp.bfloat16),
            pltpu.VMEM((2, LANES, span), jnp.float32),
            pltpu.VMEM((length, LANES), jnp.float32),
            pltpu.VMEM((length, LANES), jnp.float32),
            pltpu.VMEM((n_ctx, rows, 2 * LANES), jnp.bfloat16),
            pltpu.VMEM((pairs, n_ctx, rows, 2 * LANES), jnp.bfloat16),
            pltpu.SemaphoreType.DMA((pairs, n_ctx)),
            pltpu.SemaphoreType.DMA((pairs, n_ctx)),
        ]
        + LineSum.scratch(rows, width, SUM_ROWS),
        compiler_params=pltpu.CompilerParams(
            collective_id=1, has_side_effects=True, vmem_limit_bytes=60 * MIB
        ),
        cost_estimate=pl.CostEstimate(flops=40 * rows * length * cols, bytes_accessed=24 * length * cols, transcendentals=rows * length * cols // DH),
    )(query, key_value, key_value, grad, mixed, logs, lines, part)


def tail_kernel(
    n_fsdp,
    n_ctx,
    n_tp,
    blocks,
    sum_rows,
    part_ref,
    small_ref,
    grad_ref,
    scale_ref,
    s_right,
    p_right,
    s_left,
    p_left,
    w_ref,
    new_right,
    new_left,
    new_w,
    total_ref,
    small_out,
    turned,
    direction,
    squares,
    plane_got,
    line_got,
    line_own,
    plane_send,
    plane_sem,
    tp_send,
    tp_sem,
    left,
    right,
    stage,
    total,
    sems,
):
    turn = pl.program_id(0)
    turns = pl.num_programs(0)
    rights, lefts = blocks
    line = LineSum("tp", n_tp, SUM_ROWS, part_ref.shape[0] // SUM_ROWS // 2, part_ref, left, right, stage, total, sems)
    here = lax.axis_index("fsdp") * n_ctx + lax.axis_index("ctx")
    tp_here = lax.axis_index("tp")
    shards = n_fsdp * n_ctx
    plane = [(f * n_ctx + c, {"fsdp": f, "ctx": c}) for f in range(n_fsdp) for c in range(n_ctx)]
    column = [(t, {"tp": t}) for t in range(n_tp)]
    other = jnp.where(here == 0, 1, 0)
    other_where = {"fsdp": other // n_ctx, "ctx": other % n_ctx}
    other_tp = {"tp": jnp.where(tp_here == 0, 1, 0)}
    middle = rights + 2

    def plane_copy(number, where):
        return remote(small_ref.at[number], plane_got.at[here], plane_send.at[number], plane_sem.at[here], where)

    def tp_copy(number, where):
        return remote(line_own, line_got.at[tp_here], tp_send.at[number], tp_sem.at[tp_here], where)

    @pl.when(turn == 0)
    def _():
        barrier = pltpu.get_barrier_semaphore()
        greet(barrier, here, plane)
        greet(barrier, tp_here, column)
        squares[...] = jnp.zeros_like(squares)
        pl.semaphore_wait(barrier, shards - 1 + n_tp - 1)
        for number, where in plane:

            @pl.when(number != here)
            def _():
                plane_copy(number, where).start()

        plane_got[here] = small_ref[here]

    @pl.when(turn == middle)
    def _():
        for number, where in plane:

            @pl.when(number != here)
            def _():
                remote(plane_got.at[number], plane_got.at[number], plane_sem.at[number], plane_sem.at[number], other_where).wait_recv()

        added = plane_got[0]
        largest = plane_got[0]
        for number in range(1, shards):
            added = added + plane_got[number]
            largest = jnp.maximum(largest, plane_got[number])
        row = lax.broadcasted_iota(jnp.int32, added.shape, 0)
        line_own[...] = jnp.where(row == sum_rows + 1, largest, added)
        for number, where in column:

            @pl.when(number != tp_here)
            def _():
                tp_copy(number, where).start()

        line_got[tp_here] = line_own[...]

    def one(number, carry):
        line.step(number)
        return carry

    lax.fori_loop(turn * line.steps // turns, (turn + 1) * line.steps // turns, one, 0)

    @pl.when(turn < rights)
    def _():
        spot = pl.ds(pl.multiple_of(turn * LANES, LANES), LANES)
        grad = grad_ref[...]
        new_right[...] = decay * s_right[...] + (1.0 - decay) * dot_nt(grad_ref[spot, :], grad)
        turned[spot, :] = dot_nn(p_right[...].astype(jnp.bfloat16), grad).astype(jnp.bfloat16)

    @pl.when((turn >= rights) & (turn < rights + lefts))
    def _():
        spot = pl.ds(pl.multiple_of((turn - rights) * LANES, LANES), LANES)
        new_left[...] = decay * s_left[...] + (1.0 - decay) * dot_tn(grad_ref[:, spot], grad_ref[...])
        value = dot_nn(turned[...], p_left[...].astype(jnp.bfloat16))
        squares[...] = squares[...] + jnp.sum(value * value, 0, keepdims=True)
        direction[:, spot] = value.astype(jnp.bfloat16)

    @pl.when(turn >= rights + lefts)
    def _():
        spot = pl.ds(pl.multiple_of((turn - rights - lefts) * LANES, LANES), LANES)
        mean = jnp.sum(squares[0:1, :], 1, keepdims=True) / (grad_ref.shape[0] * grad_ref.shape[1])
        factor = scale_ref[0:1, 0:1] * lax.rsqrt(mean + step_epsilon)
        new_w[...] = w_ref[...] - factor * direction[spot, :].astype(jnp.float32)

    @pl.when(turn == turns - 1)
    def _():
        total_ref[...] = total[...]
        for number, where in column:

            @pl.when(number != tp_here)
            def _():
                remote(line_got.at[number], line_got.at[number], tp_sem.at[number], tp_sem.at[number], other_tp).wait_recv()

        added = line_got[0]
        for number in range(1, n_tp):
            added = added + line_got[number]
        row = lax.broadcasted_iota(jnp.int32, added.shape, 0)
        small_out[...] = jnp.where(row < sum_rows, added, line_own[...])
        for number, where in plane:

            @pl.when(number != here)
            def _():
                plane_copy(number, where).wait_send()

        for number, where in column:

            @pl.when(number != tp_here)
            def _():
                tp_copy(number, where).wait_send()

        line.finish()


def tail(part, small, sum_rows, grad, scale, left, right, weight):
    rows, width = part.shape
    deep, wide = grad.shape
    n_fsdp, n_ctx, n_tp = lax.axis_size("fsdp"), lax.axis_size("ctx"), lax.axis_size("tp")
    rights, lefts = deep // LANES, wide // LANES
    turns = 2 * rights + lefts
    small_rows = small.shape[1]
    vmem = pl.BlockSpec(memory_space=pltpu.VMEM)

    def at_right(turn):
        return jnp.minimum(turn, rights - 1)

    def at_left(turn):
        return jnp.clip(turn - rights, 0, lefts - 1)

    def at_weight(turn):
        return jnp.clip(turn - rights - lefts, 0, rights - 1)

    return pl.pallas_call(
        functools.partial(tail_kernel, n_fsdp, n_ctx, n_tp, (rights, lefts), sum_rows),
        grid=(turns,),
        in_specs=[
            vmem,
            vmem,
            vmem,
            vmem,
            pl.BlockSpec((None, LANES, deep), lambda t: (0, at_right(t), 0)),
            pl.BlockSpec((None, LANES, deep), lambda t: (1, at_right(t), 0)),
            pl.BlockSpec((None, LANES, wide), lambda t: (0, at_left(t), 0)),
            pl.BlockSpec((None, wide, LANES), lambda t: (1, 0, at_left(t))),
            pl.BlockSpec((LANES, wide), lambda t: (at_weight(t), 0)),
        ],
        out_specs=[
            pl.BlockSpec((LANES, deep), lambda t: (at_right(t), 0)),
            pl.BlockSpec((LANES, wide), lambda t: (at_left(t), 0)),
            pl.BlockSpec((LANES, wide), lambda t: (at_weight(t), 0)),
            vmem,
            vmem,
        ],
        out_shape=[
            jax.ShapeDtypeStruct((deep, deep), jnp.float32),
            jax.ShapeDtypeStruct((wide, wide), jnp.float32),
            jax.ShapeDtypeStruct((deep, wide), jnp.float32),
            jax.ShapeDtypeStruct((rows, width), jnp.bfloat16),
            jax.ShapeDtypeStruct((small_rows, LANES), jnp.float32),
        ],
        scratch_shapes=[
            pltpu.VMEM((deep, wide), jnp.bfloat16),
            pltpu.VMEM((deep, wide), jnp.bfloat16),
            pltpu.VMEM((1, LANES), jnp.float32),
            pltpu.VMEM((n_fsdp * n_ctx, small_rows, LANES), jnp.float32),
            pltpu.VMEM((n_tp, small_rows, LANES), jnp.float32),
            pltpu.VMEM((small_rows, LANES), jnp.float32),
            pltpu.SemaphoreType.DMA((n_fsdp * n_ctx,)),
            pltpu.SemaphoreType.DMA((n_fsdp * n_ctx,)),
            pltpu.SemaphoreType.DMA((n_tp,)),
            pltpu.SemaphoreType.DMA((n_tp,)),
        ]
        + LineSum.scratch(rows, width, SUM_ROWS),
        compiler_params=pltpu.CompilerParams(
            collective_id=2, has_side_effects=True, vmem_limit_bytes=56 * MIB
        ),
        cost_estimate=pl.CostEstimate(
            flops=8 * deep * wide * (deep + wide), bytes_accessed=240 * rows * width, transcendentals=0
        ),
    )(part, small, grad, scale, right, right, left, left, weight)


GELU_A = 0.7978845608028654
GELU_B = 0.044715


def expert_kernel(x_ref, plain_ref, other_ref, here_ref, w_ref, router_ref, sent_ref, hidden_ref, mixed_ref, choice_ref):
    half = w_ref.shape[0] // 2
    rows = x_ref[...]
    first = dot_nt(rows, w_ref[:half, :])
    second = dot_nt(rows, w_ref[half:, :])
    logits = dot_nn(rows, router_ref[...])
    lane = lax.broadcasted_iota(jnp.int32, logits.shape, 1)
    contrast = (lane == here_ref[0:1, 0:1]).astype(jnp.float32) - (lane == other_ref[...]).astype(jnp.float32)
    gate = jax.nn.sigmoid(jnp.sum(logits * contrast, 1, keepdims=True))
    square = first * first
    bent = jnp.tanh(GELU_A * first * (1.0 + GELU_B * square))
    rise = 0.5 * (1.0 + bent)
    gelu = first * rise
    slope = rise + 0.5 * GELU_A * first * (1.0 - bent * bent) * (1.0 + 3.0 * GELU_B * square)
    hidden = gelu * second
    plain = plain_ref[...]
    grad_gate = jnp.sum(plain * hidden, 1, keepdims=True)
    choice = (gate * (1.0 - gate) * grad_gate * contrast).astype(jnp.bfloat16)
    scaled = gate * plain
    grad_first = (scaled * second * slope).astype(jnp.bfloat16)
    grad_second = (scaled * gelu).astype(jnp.bfloat16)
    hidden_ref[...] = (gate * hidden).astype(jnp.bfloat16)
    mixed_ref[0] = grad_first
    mixed_ref[1] = grad_second
    choice_ref[...] = choice
    sent = dot_nn(grad_first, w_ref[:half, :]) + dot_nn(grad_second, w_ref[half:, :])
    sent_ref[...] = (sent + dot_nt(choice, router_ref[...])).astype(jnp.bfloat16)


def expert_chain(rows, plain, other, here, weight, router):
    count, width = rows.shape
    half = weight.shape[0] // 2
    tile = 320
    vmem = pl.BlockSpec(memory_space=pltpu.VMEM)
    return pl.pallas_call(
        expert_kernel,
        grid=(count // tile,),
        in_specs=[
            pl.BlockSpec((tile, width), lambda t: (t, 0)),
            pl.BlockSpec((tile, half), lambda t: (t, 0)),
            pl.BlockSpec((tile, 1), lambda t: (t, 0)),
            vmem,
            vmem,
            vmem,
        ],
        out_specs=[
            pl.BlockSpec((tile, width), lambda t: (t, 0)),
            pl.BlockSpec((tile, half), lambda t: (t, 0)),
            pl.BlockSpec((2, tile, half), lambda t: (0, t, 0)),
            pl.BlockSpec((tile, LANES), lambda t: (t, 0)),
        ],
        out_shape=[
            jax.ShapeDtypeStruct((count, width), jnp.bfloat16),
            jax.ShapeDtypeStruct((count, half), jnp.bfloat16),
            jax.ShapeDtypeStruct((2, count, half), jnp.bfloat16),
            jax.ShapeDtypeStruct((count, LANES), jnp.bfloat16),
        ],
        compiler_params=pltpu.CompilerParams(vmem_limit_bytes=48 * MIB),
        cost_estimate=pl.CostEstimate(
            flops=8 * count * width * half, bytes_accessed=16 * count * width, transcendentals=count * half
        ),
    )(rows, plain, other, here, weight, router)


def normalize(values, gain):
    return values * lax.rsqrt(jnp.mean(values * values, -1, keepdims=True) + norm_epsilon) * gain


def gated_gelu(both):
    return jax.nn.gelu(both[..., 0, :], approximate=True) * both[..., 1, :]


def precondition(grad, master, left, right):
    low = grad.astype(jnp.bfloat16)
    new_left = decay * left[0] + (1.0 - decay) * dot_nt(low, low)
    new_right = decay * right[0] + (1.0 - decay) * dot_tn(low, low)
    turned = dot_nn(left[1].astype(jnp.bfloat16), low).astype(jnp.bfloat16)
    direction = dot_nn(turned, right[1].astype(jnp.bfloat16))
    size = jnp.sqrt(jnp.mean(master * master) + step_epsilon)
    step = (
        matrix_rate * size * direction * lax.rsqrt(jnp.mean(direction * direction) + step_epsilon)
    )
    return (new_left, new_right, master - step)


def adapt(grad, moment, master, rate):
    new_moment = decay * moment + (1.0 - decay) * grad * grad
    return (new_moment, master - rate * grad * lax.rsqrt(new_moment + moment_epsilon))


def barrier(*values):
    return lax.optimization_barrier(values)


def crossing(values):
    return lax.all_to_all(values, ("fsdp", "ctx"), split_axis=0, concat_axis=0, tiled=True)


def on_device(
    tokens,
    cotangent,
    routes,
    buckets,
    attention_in,
    attention_out,
    router,
    gains,
    bias_table,
    expert_in,
    expert_out,
    attention_in_left,
    attention_in_right,
    attention_out_left,
    attention_out_right,
    expert_in_left,
    expert_in_right,
    expert_out_left,
    expert_out_right,
    router_moment,
    gains_moment,
    table_moment,
):
    low = jnp.bfloat16
    rows = tokens.shape[0]
    width = tokens.shape[1]
    shards = lax.axis_size("fsdp") * lax.axis_size("ctx")
    n_ctx = lax.axis_size("ctx")
    n_tp = lax.axis_size("tp")
    here = lax.axis_index("fsdp") * n_ctx + lax.axis_index("ctx")
    tp_here = lax.axis_index("tp")
    length = rows * n_ctx
    depth = attention_in.shape[1]
    head_cols = attention_in.shape[2]
    local_heads = head_cols // DH
    head_pairs = head_cols // LANES
    table_size = bias_table.shape[0]
    experts = router.shape[1]
    capacity = rows * TOPK * 5 // (4 * experts)
    slots_all = experts * capacity
    span = length + rows

    sizes = (depth * experts, 2 * depth, table_size * local_heads)
    small = jnp.concatenate(
        [router.astype(low).reshape(-1), gains.astype(low).reshape(-1), bias_table.astype(low).reshape(-1)]
    )
    small = jnp.pad(small, (0, -small.shape[0] % (16 * head_cols))).reshape(-1, head_cols)
    gathered = lax.all_gather(
        jnp.concatenate(
            [
                attention_in.astype(low).reshape(3 * depth, head_cols),
                attention_out.astype(low).reshape(depth, head_cols),
                small,
            ],
            0,
        ),
        ("fsdp", "ctx"),
        axis=0,
        tiled=False,
    )
    entry_full = (
        gathered[:, : 3 * depth]
        .reshape(shards, 3, depth, head_cols)
        .transpose(1, 0, 2, 3)
        .reshape(3, width, head_cols)
    )
    exit_own = (
        gathered[:, 3 * depth : 4 * depth]
        .reshape(shards, head_cols, depth)
        .transpose(1, 0, 2)
        .reshape(head_cols, width)
    )
    small = gathered[:, 4 * depth :].reshape(shards, -1)
    router_full = small[:, : sizes[0]].reshape(width, experts)
    gains_full = (
        small[:, sizes[0] : sizes[0] + sizes[1]]
        .reshape(shards, 2, depth)
        .transpose(1, 0, 2)
        .reshape(2, width)
    )
    table_full = small[:, sizes[0] + sizes[1] : sum(sizes)].reshape(shards * table_size, local_heads)
    gain_first = gains_full[0].astype(jnp.float32)
    gain_second = gains_full[1].astype(jnp.float32)
    expand_out = expert_out[0].astype(low)

    chosen = routes.reshape(-1)
    route_hits = (chosen[:, None] == jnp.arange(experts, dtype=jnp.int32)[None, :]).astype(
        jnp.int32
    )
    slots = jnp.sum(route_hits * (jnp.cumsum(route_hits, 0) - 1), 1)
    slot_rows = (chosen * capacity + slots).reshape(rows, TOPK)
    place = jnp.arange(slots_all, dtype=jnp.int32)
    first_hit = place[:, None] == slot_rows[None, :, 0]
    second_hit = place[:, None] == slot_rows[None, :, 1]
    picks = (first_hit | second_hit).astype(low)
    other = jnp.sum(
        jnp.where(first_hit, routes[None, :, 1], 0) + jnp.where(second_hit, routes[None, :, 0], 0),
        1,
    )
    grad_buffer = dot_nn(picks, cotangent).astype(low).reshape(experts, capacity, width)
    other_arrived = crossing(other.reshape(experts, capacity)).reshape(-1)

    inputs = tokens.astype(jnp.float32)
    first = normalize(inputs, gain_first).astype(low)
    projected = jnp.einsum(
        "sd,kde->kse", first, entry_full, preferred_element_type=jnp.float32
    )
    query = (projected[0].astype(low) * (DH**-0.5)).astype(low)
    own_pairs = (
        projected[1:].astype(low).reshape(2, rows, head_pairs, LANES).transpose(2, 0, 1, 3)
    )
    low_end = length - rows - lax.axis_index("ctx") * rows
    near = lax.dynamic_slice_in_dim(jnp.pad(buckets, (0, 1)), low_end, span, 0)
    hits = (near[:, None] == jnp.arange(table_full.shape[0], dtype=jnp.int32)[None, :]).astype(low)
    lines = lax.dot_general(
        table_full, hits, (((0,), (1,)), ((), ())), preferred_element_type=jnp.float32
    ).reshape(head_pairs, 2, span)
    hits_back = (near[::-1][:, None] == jnp.arange(table_full.shape[0], dtype=jnp.int32)[None, :]).astype(low)
    back_lines = lax.dot_general(
        table_full, hits_back, (((0,), (1,)), ((), ())), preferred_element_type=jnp.float32
    ).reshape(head_pairs, 2, span)
    exit_all = lax.dynamic_update_slice_in_dim(
        jnp.zeros((n_tp * head_cols, width), low), exit_own, tp_here * head_cols, 0
    )
    for shift in range(1, n_tp):
        piece = lax.ppermute(exit_own, "tp", [(i, (i + shift) % n_tp) for i in range(n_tp)])
        exit_all = lax.dynamic_update_slice_in_dim(
            exit_all, piece, (tp_here + n_tp - shift) % n_tp * head_cols, 0
        )
    mixed, logs, peak_own, key_value, mixed_all, grad_arrived = attend(
        query, own_pairs, lines, grad_buffer
    )
    grad_arrived = grad_arrived.reshape(slots_all, width)
    value = dot_nn(mixed_all, exit_all)
    middle = inputs + value
    second = normalize(middle, gain_second).astype(low)

    buffer = dot_nn(picks, second).astype(low).reshape(experts, capacity, width)
    arrived = crossing(buffer).reshape(slots_all, width)
    columns = 2 * expert_in.shape[3]
    flat_master = expert_in[0].transpose(1, 2, 0).reshape(columns, width)
    flat_low = flat_master.astype(low)
    wide_router = jnp.pad(router_full, ((0, 0), (0, LANES - experts)))
    plain_grad = dot_nt(grad_arrived, expand_out)
    arrived, plain_grad, flat_low, wide_router = barrier(arrived, plain_grad, flat_low, wide_router)
    sent_grads, gated_hidden, grad_mixed_up, grad_choice = expert_chain(
        arrived,
        plain_grad,
        other_arrived[:, None],
        jnp.full((8, LANES), here, jnp.int32),
        flat_low,
        wide_router,
    )
    back_grads = crossing(sent_grads.reshape(experts, capacity, width)).reshape(slots_all, width)

    sent_rows = dot_nn(gated_hidden, expand_out).astype(low)
    grad_router = dot_tn(arrived, grad_choice)[:, :experts]
    grad_expand_out = dot_tn(gated_hidden, grad_arrived)
    shrink_left, shrink_right, shrink_new = precondition(
        grad_expand_out, expert_out[0], expert_out_left, expert_out_right
    )
    grad_expand_in = jnp.einsum(
        "gsf,sd->gfd", grad_mixed_up, arrived, preferred_element_type=jnp.float32
    )
    back_grads, sent_rows, grad_router, grad_expand_out, grad_expand_in, shrink_left, shrink_right, shrink_new = barrier(
        back_grads, sent_rows, grad_router, grad_expand_out, grad_expand_in, shrink_left, shrink_right, shrink_new
    )
    grad_second = combine_sum(slot_rows, back_grads, rows)

    back_rows = crossing(sent_rows.reshape(experts, capacity, width)).reshape(slots_all, width)
    grad_second, back_rows = barrier(grad_second, back_rows)
    result_part = dot_tn(picks, back_rows).astype(low)

    unused, pull = jax.vjp(normalize, middle, gain_second)
    grad_middle_norm, grad_gain_second = pull(grad_second.astype(jnp.float32))
    grad_middle = cotangent.astype(jnp.float32) + grad_middle_norm
    grad_attention = grad_middle.astype(low)
    grad_mixed = dot_nt(grad_attention, exit_own).astype(low)
    grad_query, key_value_grad, sums, result_sum = attend_back(
        query, key_value, grad_mixed, mixed, logs, back_lines, result_part
    )
    result = (middle + result_sum.astype(jnp.float32)).astype(low)
    grad_projected = jnp.stack(
        [
            grad_query,
            jnp.concatenate([key_value_grad[pair, :, :LANES] for pair in range(head_pairs)], 1),
            jnp.concatenate([key_value_grad[pair, :, LANES:] for pair in range(head_pairs)], 1),
        ]
    )
    grad_exit = dot_tn(mixed, grad_attention).astype(low)
    grad_first_part = jnp.einsum(
        "kse,kde->sd", grad_projected, entry_full, preferred_element_type=jnp.float32
    )
    unused, pull = jax.vjp(normalize, inputs, gain_first)
    grad_gain_first = pull(grad_first_part)[1]
    grad_entry = jnp.einsum(
        "sd,kse->dke", first, grad_projected, preferred_element_type=jnp.float32
    ).astype(low)
    table_grad = lax.dot_general(
        hits_back.astype(jnp.float32),
        sums.reshape(local_heads, span),
        (((0,), (1,)), ((), ())),
        precision=highest,
        preferred_element_type=jnp.float32,
    )
    gain_sums = jnp.stack([grad_gain_first, jnp.where(tp_here == 0, grad_gain_second, 0.0)])
    peak_own = peak_own[:, :, 0].reshape(local_heads)
    pieces = [
        grad_router.reshape(shards, -1),
        gain_sums.reshape(2, shards, depth).transpose(1, 0, 2).reshape(shards, -1),
        table_grad.reshape(shards, -1),
        jnp.broadcast_to(peak_own[None], (shards, local_heads)),
    ]
    spots = [0]
    padded = []
    for piece in pieces:
        padded.append(jnp.pad(piece, ((0, 0), (0, -piece.shape[1] % LANES))))
        spots.append(spots[-1] + padded[-1].shape[1] // LANES)
    small = jnp.concatenate(padded, 1)
    small = jnp.pad(small, ((0, 0), (0, -small.shape[1] % (8 * LANES)))).reshape(shards, -1, LANES)
    size = jnp.sqrt(jnp.mean(flat_master * flat_master) + step_epsilon)
    weight_terms = jnp.concatenate(
        [
            grad_entry.reshape(shards, 3 * depth, head_cols),
            grad_exit.reshape(head_cols, shards, depth)
            .transpose(1, 0, 2)
            .reshape(shards, depth, head_cols),
        ],
        1,
    )
    first_part, small, weight_terms = barrier(grad_first_part.astype(low), small, weight_terms)
    weight_terms = crossing(weight_terms)
    expand_right, expand_left, expand_new, grad_first, small_sum = tail(
        first_part,
        small,
        spots[2],
        grad_expand_in.reshape(columns, width).astype(low),
        jnp.full((8, LANES), matrix_rate * size, jnp.float32),
        expert_in_left,
        expert_in_right,
        flat_master,
    )
    grad_first, weight_terms = barrier(grad_first, weight_terms)
    owned = jnp.sum(weight_terms.astype(jnp.float32), 0)
    owned_in = owned[: 3 * depth].reshape(depth, 3, head_cols).transpose(1, 0, 2)
    owned_out = owned[3 * depth :].reshape(head_cols, depth)
    grad_tokens = grad_middle + pull(grad_first.astype(jnp.float32))[0]

    def small_piece(number, shape):
        count = 1
        for extent in shape:
            count *= extent
        return small_sum[spots[number] : spots[number + 1]].reshape(-1)[:count].reshape(shape)

    owned_router = small_piece(0, (depth, experts))
    owned_gains = small_piece(1, (2, depth))
    owned_table = small_piece(2, (table_size, local_heads))
    peaks = small_piece(3, (local_heads,))
    in_left, in_right, in_new = jax.vmap(precondition)(
        owned_in,
        attention_in,
        jnp.swapaxes(attention_in_left, 0, 1),
        jnp.swapaxes(attention_in_right, 0, 1),
    )
    column = jnp.sqrt(jnp.repeat(clip_level / jnp.maximum(peaks, clip_level), DH))
    in_new = in_new * jnp.stack([column, column, jnp.ones_like(column)])[:, None, :]
    out_left, out_right, out_new = precondition(
        owned_out, attention_out, attention_out_left, attention_out_right
    )
    router_moment_new, router_new = adapt(owned_router, router_moment, router, router_rate)
    gains_moment_new, gains_new = adapt(owned_gains, gains_moment, gains, gain_rate)
    table_moment_new, table_new = adapt(owned_table, table_moment, bias_table, table_rate)
    return (
        result,
        grad_tokens,
        owned_in,
        in_new,
        in_left,
        in_right,
        owned_out,
        out_new,
        out_left,
        out_right,
        grad_expand_in.transpose(2, 0, 1)[None],
        expand_new.reshape(2, -1, width).transpose(2, 0, 1)[None],
        expand_left,
        expand_right,
        grad_expand_out[None],
        shrink_new[None],
        shrink_left,
        shrink_right,
        owned_router,
        router_moment_new,
        router_new,
        owned_gains,
        gains_moment_new,
        gains_new,
        owned_table,
        table_moment_new,
        table_new,
    )


def solution(mesh):
    placed = (
        P(("fsdp", "ctx"), None),
        P(("fsdp", "ctx"), None),
        P(("fsdp", "ctx"), None),
        P(),
        P(None, ("fsdp", "ctx"), "tp"),
        P("tp", ("fsdp", "ctx")),
        P(("fsdp", "ctx"), None),
        P(None, ("fsdp", "ctx")),
        P(("fsdp", "ctx"), "tp"),
        P(("fsdp", "ctx"), None, None, "tp"),
        P(("fsdp", "ctx"), "tp", None),
        P(None, None, ("fsdp", "ctx", "tp"), None),
        P(None, None, ("fsdp", "ctx", "tp"), None),
        P(None, ("fsdp", "ctx", "tp"), None),
        P(None, ("fsdp", "ctx", "tp"), None),
        P(None, ("fsdp", "ctx", "tp"), None),
        P(None, ("fsdp", "ctx", "tp"), None),
        P(None, ("fsdp", "ctx", "tp"), None),
        P(None, ("fsdp", "ctx", "tp"), None),
        P(("fsdp", "ctx"), None),
        P(None, ("fsdp", "ctx")),
        P(("fsdp", "ctx"), "tp"),
    )
    return jax.shard_map(
        on_device,
        mesh=mesh,
        in_specs=placed,
        out_specs=(
            P(("fsdp", "ctx"), None),
            P(("fsdp", "ctx"), None),
            P(None, ("fsdp", "ctx"), "tp"),
            P(None, ("fsdp", "ctx"), "tp"),
            P(None, ("fsdp", "ctx", "tp"), None),
            P(None, ("fsdp", "ctx", "tp"), None),
            P("tp", ("fsdp", "ctx")),
            P("tp", ("fsdp", "ctx")),
            P(("fsdp", "ctx", "tp"), None),
            P(("fsdp", "ctx", "tp"), None),
            P(("fsdp", "ctx"), None, None, "tp"),
            P(("fsdp", "ctx"), None, None, "tp"),
            P(("fsdp", "ctx", "tp"), None),
            P(("fsdp", "ctx", "tp"), None),
            P(("fsdp", "ctx"), "tp", None),
            P(("fsdp", "ctx"), "tp", None),
            P(("fsdp", "ctx", "tp"), None),
            P(("fsdp", "ctx", "tp"), None),
            P(("fsdp", "ctx"), None),
            P(("fsdp", "ctx"), None),
            P(("fsdp", "ctx"), None),
            P(None, ("fsdp", "ctx")),
            P(None, ("fsdp", "ctx")),
            P(None, ("fsdp", "ctx")),
            P(("fsdp", "ctx"), "tp"),
            P(("fsdp", "ctx"), "tp"),
            P(("fsdp", "ctx"), "tp"),
        ),
        check_vma=False,
    )
```

```python
import functools

import jax
import jax.numpy as jnp
from jax import lax
from jax.experimental import pallas as pl
from jax.experimental.pallas import tpu as pltpu

from jax.sharding import PartitionSpec as P

DH = 64
LANES = 128
MIB = 1024 * 1024


TOPK = 2

highest = lax.Precision.HIGHEST
norm_epsilon = 1e-06
step_epsilon = 1e-06
moment_epsilon = 1e-08
clip_level = 4.0
decay = 0.5
matrix_rate = 0.3
gain_rate = 0.25
router_rate = 0.01
table_rate = 0.3


def dot_nt(left, right):
    return lax.dot_general(left, right, (((1,), (1,)), ((), ())), preferred_element_type=jnp.float32)


def dot_nn(left, right):
    return lax.dot_general(left, right, (((1,), (0,)), ((), ())), preferred_element_type=jnp.float32)


def dot_tn(left, right):
    return lax.dot_general(left, right, (((0,), (0,)), ((), ())), preferred_element_type=jnp.float32)


def half_mask(shape, half):
    lane = lax.broadcasted_iota(jnp.int32, shape, 1)
    return (lane // DH) == half


def attend_kernel(length, rows, tile, pairs, n_fsdp, n_ctx, n_tp, q_ref, own_ref, line_ref, cross_ref, mixed_ref, log_ref, peak_ref, kv_out, all_out, cross_out, strip, wide, kv_ref, all_ref, kv_send, kv_got, mix_send, mix_got, out_sem, cross_send, cross_got):
    pair = pl.program_id(0)
    step = pl.program_id(1)
    steps = rows // tile
    span = line_ref.shape[2]
    here = lax.axis_index("ctx")
    tp_here = lax.axis_index("tp")
    own_rows = pl.ds(pl.multiple_of(here * rows, rows), rows)
    ctx_peers = [(number, {"ctx": number}) for number in range(n_ctx)]
    tp_peers = [(number, {"tp": number}) for number in range(n_tp)]
    shard = lax.axis_index("fsdp") * n_ctx + here
    plane = [(f * n_ctx + c, {"fsdp": f, "ctx": c}) for f in range(n_fsdp) for c in range(n_ctx)]
    other = jnp.where(shard == 0, 1, 0)
    other_plane = {"fsdp": other // n_ctx, "ctx": other % n_ctx}
    other_ctx = {"ctx": jnp.where(here == 0, 1, 0)}
    other_tp = {"tp": jnp.where(tp_here == 0, 1, 0)}

    def kv_copy(slot, number, where):
        return remote(
            own_ref.at[slot], kv_ref.at[slot, :, own_rows, :], kv_send.at[slot, number], kv_got.at[slot, here], where
        )

    def kv_arrived(slot, number):
        spot = kv_ref.at[slot, :, pl.ds(number * rows, rows), :]
        remote(spot, spot, kv_got.at[slot, number], kv_got.at[slot, number], other_ctx).wait_recv()

    def cross_copy(number, where):
        return remote(
            cross_ref.at[number], cross_out.at[shard], cross_send.at[number], cross_got.at[shard], where
        )

    def cross_own():
        return pltpu.make_async_copy(cross_ref.at[shard], cross_out.at[shard], out_sem.at[2])

    def mix_spot(slot, turn, number):
        return (
            pl.ds(pl.multiple_of(turn * tile, tile), tile),
            pl.ds(pl.multiple_of((number * pairs + slot) * LANES, LANES), LANES),
        )

    def mix_copy(slot, turn, number, where):
        spot = all_ref.at[mix_spot(slot, turn, tp_here)]
        return remote(spot, spot, mix_send.at[slot, turn, number], mix_got.at[slot, turn, tp_here], where)

    @pl.when((pair == 0) & (step == 0))
    def _():
        barrier = pltpu.get_barrier_semaphore()
        greet(barrier, shard, plane)
        greet(barrier, tp_here, tp_peers)
        pl.semaphore_wait(barrier, n_fsdp * n_ctx - 1 + n_tp - 1)
        for slot in range(pairs):
            for number, where in ctx_peers:

                @pl.when(number != here)
                def _():
                    kv_copy(slot, number, where).start()

            kv_ref[slot, :, own_rows, :] = own_ref[slot]

    @pl.when(step == 0)
    def _():
        for half in range(2):
            line = jnp.broadcast_to(line_ref[0, half : half + 1, :], (LANES, span))
            strip[half] = pltpu.roll(line, span - (LANES - 1), 1, stride=1, stride_axis=0)
        wide[:, LANES:] = jnp.ones((length, LANES), jnp.bfloat16)
        peak_ref[...] = jnp.full(peak_ref.shape, -jnp.inf, jnp.float32)
        for number, where in ctx_peers:

            @pl.when(number != here)
            def _():
                kv_arrived(pair, number)

        wide[:, :LANES] = kv_ref[pair, 1]

    @pl.when((pair == 0) & (step == 2))
    def _():
        cross_own().start()
        for number, where in plane:

            @pl.when(number != shard)
            def _():
                cross_copy(number, where).start()

    query = q_ref[...]
    groups = tile // LANES
    last = rows // LANES - 1
    mixed = jnp.zeros((tile, LANES), jnp.float32)
    for half in range(2):
        mine = half_mask((tile, LANES), half)
        own = jnp.where(mine, query, jnp.zeros_like(query))
        logit = dot_nt(own, kv_ref[pair, 0])
        top = jnp.max(logit, 1, keepdims=True)
        bias = []
        for group in range(groups):
            start = pl.multiple_of((last - (step * groups + group)) * LANES, LANES)
            bias.append(strip[half, :, pl.ds(start, length)])
        bias = jnp.concatenate(bias, 0) if groups > 1 else bias[0]
        powers = jnp.exp(logit + bias - top)
        both = dot_nn(powers.astype(jnp.bfloat16), wide[...])
        total = both[:, LANES:]
        mixed = jnp.where(mine, both[:, :LANES] / total, mixed)
        log_total = top + jnp.log(total)
        log_ref[0, half : half + 1, :] = log_total.T[0:1, :]
        best = jnp.max(jnp.broadcast_to(top, (tile, LANES)), 0, keepdims=True)
        peak_ref[0, half : half + 1, :] = jnp.maximum(peak_ref[0, half : half + 1, :], best)
    low = mixed.astype(jnp.bfloat16)
    mixed_ref[...] = low
    all_ref[mix_spot(pair, step, tp_here)] = low
    for number, where in reversed(tp_peers):

        @pl.when(number != tp_here)
        def _():
            mix_copy(pair, step, number, where).start()

    @pl.when((pair == pairs - 1) & (step == steps - 1))
    def _():
        for slot in range(pairs):
            for number, where in ctx_peers:

                @pl.when(number != here)
                def _():
                    kv_copy(slot, number, where).wait_send()

        def one(index, carry):
            slot, turn = index // steps, index % steps
            for number, where in tp_peers:

                @pl.when(number != tp_here)
                def _():
                    spot = all_ref.at[mix_spot(slot, turn, number)]
                    got = mix_got.at[slot, turn, number]
                    remote(spot, spot, got, got, other_tp).wait_recv()
                    mix_copy(slot, turn, number, where).wait_send()

            return carry

        kept = pltpu.make_async_copy(kv_ref, kv_out, out_sem.at[0])
        kept.start()
        lax.fori_loop(0, pairs * steps, one, 0)
        gathered = pltpu.make_async_copy(all_ref, all_out, out_sem.at[1])
        gathered.start()
        kept.wait()
        gathered.wait()
        cross_own().wait()
        for number, where in plane:

            @pl.when(number != shard)
            def _():
                spot = cross_out.at[number]
                remote(spot, spot, cross_got.at[number], cross_got.at[number], other_plane).wait_recv()
                cross_copy(number, where).wait_send()


def attend(query, own, lines, cross):
    rows, cols = query.shape
    n_fsdp, n_ctx, n_tp = lax.axis_size("fsdp"), lax.axis_size("ctx"), lax.axis_size("tp")
    length = rows * n_ctx
    pairs = cols // LANES
    tile = 256 if length <= 4096 else 128
    span = lines.shape[2]
    vmem = pl.BlockSpec(memory_space=pltpu.VMEM)
    return pl.pallas_call(
        functools.partial(attend_kernel, length, rows, tile, pairs, n_fsdp, n_ctx, n_tp),
        grid=(pairs, rows // tile),
        in_specs=[
            pl.BlockSpec((tile, LANES), lambda p, t: (t, p)),
            vmem,
            pl.BlockSpec((1, 2, span), lambda p, t: (p, 0, 0)),
            pl.BlockSpec(memory_space=pl.ANY),
        ],
        out_specs=[
            pl.BlockSpec((tile, LANES), lambda p, t: (t, p)),
            pl.BlockSpec((1, 2, tile), lambda p, t: (p, 0, t)),
            pl.BlockSpec((1, 2, LANES), lambda p, t: (p, 0, 0)),
            pl.BlockSpec(memory_space=pl.ANY),
            pl.BlockSpec(memory_space=pl.ANY),
            pl.BlockSpec(memory_space=pl.ANY),
        ],
        out_shape=[
            jax.ShapeDtypeStruct((rows, cols), jnp.bfloat16),
            jax.ShapeDtypeStruct((pairs, 2, rows), jnp.float32),
            jax.ShapeDtypeStruct((pairs, 2, LANES), jnp.float32),
            jax.ShapeDtypeStruct((pairs, 2, length, LANES), jnp.bfloat16),
            jax.ShapeDtypeStruct((rows, n_tp * cols), jnp.bfloat16),
            jax.ShapeDtypeStruct(cross.shape, cross.dtype),
        ],
        scratch_shapes=[
            pltpu.VMEM((2, LANES, span), jnp.float32),
            pltpu.VMEM((length, 2 * LANES), jnp.bfloat16),
            pltpu.VMEM((pairs, 2, length, LANES), jnp.bfloat16),
            pltpu.VMEM((rows, n_tp * cols), jnp.bfloat16),
            pltpu.SemaphoreType.DMA((pairs, n_ctx)),
            pltpu.SemaphoreType.DMA((pairs, n_ctx)),
            pltpu.SemaphoreType.DMA((pairs, rows // tile, n_tp)),
            pltpu.SemaphoreType.DMA((pairs, rows // tile, n_tp)),
            pltpu.SemaphoreType.DMA((3,)),
            pltpu.SemaphoreType.DMA((n_fsdp * n_ctx,)),
            pltpu.SemaphoreType.DMA((n_fsdp * n_ctx,)),
        ],
        compiler_params=pltpu.CompilerParams(
            collective_id=3, has_side_effects=True, vmem_limit_bytes=60 * MIB
        ),
        cost_estimate=pl.CostEstimate(flops=100 * rows * length * cols, bytes_accessed=8 * length * cols, transcendentals=rows * length * cols // DH),
    )(query, own, lines, cross)


def remote(source, target, send, receive, where):
    return pltpu.make_async_remote_copy(
        src_ref=source,
        dst_ref=target,
        send_sem=send,
        recv_sem=receive,
        device_id=where,
        device_id_type=pl.DeviceIdType.MESH,
    )


def greet(barrier, me, peers):
    for number, where in peers:

        @pl.when(number != me)
        def _():
            pl.semaphore_signal(
                barrier, inc=1, device_id=where, device_id_type=pl.DeviceIdType.MESH
            )


class LineSum:
    def __init__(self, axis, count, size, pairs, own, left, right, stage, total, sems, lag):
        self.lag = lag
        self.axis, self.count, self.size, self.pairs = axis, count, size, pairs
        self.own, self.left, self.right, self.stage, self.total = own, left, right, stage, total
        self.part_send, self.left_got, self.right_got, self.total_got, self.down_send, self.up_send = (
            sems.at[0], sems.at[1], sems.at[2], sems.at[3], sems.at[4], sems.at[5],
        )
        self.owners = ((count - 1) // 2, count // 2)
        self.reach = [max(owner, count - 1 - owner) for owner in self.owners]
        self.steps = pairs + self.lag * 2 * max(self.reach)

    @staticmethod
    def scratch(rows, width, size):
        return [pltpu.VMEM((rows, width), jnp.bfloat16)] * 4 + [
            pltpu.SemaphoreType.DMA((6, rows // size))
        ]

    def signal_neighbours(self, barrier):
        me = lax.axis_index(self.axis)
        for offset, there in ((-1, me > 0), (1, me < self.count - 1)):

            @pl.when(there)
            def _():
                pl.semaphore_signal(
                    barrier,
                    inc=1,
                    device_id={self.axis: me + offset},
                    device_id_type=pl.DeviceIdType.MESH,
                )

    def neighbours(self):
        me = lax.axis_index(self.axis)
        return jnp.where(me > 0, 1, 0) + jnp.where(me < self.count - 1, 1, 0)

    def place(self, side, pair):
        chunk = side * self.pairs + pair
        return chunk, pl.ds(pl.multiple_of(chunk * self.size, self.size), self.size)

    def part_up(self, chunk, rows):
        me = lax.axis_index(self.axis)
        return remote(
            self.stage.at[rows], self.left.at[rows], self.part_send.at[chunk], self.left_got.at[chunk], {self.axis: me + 1}
        )

    def part_down(self, chunk, rows):
        me = lax.axis_index(self.axis)
        return remote(
            self.stage.at[rows], self.right.at[rows], self.part_send.at[chunk], self.right_got.at[chunk], {self.axis: me - 1}
        )

    def total_up(self, chunk, rows):
        me = lax.axis_index(self.axis)
        return remote(
            self.total.at[rows], self.total.at[rows], self.up_send.at[chunk], self.total_got.at[chunk], {self.axis: me + 1}
        )

    def total_down(self, chunk, rows):
        me = lax.axis_index(self.axis)
        return remote(
            self.total.at[rows], self.total.at[rows], self.down_send.at[chunk], self.total_got.at[chunk], {self.axis: me - 1}
        )

    def arrived(self, target, rows, got):
        me = lax.axis_index(self.axis)
        peer = jnp.where(me < self.count - 1, me + 1, me - 1)
        remote(target.at[rows], target.at[rows], got, got, {self.axis: peer}).wait_recv()

    def step(self, number):
        me = lax.axis_index(self.axis)
        last = self.count - 1
        wide = jnp.float32
        for side, owner in enumerate(self.owners):
            reach = self.reach[side]
            from_end = jnp.where(me < owner, me, jnp.where(me > owner, last - me, reach))
            pair = number - self.lag * from_end
            chunk, rows = self.place(side, pair)
            inside = (pair >= 0) & (pair < self.pairs)

            @pl.when(inside & (me == 0) & (me < owner))
            def _():
                self.stage[rows, :] = self.own[rows, :]
                self.part_up(chunk, rows).start()

            @pl.when(inside & (me > 0) & (me < owner))
            def _():
                self.arrived(self.left, rows, self.left_got.at[chunk])
                self.stage[rows, :] = (self.own[rows, :].astype(wide) + self.left[rows, :].astype(wide)).astype(jnp.bfloat16)
                self.part_up(chunk, rows).start()

            @pl.when(inside & (me == last) & (me > owner))
            def _():
                self.stage[rows, :] = self.own[rows, :]
                self.part_down(chunk, rows).start()

            @pl.when(inside & (me < last) & (me > owner))
            def _():
                self.arrived(self.right, rows, self.right_got.at[chunk])
                self.stage[rows, :] = (self.own[rows, :].astype(wide) + self.right[rows, :].astype(wide)).astype(jnp.bfloat16)
                self.part_down(chunk, rows).start()

            @pl.when(inside & (me == owner))
            def _():
                value = self.own[rows, :].astype(wide)
                if owner > 0:
                    self.arrived(self.left, rows, self.left_got.at[chunk])
                    value = value + self.left[rows, :].astype(wide)
                if owner < last:
                    self.arrived(self.right, rows, self.right_got.at[chunk])
                    value = value + self.right[rows, :].astype(wide)
                self.total[rows, :] = value.astype(jnp.bfloat16)
                if owner > 0:
                    self.total_down(chunk, rows).start()
                if owner < last:
                    self.total_up(chunk, rows).start()

            away = jnp.where(me < owner, owner - me, me - owner)
            pair = number - self.lag * (reach + away)
            chunk, rows = self.place(side, pair)
            inside = (pair >= 0) & (pair < self.pairs) & (me != owner)

            @pl.when(inside)
            def _():
                self.arrived(self.total, rows, self.total_got.at[chunk])

            @pl.when(inside & (me < owner) & (me > 0))
            def _():
                self.total_down(chunk, rows).start()

            @pl.when(inside & (me > owner) & (me < last))
            def _():
                self.total_up(chunk, rows).start()

    def finish(self):
        me = lax.axis_index(self.axis)
        last = self.count - 1
        for side, owner in enumerate(self.owners):

            def one(pair, carry):
                chunk, rows = self.place(side, pair)

                @pl.when(me < owner)
                def _():
                    self.part_up(chunk, rows).wait_send()

                @pl.when(me > owner)
                def _():
                    self.part_down(chunk, rows).wait_send()

                @pl.when((me <= owner) & (me > 0))
                def _():
                    self.total_down(chunk, rows).wait_send()

                @pl.when((me >= owner) & (me < last))
                def _():
                    self.total_up(chunk, rows).wait_send()

                return carry

            lax.fori_loop(0, self.pairs, one, 0)


SUM_ROWS = 16
BACK_ROWS = 32


def combine_sum_kernel(count, slots_ref, back_ref, out_ref, own, left, right, stage, total, sems):
    rows, width = own.shape
    places = back_ref.shape[0]
    line = LineSum("tp", count, SUM_ROWS, rows // SUM_ROWS // 2, own, left, right, stage, total, sems, 3)
    barrier = pltpu.get_barrier_semaphore()
    line.signal_neighbours(barrier)
    size, depth = 256, 512

    def one(number, carry):
        spot = pl.ds(pl.multiple_of(number * size, size), size)
        slots = slots_ref[spot, :]
        value = jnp.zeros((size, width), jnp.float32)
        for start in range(0, places, depth):
            lane = lax.broadcasted_iota(jnp.int32, (size, depth), 1) + start
            hit = (lane == slots[:, 0:1]) | (lane == slots[:, 1:2])
            value = value + dot_nn(
                jnp.where(hit, 1.0, 0.0).astype(jnp.bfloat16), back_ref[start : start + depth, :]
            )
        own[spot, :] = value.astype(jnp.bfloat16)
        return carry

    lax.fori_loop(0, rows // size, one, 0)
    pl.semaphore_wait(barrier, line.neighbours())

    def step(number, carry):
        line.step(number)
        return carry

    lax.fori_loop(0, line.steps, step, 0)
    out_ref[...] = total[...]
    line.finish()


def combine_sum(slots, back, rows):
    width = back.shape[1]
    vmem = pl.BlockSpec(memory_space=pltpu.VMEM)
    return pl.pallas_call(
        functools.partial(combine_sum_kernel, lax.axis_size("tp")),
        out_shape=jax.ShapeDtypeStruct((rows, width), jnp.bfloat16),
        in_specs=[vmem, vmem],
        out_specs=vmem,
        scratch_shapes=[pltpu.VMEM((rows, width), jnp.bfloat16)] + LineSum.scratch(rows, width, SUM_ROWS),
        compiler_params=pltpu.CompilerParams(
            collective_id=0, has_side_effects=True, vmem_limit_bytes=48 * MIB
        ),
        cost_estimate=pl.CostEstimate(
            flops=2 * rows * back.shape[0] * width, bytes_accessed=200 * rows * width, transcendentals=0
        ),
    )(slots, back)


def attend_back_kernel(length, rows, tile, chunk, n_pairs_all, n_ctx, n_tp, q_ref, k_ref, v_ref, g_ref, m_ref, log_ref, line_ref, part_ref, dq_ref, dkv_ref, sums_ref, total_ref, strip, gather, dk_ref, dv_ref, mine_ref, got_ref, swap_send, swap_got, left, right, stage, total, sems):
    pair = pl.program_id(0)
    step = pl.program_id(1)
    n_pairs = n_pairs_all
    steps = rows // tile
    span = line_ref.shape[2]
    last = length // LANES - 1
    here = lax.axis_index("ctx")
    turn = pair * steps + step
    line_sum = LineSum("tp", n_tp, BACK_ROWS, part_ref.shape[0] // BACK_ROWS // 2, part_ref, left, right, stage, total, sems, 2)
    barrier = pltpu.get_barrier_semaphore()

    def swap(slot, peer):
        return remote(
            mine_ref.at[peer], got_ref.at[slot, here], swap_send.at[slot, peer], swap_got.at[slot, here], {"ctx": peer}
        )

    def arrival(slot, peer):
        return remote(
            mine_ref.at[peer], got_ref.at[slot, peer], swap_send.at[slot, peer], swap_got.at[slot, peer], {"ctx": peer}
        )

    @pl.when(turn == 0)
    def _():
        line_sum.signal_neighbours(barrier)
        for peer in range(n_ctx):

            @pl.when(peer != here)
            def _():
                pl.semaphore_signal(
                    barrier, inc=1, device_id={"ctx": peer}, device_id_type=pl.DeviceIdType.MESH
                )

        pl.semaphore_wait(barrier, line_sum.neighbours() + (n_ctx - 1))

    @pl.when(step == 0)
    def _():
        for half in range(2):
            line = jnp.broadcast_to(line_ref[0, half : half + 1, :], (LANES, span))
            strip[half] = pltpu.roll(line, span - LANES, 1, stride=1, stride_axis=0).astype(strip.dtype)
        gather[...] = jnp.zeros_like(gather)
        dk_ref[...] = jnp.zeros_like(dk_ref)
        dv_ref[...] = jnp.zeros_like(dv_ref)

    chunks = length // chunk
    turns = n_pairs_all * steps * chunks

    def sum_step(number, carry):
        line_sum.step(number)
        return carry

    query = q_ref[...]
    grad = g_ref[...]
    product = grad.astype(jnp.float32) * m_ref[...].astype(jnp.float32)
    owns, grads, deltas, logs = [], [], [], []
    for half in range(2):
        mine = half_mask((tile, LANES), half)
        owns.append(jnp.where(mine, query, jnp.zeros_like(query)))
        grads.append(jnp.where(mine, grad, jnp.zeros_like(grad)))
        picks = half_mask((8, LANES), half).astype(jnp.float32)
        deltas.append(
            lax.dot_general(picks, product, (((1,), (1,)), ((), ())), precision=lax.Precision.HIGHEST, preferred_element_type=jnp.float32)[0:1, :]
        )
        logs.append(log_ref[0, half : half + 1, :])

    def one_chunk(number, carry):
        outs = []
        now = turn * chunks + number
        lax.fori_loop(now * line_sum.steps // turns, (now + 1) * line_sum.steps // turns, sum_step, 0)
        base = pl.multiple_of(number * chunk, chunk)
        keys = k_ref[pl.ds(base, chunk), :]
        values = v_ref[pl.ds(base, chunk), :]
        new_key = dk_ref[pl.ds(base, chunk), :]
        new_value = dv_ref[pl.ds(base, chunk), :]
        for half in range(2):
            logit = dot_nt(keys, owns[half])
            places = []
            bias = []
            for group in range(chunk // LANES):
                row_group = number * (chunk // LANES) + group
                start = pl.multiple_of((last - row_group) * LANES + step * tile, LANES)
                places.append(start)
                bias.append(strip[half, :, pl.ds(start, tile)].astype(jnp.float32))
            bias = jnp.concatenate(bias, 0) if len(bias) > 1 else bias[0]
            shares = jnp.exp(logit + bias - logs[half])
            grad_shares = dot_nt(values, grads[half])
            scores = shares * (grad_shares - deltas[half])
            low_shares = shares.astype(jnp.bfloat16)
            low_scores = scores.astype(jnp.bfloat16)
            new_value = new_value + dot_nn(low_shares, grads[half])
            new_key = new_key + dot_nn(low_scores, owns[half])
            outs.append(carry[half] + dot_tn(low_scores, keys))
            for group, start in enumerate(places):
                gather[half, :, pl.ds(start, tile)] += scores[group * LANES : (group + 1) * LANES]
        dk_ref[pl.ds(base, chunk), :] = new_key
        dv_ref[pl.ds(base, chunk), :] = new_value
        return tuple(outs)

    zero = jnp.zeros((tile, LANES), jnp.float32)
    first, second = lax.fori_loop(0, length // chunk, one_chunk, (zero, zero))
    both = jnp.where(half_mask((tile, LANES), 0), first, second)
    dq_ref[...] = (both * (DH**-0.5)).astype(dq_ref.dtype)

    @pl.when(step == steps - 1)
    def _():
        for peer in range(n_ctx):
            spot = slice(peer * rows, (peer + 1) * rows)

            @pl.when((peer != here) & (pair > 0))
            def _():
                swap(pair - 1, peer).wait_send()

            mine_ref[peer, :, :LANES] = dk_ref[spot, :].astype(jnp.bfloat16)
            mine_ref[peer, :, LANES:] = dv_ref[spot, :].astype(jnp.bfloat16)

            @pl.when(peer != here)
            def _():
                swap(pair, peer).start()

        got_ref[pair, here] = mine_ref[here]
        for half in range(2):
            values = gather[half]
            size = LANES // 2
            while size >= 1:
                values = values[:size] + pltpu.roll(values[size : 2 * size], span - size, 1)
                size //= 2
            sums_ref[0, half : half + 1, :] = pltpu.roll(jnp.broadcast_to(values, (8, span)), LANES, 1)[0:1]

    @pl.when((step == steps - 1) & (pair == n_pairs - 1))
    def _():
        total_ref[...] = total[...]
        for slot in range(2):
            for peer in range(n_ctx):

                @pl.when(peer != here)
                def _():
                    arrival(slot, peer).wait_recv()

            value = got_ref[slot, 0].astype(jnp.float32)
            for peer in range(1, n_ctx):
                value = value + got_ref[slot, peer].astype(jnp.float32)
            dkv_ref[slot] = value.astype(jnp.bfloat16)
        for peer in range(n_ctx):

            @pl.when(peer != here)
            def _():
                swap(1, peer).wait_send()

        line_sum.finish()


def attend_back(query, key_value, grad, mixed, logs, lines, part):
    rows, cols = query.shape
    length = key_value.shape[2]
    pairs = cols // LANES
    depth = 2 if length <= 4096 else 1
    n_ctx = lax.axis_size("ctx")
    tile = 256
    chunk = 512
    span = lines.shape[2]
    width = part.shape[1]
    return pl.pallas_call(
        functools.partial(attend_back_kernel, length, rows, tile, chunk, pairs, n_ctx, lax.axis_size("tp")),
        grid=(pairs, rows // tile),
        in_specs=[
            pl.BlockSpec((tile, LANES), lambda p, t: (t, p)),
            pl.BlockSpec((None, None, length, LANES), lambda p, t: (p, 0, 0, 0), pipeline_mode=pl.Buffered(depth)),
            pl.BlockSpec((None, None, length, LANES), lambda p, t: (p, 1, 0, 0), pipeline_mode=pl.Buffered(depth)),
            pl.BlockSpec((tile, LANES), lambda p, t: (t, p)),
            pl.BlockSpec((tile, LANES), lambda p, t: (t, p)),
            pl.BlockSpec((1, 2, tile), lambda p, t: (p, 0, t)),
            pl.BlockSpec((1, 2, span), lambda p, t: (p, 0, 0)),
            pl.BlockSpec(memory_space=pltpu.VMEM),
        ],
        out_specs=[
            pl.BlockSpec((tile, LANES), lambda p, t: (t, p)),
            pl.BlockSpec(memory_space=pltpu.VMEM),
            pl.BlockSpec((1, 2, span), lambda p, t: (p, 0, 0)),
            pl.BlockSpec(memory_space=pltpu.VMEM),
        ],
        out_shape=[
            jax.ShapeDtypeStruct((rows, cols), jnp.bfloat16),
            jax.ShapeDtypeStruct((pairs, rows, 2 * LANES), jnp.bfloat16),
            jax.ShapeDtypeStruct((pairs, 2, span), jnp.float32),
            jax.ShapeDtypeStruct((rows, width), jnp.bfloat16),
        ],
        scratch_shapes=[
            pltpu.VMEM((2, LANES, span), jnp.float32 if length <= 4096 else jnp.bfloat16),
            pltpu.VMEM((2, LANES, span), jnp.float32),
            pltpu.VMEM((length, LANES), jnp.float32),
            pltpu.VMEM((length, LANES), jnp.float32),
            pltpu.VMEM((n_ctx, rows, 2 * LANES), jnp.bfloat16),
            pltpu.VMEM((pairs, n_ctx, rows, 2 * LANES), jnp.bfloat16),
            pltpu.SemaphoreType.DMA((pairs, n_ctx)),
            pltpu.SemaphoreType.DMA((pairs, n_ctx)),
        ]
        + LineSum.scratch(rows, width, BACK_ROWS),
        compiler_params=pltpu.CompilerParams(
            collective_id=1, has_side_effects=True, vmem_limit_bytes=60 * MIB
        ),
        cost_estimate=pl.CostEstimate(flops=40 * rows * length * cols, bytes_accessed=24 * length * cols, transcendentals=rows * length * cols // DH),
    )(query, key_value, key_value, grad, mixed, logs, lines, part)


def tail_kernel(
    n_fsdp,
    n_ctx,
    n_tp,
    blocks,
    sum_rows,
    part_ref,
    small_ref,
    grad_ref,
    scale_ref,
    s_right,
    p_right,
    s_left,
    p_left,
    w_ref,
    new_right,
    new_left,
    new_w,
    total_ref,
    small_out,
    turned,
    direction,
    squares,
    plane_got,
    line_got,
    line_own,
    plane_send,
    plane_sem,
    tp_send,
    tp_sem,
    left,
    right,
    stage,
    total,
    sems,
):
    turn = pl.program_id(0)
    turns = pl.num_programs(0)
    rights, lefts = blocks
    line = LineSum("tp", n_tp, BACK_ROWS, part_ref.shape[0] // BACK_ROWS // 2, part_ref, left, right, stage, total, sems, 2)
    here = lax.axis_index("fsdp") * n_ctx + lax.axis_index("ctx")
    tp_here = lax.axis_index("tp")
    shards = n_fsdp * n_ctx
    plane = [(f * n_ctx + c, {"fsdp": f, "ctx": c}) for f in range(n_fsdp) for c in range(n_ctx)]
    column = [(t, {"tp": t}) for t in range(n_tp)]
    other = jnp.where(here == 0, 1, 0)
    other_where = {"fsdp": other // n_ctx, "ctx": other % n_ctx}
    other_tp = {"tp": jnp.where(tp_here == 0, 1, 0)}
    middle = rights + 2

    def plane_copy(number, where):
        return remote(small_ref.at[number], plane_got.at[here], plane_send.at[number], plane_sem.at[here], where)

    def tp_copy(number, where):
        return remote(line_own, line_got.at[tp_here], tp_send.at[number], tp_sem.at[tp_here], where)

    @pl.when(turn == 0)
    def _():
        barrier = pltpu.get_barrier_semaphore()
        greet(barrier, here, plane)
        greet(barrier, tp_here, column)
        squares[...] = jnp.zeros_like(squares)
        pl.semaphore_wait(barrier, shards - 1 + n_tp - 1)
        for number, where in plane:

            @pl.when(number != here)
            def _():
                plane_copy(number, where).start()

        plane_got[here] = small_ref[here]

    @pl.when(turn == middle)
    def _():
        for number, where in plane:

            @pl.when(number != here)
            def _():
                remote(plane_got.at[number], plane_got.at[number], plane_sem.at[number], plane_sem.at[number], other_where).wait_recv()

        added = plane_got[0]
        largest = plane_got[0]
        for number in range(1, shards):
            added = added + plane_got[number]
            largest = jnp.maximum(largest, plane_got[number])
        row = lax.broadcasted_iota(jnp.int32, added.shape, 0)
        line_own[...] = jnp.where(row == sum_rows + 1, largest, added)
        for number, where in column:

            @pl.when(number != tp_here)
            def _():
                tp_copy(number, where).start()

        line_got[tp_here] = line_own[...]

    def one(number, carry):
        line.step(number)
        return carry

    lax.fori_loop(turn * line.steps // turns, (turn + 1) * line.steps // turns, one, 0)

    @pl.when(turn < rights)
    def _():
        spot = pl.ds(pl.multiple_of(turn * LANES, LANES), LANES)
        grad = grad_ref[...]
        new_right[...] = decay * s_right[...] + (1.0 - decay) * dot_nt(grad_ref[spot, :], grad)
        turned[spot, :] = dot_nn(p_right[...].astype(jnp.bfloat16), grad).astype(jnp.bfloat16)

    @pl.when((turn >= rights) & (turn < rights + lefts))
    def _():
        spot = pl.ds(pl.multiple_of((turn - rights) * LANES, LANES), LANES)
        new_left[...] = decay * s_left[...] + (1.0 - decay) * dot_tn(grad_ref[:, spot], grad_ref[...])
        value = dot_nn(turned[...], p_left[...].astype(jnp.bfloat16))
        squares[...] = squares[...] + jnp.sum(value * value, 0, keepdims=True)
        direction[:, spot] = value.astype(jnp.bfloat16)

    @pl.when(turn >= rights + lefts)
    def _():
        spot = pl.ds(pl.multiple_of((turn - rights - lefts) * LANES, LANES), LANES)
        mean = jnp.sum(squares[0:1, :], 1, keepdims=True) / (grad_ref.shape[0] * grad_ref.shape[1])
        factor = scale_ref[0:1, 0:1] * lax.rsqrt(mean + step_epsilon)
        new_w[...] = w_ref[...] - factor * direction[spot, :].astype(jnp.float32)

    @pl.when(turn == turns - 1)
    def _():
        total_ref[...] = total[...]
        for number, where in column:

            @pl.when(number != tp_here)
            def _():
                remote(line_got.at[number], line_got.at[number], tp_sem.at[number], tp_sem.at[number], other_tp).wait_recv()

        added = line_got[0]
        for number in range(1, n_tp):
            added = added + line_got[number]
        row = lax.broadcasted_iota(jnp.int32, added.shape, 0)
        small_out[...] = jnp.where(row < sum_rows, added, line_own[...])
        for number, where in plane:

            @pl.when(number != here)
            def _():
                plane_copy(number, where).wait_send()

        for number, where in column:

            @pl.when(number != tp_here)
            def _():
                tp_copy(number, where).wait_send()

        line.finish()


def tail(part, small, sum_rows, grad, scale, left, right, weight):
    rows, width = part.shape
    deep, wide = grad.shape
    n_fsdp, n_ctx, n_tp = lax.axis_size("fsdp"), lax.axis_size("ctx"), lax.axis_size("tp")
    rights, lefts = deep // LANES, wide // LANES
    turns = 2 * rights + lefts
    small_rows = small.shape[1]
    vmem = pl.BlockSpec(memory_space=pltpu.VMEM)

    def at_right(turn):
        return jnp.minimum(turn, rights - 1)

    def at_left(turn):
        return jnp.clip(turn - rights, 0, lefts - 1)

    def at_weight(turn):
        return jnp.clip(turn - rights - lefts, 0, rights - 1)

    return pl.pallas_call(
        functools.partial(tail_kernel, n_fsdp, n_ctx, n_tp, (rights, lefts), sum_rows),
        grid=(turns,),
        in_specs=[
            vmem,
            vmem,
            vmem,
            vmem,
            pl.BlockSpec((None, LANES, deep), lambda t: (0, at_right(t), 0)),
            pl.BlockSpec((None, LANES, deep), lambda t: (1, at_right(t), 0)),
            pl.BlockSpec((None, LANES, wide), lambda t: (0, at_left(t), 0)),
            pl.BlockSpec((None, wide, LANES), lambda t: (1, 0, at_left(t))),
            pl.BlockSpec((LANES, wide), lambda t: (at_weight(t), 0)),
        ],
        out_specs=[
            pl.BlockSpec((LANES, deep), lambda t: (at_right(t), 0)),
            pl.BlockSpec((LANES, wide), lambda t: (at_left(t), 0)),
            pl.BlockSpec((LANES, wide), lambda t: (at_weight(t), 0)),
            vmem,
            vmem,
        ],
        out_shape=[
            jax.ShapeDtypeStruct((deep, deep), jnp.float32),
            jax.ShapeDtypeStruct((wide, wide), jnp.float32),
            jax.ShapeDtypeStruct((deep, wide), jnp.float32),
            jax.ShapeDtypeStruct((rows, width), jnp.bfloat16),
            jax.ShapeDtypeStruct((small_rows, LANES), jnp.float32),
        ],
        scratch_shapes=[
            pltpu.VMEM((deep, wide), jnp.bfloat16),
            pltpu.VMEM((deep, wide), jnp.bfloat16),
            pltpu.VMEM((1, LANES), jnp.float32),
            pltpu.VMEM((n_fsdp * n_ctx, small_rows, LANES), jnp.float32),
            pltpu.VMEM((n_tp, small_rows, LANES), jnp.float32),
            pltpu.VMEM((small_rows, LANES), jnp.float32),
            pltpu.SemaphoreType.DMA((n_fsdp * n_ctx,)),
            pltpu.SemaphoreType.DMA((n_fsdp * n_ctx,)),
            pltpu.SemaphoreType.DMA((n_tp,)),
            pltpu.SemaphoreType.DMA((n_tp,)),
        ]
        + LineSum.scratch(rows, width, BACK_ROWS),
        compiler_params=pltpu.CompilerParams(
            collective_id=2, has_side_effects=True, vmem_limit_bytes=56 * MIB
        ),
        cost_estimate=pl.CostEstimate(
            flops=8 * deep * wide * (deep + wide), bytes_accessed=240 * rows * width, transcendentals=0
        ),
    )(part, small, grad, scale, right, right, left, left, weight)


GELU_A = 0.7978845608028654
GELU_B = 0.044715


def expert_kernel(x_ref, grad_ref, other_ref, here_ref, w_ref, out_ref, router_ref, sent_ref, hidden_ref, mixed_ref, choice_ref):
    half = w_ref.shape[0] // 2
    rows = x_ref[...]
    first = dot_nt(rows, w_ref[:half, :])
    second = dot_nt(rows, w_ref[half:, :])
    logits = dot_nn(rows, router_ref[...])
    lane = lax.broadcasted_iota(jnp.int32, logits.shape, 1)
    contrast = (lane == here_ref[0:1, 0:1]).astype(jnp.float32) - (lane == other_ref[...]).astype(jnp.float32)
    gate = jax.nn.sigmoid(jnp.sum(logits * contrast, 1, keepdims=True))
    square = first * first
    bent = jnp.tanh(GELU_A * first * (1.0 + GELU_B * square))
    rise = 0.5 * (1.0 + bent)
    gelu = first * rise
    slope = rise + 0.5 * GELU_A * first * (1.0 - bent * bent) * (1.0 + 3.0 * GELU_B * square)
    hidden = gelu * second
    plain = dot_nt(grad_ref[...], out_ref[...])
    grad_gate = jnp.sum(plain * hidden, 1, keepdims=True)
    choice = (gate * (1.0 - gate) * grad_gate * contrast).astype(jnp.bfloat16)
    scaled = gate * plain
    grad_first = (scaled * second * slope).astype(jnp.bfloat16)
    grad_second = (scaled * gelu).astype(jnp.bfloat16)
    hidden_ref[...] = (gate * hidden).astype(jnp.bfloat16)
    mixed_ref[0] = grad_first
    mixed_ref[1] = grad_second
    choice_ref[...] = choice
    sent = dot_nn(grad_first, w_ref[:half, :]) + dot_nn(grad_second, w_ref[half:, :])
    sent_ref[...] = (sent + dot_nt(choice, router_ref[...])).astype(jnp.bfloat16)


def expert_chain(rows, grads, other, here, weight, weight_out, router):
    count, width = rows.shape
    half = weight.shape[0] // 2
    tile = 320
    vmem = pl.BlockSpec(memory_space=pltpu.VMEM)
    return pl.pallas_call(
        expert_kernel,
        grid=(count // tile,),
        in_specs=[
            pl.BlockSpec((tile, width), lambda t: (t, 0)),
            pl.BlockSpec((tile, width), lambda t: (t, 0)),
            pl.BlockSpec((tile, 1), lambda t: (t, 0)),
            vmem,
            vmem,
            vmem,
            vmem,
        ],
        out_specs=[
            pl.BlockSpec((tile, width), lambda t: (t, 0)),
            pl.BlockSpec((tile, half), lambda t: (t, 0)),
            pl.BlockSpec((2, tile, half), lambda t: (0, t, 0)),
            pl.BlockSpec((tile, LANES), lambda t: (t, 0)),
        ],
        out_shape=[
            jax.ShapeDtypeStruct((count, width), jnp.bfloat16),
            jax.ShapeDtypeStruct((count, half), jnp.bfloat16),
            jax.ShapeDtypeStruct((2, count, half), jnp.bfloat16),
            jax.ShapeDtypeStruct((count, LANES), jnp.bfloat16),
        ],
        compiler_params=pltpu.CompilerParams(vmem_limit_bytes=48 * MIB),
        cost_estimate=pl.CostEstimate(
            flops=8 * count * width * half, bytes_accessed=16 * count * width, transcendentals=count * half
        ),
    )(rows, grads, other, here, weight, weight_out, router)


def normalize(values, gain):
    return values * lax.rsqrt(jnp.mean(values * values, -1, keepdims=True) + norm_epsilon) * gain


def gated_gelu(both):
    return jax.nn.gelu(both[..., 0, :], approximate=True) * both[..., 1, :]


def precondition(grad, master, left, right):
    low = grad.astype(jnp.bfloat16)
    new_left = decay * left[0] + (1.0 - decay) * dot_nt(low, low)
    new_right = decay * right[0] + (1.0 - decay) * dot_tn(low, low)
    turned = dot_nn(left[1].astype(jnp.bfloat16), low).astype(jnp.bfloat16)
    direction = dot_nn(turned, right[1].astype(jnp.bfloat16))
    size = jnp.sqrt(jnp.mean(master * master) + step_epsilon)
    step = (
        matrix_rate * size * direction * lax.rsqrt(jnp.mean(direction * direction) + step_epsilon)
    )
    return (new_left, new_right, master - step)


def adapt(grad, moment, master, rate):
    new_moment = decay * moment + (1.0 - decay) * grad * grad
    return (new_moment, master - rate * grad * lax.rsqrt(new_moment + moment_epsilon))


def barrier(*values):
    return lax.optimization_barrier(values)


def crossing(values):
    return lax.all_to_all(values, ("fsdp", "ctx"), split_axis=0, concat_axis=0, tiled=True)


def on_device(
    tokens,
    cotangent,
    routes,
    buckets,
    attention_in,
    attention_out,
    router,
    gains,
    bias_table,
    expert_in,
    expert_out,
    attention_in_left,
    attention_in_right,
    attention_out_left,
    attention_out_right,
    expert_in_left,
    expert_in_right,
    expert_out_left,
    expert_out_right,
    router_moment,
    gains_moment,
    table_moment,
):
    low = jnp.bfloat16
    rows = tokens.shape[0]
    width = tokens.shape[1]
    shards = lax.axis_size("fsdp") * lax.axis_size("ctx")
    n_ctx = lax.axis_size("ctx")
    n_tp = lax.axis_size("tp")
    here = lax.axis_index("fsdp") * n_ctx + lax.axis_index("ctx")
    tp_here = lax.axis_index("tp")
    length = rows * n_ctx
    depth = attention_in.shape[1]
    head_cols = attention_in.shape[2]
    local_heads = head_cols // DH
    head_pairs = head_cols // LANES
    table_size = bias_table.shape[0]
    experts = router.shape[1]
    capacity = rows * TOPK * 5 // (4 * experts)
    slots_all = experts * capacity
    span = length + rows

    sizes = (depth * experts, 2 * depth, table_size * local_heads)
    small = jnp.concatenate(
        [router.astype(low).reshape(-1), gains.astype(low).reshape(-1), bias_table.astype(low).reshape(-1)]
    )
    small = jnp.pad(small, (0, -small.shape[0] % (16 * head_cols))).reshape(-1, head_cols)
    gathered = lax.all_gather(
        jnp.concatenate(
            [
                attention_in.astype(low).reshape(3 * depth, head_cols),
                small,
            ],
            0,
        ),
        ("fsdp", "ctx"),
        axis=0,
        tiled=False,
    )
    entry_full = (
        gathered[:, : 3 * depth]
        .reshape(shards, 3, depth, head_cols)
        .transpose(1, 0, 2, 3)
        .reshape(3, width, head_cols)
    )
    small = gathered[:, 3 * depth :].reshape(shards, -1)
    router_full = small[:, : sizes[0]].reshape(width, experts)
    gains_full = (
        small[:, sizes[0] : sizes[0] + sizes[1]]
        .reshape(shards, 2, depth)
        .transpose(1, 0, 2)
        .reshape(2, width)
    )
    table_full = small[:, sizes[0] + sizes[1] : sum(sizes)].reshape(shards * table_size, local_heads)
    gain_first = gains_full[0].astype(jnp.float32)
    gain_second = gains_full[1].astype(jnp.float32)
    expand_out = expert_out[0].astype(low)

    chosen = routes.reshape(-1)
    route_hits = (chosen[:, None] == jnp.arange(experts, dtype=jnp.int32)[None, :]).astype(
        jnp.int32
    )
    slots = jnp.sum(route_hits * (jnp.cumsum(route_hits, 0) - 1), 1)
    slot_rows = (chosen * capacity + slots).reshape(rows, TOPK)
    place = jnp.arange(slots_all, dtype=jnp.int32)
    first_hit = place[:, None] == slot_rows[None, :, 0]
    second_hit = place[:, None] == slot_rows[None, :, 1]
    picks = (first_hit | second_hit).astype(low)
    other = jnp.sum(
        jnp.where(first_hit, routes[None, :, 1], 0) + jnp.where(second_hit, routes[None, :, 0], 0),
        1,
    )
    grad_buffer = dot_nn(picks, cotangent).astype(low).reshape(experts, capacity, width)
    other_arrived = crossing(other.reshape(experts, capacity)).reshape(-1)

    inputs = tokens.astype(jnp.float32)
    first = normalize(inputs, gain_first).astype(low)
    projected = jnp.einsum(
        "sd,kde->kse", first, entry_full, preferred_element_type=jnp.float32
    )
    query = (projected[0].astype(low) * (DH**-0.5)).astype(low)
    own_pairs = (
        projected[1:].astype(low).reshape(2, rows, head_pairs, LANES).transpose(2, 0, 1, 3)
    )
    low_end = length - rows - lax.axis_index("ctx") * rows
    near = lax.dynamic_slice_in_dim(jnp.pad(buckets, (0, 1)), low_end, span, 0)
    hits = (near[:, None] == jnp.arange(table_full.shape[0], dtype=jnp.int32)[None, :]).astype(low)
    lines = lax.dot_general(
        table_full, hits, (((0,), (1,)), ((), ())), preferred_element_type=jnp.float32
    ).reshape(head_pairs, 2, span)
    hits_back = (near[::-1][:, None] == jnp.arange(table_full.shape[0], dtype=jnp.int32)[None, :]).astype(low)
    back_lines = lax.dot_general(
        table_full, hits_back, (((0,), (1,)), ((), ())), preferred_element_type=jnp.float32
    ).reshape(head_pairs, 2, span)
    exit_piece = attention_out.astype(low)
    exit_rows = lax.dynamic_update_slice_in_dim(
        jnp.zeros((n_tp * head_cols, depth), low), exit_piece, tp_here * head_cols, 0
    )
    for shift in range(1, n_tp):
        piece = lax.ppermute(exit_piece, "tp", [(i, (i + shift) % n_tp) for i in range(n_tp)])
        exit_rows = lax.dynamic_update_slice_in_dim(
            exit_rows, piece, (tp_here + n_tp - shift) % n_tp * head_cols, 0
        )
    exit_all = lax.all_gather(exit_rows, ("fsdp", "ctx"), axis=1, tiled=True)
    exit_own = lax.dynamic_slice_in_dim(exit_all, tp_here * head_cols, head_cols, 0)
    mixed, logs, peak_own, key_value, mixed_all, grad_arrived = attend(
        query, own_pairs, lines, grad_buffer
    )
    grad_arrived = grad_arrived.reshape(slots_all, width)
    value = dot_nn(mixed_all, exit_all)
    middle = inputs + value
    second = normalize(middle, gain_second).astype(low)

    buffer = dot_nn(picks, second).astype(low).reshape(experts, capacity, width)
    arrived = crossing(buffer).reshape(slots_all, width)
    columns = 2 * expert_in.shape[3]
    flat_master = expert_in[0].transpose(1, 2, 0).reshape(columns, width)
    flat_low = flat_master.astype(low)
    wide_router = jnp.pad(router_full, ((0, 0), (0, LANES - experts)))
    arrived, low_out, flat_low, wide_router = barrier(arrived, expand_out, flat_low, wide_router)
    sent_grads, gated_hidden, grad_mixed_up, grad_choice = expert_chain(
        arrived,
        grad_arrived,
        other_arrived[:, None],
        jnp.full((8, LANES), here, jnp.int32),
        flat_low,
        low_out,
        wide_router,
    )
    back_grads = crossing(sent_grads.reshape(experts, capacity, width)).reshape(slots_all, width)

    sent_rows = dot_nn(gated_hidden, expand_out).astype(low)
    grad_router = dot_tn(arrived, grad_choice)[:, :experts]
    grad_expand_out = dot_tn(gated_hidden, grad_arrived)
    shrink_left, shrink_right, shrink_new = precondition(
        grad_expand_out, expert_out[0], expert_out_left, expert_out_right
    )
    grad_expand_in = jnp.einsum(
        "gsf,sd->gfd", grad_mixed_up, arrived, preferred_element_type=jnp.float32
    )
    back_grads, sent_rows, grad_router, grad_expand_out, grad_expand_in, shrink_left, shrink_right, shrink_new = barrier(
        back_grads, sent_rows, grad_router, grad_expand_out, grad_expand_in, shrink_left, shrink_right, shrink_new
    )
    grad_second = combine_sum(slot_rows, back_grads, rows)

    back_rows = crossing(sent_rows.reshape(experts, capacity, width)).reshape(slots_all, width)
    grad_second, back_rows = barrier(grad_second, back_rows)
    result_part = dot_tn(picks, back_rows).astype(low)

    unused, pull = jax.vjp(normalize, middle, gain_second)
    grad_middle_norm, grad_gain_second = pull(grad_second.astype(jnp.float32))
    grad_middle = cotangent.astype(jnp.float32) + grad_middle_norm
    grad_attention = grad_middle.astype(low)
    grad_mixed = dot_nt(grad_attention, exit_own).astype(low)
    grad_query, key_value_grad, sums, result_sum = attend_back(
        query, key_value, grad_mixed, mixed, logs, back_lines, result_part
    )
    result = (middle + result_sum.astype(jnp.float32)).astype(low)
    grad_projected = jnp.stack(
        [
            grad_query,
            jnp.concatenate([key_value_grad[pair, :, :LANES] for pair in range(head_pairs)], 1),
            jnp.concatenate([key_value_grad[pair, :, LANES:] for pair in range(head_pairs)], 1),
        ]
    )
    grad_exit = dot_tn(mixed, grad_attention).astype(low)
    grad_first_part = jnp.einsum(
        "kse,kde->sd", grad_projected, entry_full, preferred_element_type=jnp.float32
    )
    unused, pull = jax.vjp(normalize, inputs, gain_first)
    grad_gain_first = pull(grad_first_part)[1]
    grad_entry = jnp.einsum(
        "sd,kse->dke", first, grad_projected, preferred_element_type=jnp.float32
    ).astype(low)
    table_grad = lax.dot_general(
        hits_back.astype(jnp.float32),
        sums.reshape(local_heads, span),
        (((0,), (1,)), ((), ())),
        precision=highest,
        preferred_element_type=jnp.float32,
    )
    gain_sums = jnp.stack([grad_gain_first, jnp.where(tp_here == 0, grad_gain_second, 0.0)])
    peak_own = peak_own[:, :, 0].reshape(local_heads)
    pieces = [
        grad_router.reshape(shards, -1),
        gain_sums.reshape(2, shards, depth).transpose(1, 0, 2).reshape(shards, -1),
        table_grad.reshape(shards, -1),
        jnp.broadcast_to(peak_own[None], (shards, local_heads)),
    ]
    spots = [0]
    padded = []
    for piece in pieces:
        padded.append(jnp.pad(piece, ((0, 0), (0, -piece.shape[1] % LANES))))
        spots.append(spots[-1] + padded[-1].shape[1] // LANES)
    small = jnp.concatenate(padded, 1)
    small = jnp.pad(small, ((0, 0), (0, -small.shape[1] % (8 * LANES)))).reshape(shards, -1, LANES)
    size = jnp.sqrt(jnp.mean(flat_master * flat_master) + step_epsilon)
    weight_terms = jnp.concatenate(
        [
            grad_entry.reshape(shards, 3 * depth, head_cols),
            grad_exit.reshape(head_cols, shards, depth)
            .transpose(1, 0, 2)
            .reshape(shards, depth, head_cols),
        ],
        1,
    )
    first_part, small, weight_terms = barrier(grad_first_part.astype(low), small, weight_terms)
    weight_terms = crossing(weight_terms)
    expand_right, expand_left, expand_new, grad_first, small_sum = tail(
        first_part,
        small,
        spots[2],
        grad_expand_in.reshape(columns, width).astype(low),
        jnp.full((8, LANES), matrix_rate * size, jnp.float32),
        expert_in_left,
        expert_in_right,
        flat_master,
    )
    grad_first, weight_terms = barrier(grad_first, weight_terms)
    owned = jnp.sum(weight_terms.astype(jnp.float32), 0)
    owned_in = owned[: 3 * depth].reshape(depth, 3, head_cols).transpose(1, 0, 2)
    owned_out = owned[3 * depth :].reshape(head_cols, depth)
    grad_tokens = grad_middle + pull(grad_first.astype(jnp.float32))[0]

    def small_piece(number, shape):
        count = 1
        for extent in shape:
            count *= extent
        return small_sum[spots[number] : spots[number + 1]].reshape(-1)[:count].reshape(shape)

    owned_router = small_piece(0, (depth, experts))
    owned_gains = small_piece(1, (2, depth))
    owned_table = small_piece(2, (table_size, local_heads))
    peaks = small_piece(3, (local_heads,))
    in_left, in_right, in_new = jax.vmap(precondition)(
        owned_in,
        attention_in,
        jnp.swapaxes(attention_in_left, 0, 1),
        jnp.swapaxes(attention_in_right, 0, 1),
    )
    column = jnp.sqrt(jnp.repeat(clip_level / jnp.maximum(peaks, clip_level), DH))
    in_new = in_new * jnp.stack([column, column, jnp.ones_like(column)])[:, None, :]
    out_left, out_right, out_new = precondition(
        owned_out, attention_out, attention_out_left, attention_out_right
    )
    router_moment_new, router_new = adapt(owned_router, router_moment, router, router_rate)
    gains_moment_new, gains_new = adapt(owned_gains, gains_moment, gains, gain_rate)
    table_moment_new, table_new = adapt(owned_table, table_moment, bias_table, table_rate)
    return (
        result,
        grad_tokens,
        owned_in,
        in_new,
        in_left,
        in_right,
        owned_out,
        out_new,
        out_left,
        out_right,
        grad_expand_in.transpose(2, 0, 1)[None],
        expand_new.reshape(2, -1, width).transpose(2, 0, 1)[None],
        expand_left,
        expand_right,
        grad_expand_out[None],
        shrink_new[None],
        shrink_left,
        shrink_right,
        owned_router,
        router_moment_new,
        router_new,
        owned_gains,
        gains_moment_new,
        gains_new,
        owned_table,
        table_moment_new,
        table_new,
    )


def solution(mesh):
    placed = (
        P(("fsdp", "ctx"), None),
        P(("fsdp", "ctx"), None),
        P(("fsdp", "ctx"), None),
        P(),
        P(None, ("fsdp", "ctx"), "tp"),
        P("tp", ("fsdp", "ctx")),
        P(("fsdp", "ctx"), None),
        P(None, ("fsdp", "ctx")),
        P(("fsdp", "ctx"), "tp"),
        P(("fsdp", "ctx"), None, None, "tp"),
        P(("fsdp", "ctx"), "tp", None),
        P(None, None, ("fsdp", "ctx", "tp"), None),
        P(None, None, ("fsdp", "ctx", "tp"), None),
        P(None, ("fsdp", "ctx", "tp"), None),
        P(None, ("fsdp", "ctx", "tp"), None),
        P(None, ("fsdp", "ctx", "tp"), None),
        P(None, ("fsdp", "ctx", "tp"), None),
        P(None, ("fsdp", "ctx", "tp"), None),
        P(None, ("fsdp", "ctx", "tp"), None),
        P(("fsdp", "ctx"), None),
        P(None, ("fsdp", "ctx")),
        P(("fsdp", "ctx"), "tp"),
    )
    return jax.shard_map(
        on_device,
        mesh=mesh,
        in_specs=placed,
        out_specs=(
            P(("fsdp", "ctx"), None),
            P(("fsdp", "ctx"), None),
            P(None, ("fsdp", "ctx"), "tp"),
            P(None, ("fsdp", "ctx"), "tp"),
            P(None, ("fsdp", "ctx", "tp"), None),
            P(None, ("fsdp", "ctx", "tp"), None),
            P("tp", ("fsdp", "ctx")),
            P("tp", ("fsdp", "ctx")),
            P(("fsdp", "ctx", "tp"), None),
            P(("fsdp", "ctx", "tp"), None),
            P(("fsdp", "ctx"), None, None, "tp"),
            P(("fsdp", "ctx"), None, None, "tp"),
            P(("fsdp", "ctx", "tp"), None),
            P(("fsdp", "ctx", "tp"), None),
            P(("fsdp", "ctx"), "tp", None),
            P(("fsdp", "ctx"), "tp", None),
            P(("fsdp", "ctx", "tp"), None),
            P(("fsdp", "ctx", "tp"), None),
            P(("fsdp", "ctx"), None),
            P(("fsdp", "ctx"), None),
            P(("fsdp", "ctx"), None),
            P(None, ("fsdp", "ctx")),
            P(None, ("fsdp", "ctx")),
            P(None, ("fsdp", "ctx")),
            P(("fsdp", "ctx"), "tp"),
            P(("fsdp", "ctx"), "tp"),
            P(("fsdp", "ctx"), "tp"),
        ),
        check_vma=False,
    )
```

```python
import functools

import jax
import jax.numpy as jnp
from jax import lax
from jax.experimental import pallas as pl
from jax.experimental.pallas import tpu as pltpu

from jax.sharding import PartitionSpec as P

DH = 64
LANES = 128
MIB = 1024 * 1024


TOPK = 2

highest = lax.Precision.HIGHEST
norm_epsilon = 1e-06
step_epsilon = 1e-06
moment_epsilon = 1e-08
clip_level = 4.0
decay = 0.5
matrix_rate = 0.3
gain_rate = 0.25
router_rate = 0.01
table_rate = 0.3


def dot_nt(left, right):
    return lax.dot_general(left, right, (((1,), (1,)), ((), ())), preferred_element_type=jnp.float32)


def dot_nn(left, right):
    return lax.dot_general(left, right, (((1,), (0,)), ((), ())), preferred_element_type=jnp.float32)


def dot_tn(left, right):
    return lax.dot_general(left, right, (((0,), (0,)), ((), ())), preferred_element_type=jnp.float32)


def half_mask(shape, half):
    lane = lax.broadcasted_iota(jnp.int32, shape, 1)
    return (lane // DH) == half


def attend_kernel(length, rows, tile, pairs, n_fsdp, n_ctx, n_tp, q_ref, own_ref, line_ref, cross_ref, mixed_ref, log_ref, peak_ref, kv_out, all_out, cross_out, strip, wide, kv_ref, all_ref, kv_send, kv_got, mix_send, mix_got, out_sem, cross_send, cross_got):
    pair = pl.program_id(0)
    step = pl.program_id(1)
    steps = rows // tile
    span = line_ref.shape[2]
    here = lax.axis_index("ctx")
    tp_here = lax.axis_index("tp")
    own_rows = pl.ds(pl.multiple_of(here * rows, rows), rows)
    ctx_peers = [(number, {"ctx": number}) for number in range(n_ctx)]
    tp_peers = [(number, {"tp": number}) for number in range(n_tp)]
    shard = lax.axis_index("fsdp") * n_ctx + here
    plane = [(f * n_ctx + c, {"fsdp": f, "ctx": c}) for f in range(n_fsdp) for c in range(n_ctx)]
    other = jnp.where(shard == 0, 1, 0)
    other_plane = {"fsdp": other // n_ctx, "ctx": other % n_ctx}
    other_ctx = {"ctx": jnp.where(here == 0, 1, 0)}
    other_tp = {"tp": jnp.where(tp_here == 0, 1, 0)}

    def kv_copy(slot, number, where):
        return remote(
            own_ref.at[slot], kv_ref.at[slot, :, own_rows, :], kv_send.at[slot, number], kv_got.at[slot, here], where
        )

    def kv_arrived(slot, number):
        spot = kv_ref.at[slot, :, pl.ds(number * rows, rows), :]
        remote(spot, spot, kv_got.at[slot, number], kv_got.at[slot, number], other_ctx).wait_recv()

    def cross_copy(number, where):
        return remote(
            cross_ref.at[number], cross_out.at[shard], cross_send.at[number], cross_got.at[shard], where
        )

    def cross_own():
        return pltpu.make_async_copy(cross_ref.at[shard], cross_out.at[shard], out_sem.at[2])

    def mix_spot(slot, turn, number):
        return (
            pl.ds(pl.multiple_of(turn * tile, tile), tile),
            pl.ds(pl.multiple_of((number * pairs + slot) * LANES, LANES), LANES),
        )

    def mix_copy(slot, turn, number, where):
        spot = all_ref.at[mix_spot(slot, turn, tp_here)]
        return remote(spot, spot, mix_send.at[slot, turn, number], mix_got.at[slot, turn, tp_here], where)

    @pl.when((pair == 0) & (step == 0))
    def _():
        barrier = pltpu.get_barrier_semaphore()
        greet(barrier, shard, plane)
        greet(barrier, tp_here, tp_peers)
        pl.semaphore_wait(barrier, n_fsdp * n_ctx - 1 + n_tp - 1)
        for slot in range(pairs):
            for number, where in ctx_peers:

                @pl.when(number != here)
                def _():
                    kv_copy(slot, number, where).start()

            kv_ref[slot, :, own_rows, :] = own_ref[slot]

    @pl.when(step == 0)
    def _():
        for half in range(2):
            line = jnp.broadcast_to(line_ref[0, half : half + 1, :], (LANES, span))
            strip[half] = pltpu.roll(line, span - (LANES - 1), 1, stride=1, stride_axis=0)
        wide[:, LANES:] = jnp.ones((length, LANES), jnp.bfloat16)
        peak_ref[...] = jnp.full(peak_ref.shape, -jnp.inf, jnp.float32)
        for number, where in ctx_peers:

            @pl.when(number != here)
            def _():
                kv_arrived(pair, number)

        wide[:, :LANES] = kv_ref[pair, 1]

    @pl.when((pair == 0) & (step == 2))
    def _():
        cross_own().start()
        for number, where in plane:

            @pl.when(number != shard)
            def _():
                cross_copy(number, where).start()

    query = q_ref[...]
    groups = tile // LANES
    last = rows // LANES - 1
    mixed = jnp.zeros((tile, LANES), jnp.float32)
    for half in range(2):
        mine = half_mask((tile, LANES), half)
        own = jnp.where(mine, query, jnp.zeros_like(query))
        logit = dot_nt(own, kv_ref[pair, 0])
        top = jnp.max(logit, 1, keepdims=True)
        bias = []
        for group in range(groups):
            start = pl.multiple_of((last - (step * groups + group)) * LANES, LANES)
            bias.append(strip[half, :, pl.ds(start, length)])
        bias = jnp.concatenate(bias, 0) if groups > 1 else bias[0]
        powers = jnp.exp(logit + bias - top)
        both = dot_nn(powers.astype(jnp.bfloat16), wide[...])
        total = both[:, LANES:]
        mixed = jnp.where(mine, both[:, :LANES] / total, mixed)
        log_total = top + jnp.log(total)
        log_ref[0, half : half + 1, :] = log_total.T[0:1, :]
        best = jnp.max(jnp.broadcast_to(top, (tile, LANES)), 0, keepdims=True)
        peak_ref[0, half : half + 1, :] = jnp.maximum(peak_ref[0, half : half + 1, :], best)
    low = mixed.astype(jnp.bfloat16)
    mixed_ref[...] = low
    all_ref[mix_spot(pair, step, tp_here)] = low
    for number, where in reversed(tp_peers):

        @pl.when(number != tp_here)
        def _():
            mix_copy(pair, step, number, where).start()

    @pl.when((pair == pairs - 1) & (step == steps - 1))
    def _():
        for slot in range(pairs):
            for number, where in ctx_peers:

                @pl.when(number != here)
                def _():
                    kv_copy(slot, number, where).wait_send()

        def one(index, carry):
            slot, turn = index // steps, index % steps
            for number, where in tp_peers:

                @pl.when(number != tp_here)
                def _():
                    spot = all_ref.at[mix_spot(slot, turn, number)]
                    got = mix_got.at[slot, turn, number]
                    remote(spot, spot, got, got, other_tp).wait_recv()
                    mix_copy(slot, turn, number, where).wait_send()

            return carry

        kept = pltpu.make_async_copy(kv_ref, kv_out, out_sem.at[0])
        kept.start()
        lax.fori_loop(0, pairs * steps, one, 0)
        gathered = pltpu.make_async_copy(all_ref, all_out, out_sem.at[1])
        gathered.start()
        kept.wait()
        gathered.wait()
        cross_own().wait()
        for number, where in plane:

            @pl.when(number != shard)
            def _():
                spot = cross_out.at[number]
                remote(spot, spot, cross_got.at[number], cross_got.at[number], other_plane).wait_recv()
                cross_copy(number, where).wait_send()


def attend(query, own, lines, cross):
    rows, cols = query.shape
    n_fsdp, n_ctx, n_tp = lax.axis_size("fsdp"), lax.axis_size("ctx"), lax.axis_size("tp")
    length = rows * n_ctx
    pairs = cols // LANES
    tile = 256 if length <= 4096 else 128
    span = lines.shape[2]
    vmem = pl.BlockSpec(memory_space=pltpu.VMEM)
    return pl.pallas_call(
        functools.partial(attend_kernel, length, rows, tile, pairs, n_fsdp, n_ctx, n_tp),
        grid=(pairs, rows // tile),
        in_specs=[
            pl.BlockSpec((tile, LANES), lambda p, t: (t, p)),
            vmem,
            pl.BlockSpec((1, 2, span), lambda p, t: (p, 0, 0)),
            pl.BlockSpec(memory_space=pl.ANY),
        ],
        out_specs=[
            pl.BlockSpec((tile, LANES), lambda p, t: (t, p)),
            pl.BlockSpec((1, 2, tile), lambda p, t: (p, 0, t)),
            pl.BlockSpec((1, 2, LANES), lambda p, t: (p, 0, 0)),
            pl.BlockSpec(memory_space=pl.ANY),
            pl.BlockSpec(memory_space=pl.ANY),
            pl.BlockSpec(memory_space=pl.ANY),
        ],
        out_shape=[
            jax.ShapeDtypeStruct((rows, cols), jnp.bfloat16),
            jax.ShapeDtypeStruct((pairs, 2, rows), jnp.float32),
            jax.ShapeDtypeStruct((pairs, 2, LANES), jnp.float32),
            jax.ShapeDtypeStruct((pairs, 2, length, LANES), jnp.bfloat16),
            jax.ShapeDtypeStruct((rows, n_tp * cols), jnp.bfloat16),
            jax.ShapeDtypeStruct(cross.shape, cross.dtype),
        ],
        scratch_shapes=[
            pltpu.VMEM((2, LANES, span), jnp.float32),
            pltpu.VMEM((length, 2 * LANES), jnp.bfloat16),
            pltpu.VMEM((pairs, 2, length, LANES), jnp.bfloat16),
            pltpu.VMEM((rows, n_tp * cols), jnp.bfloat16),
            pltpu.SemaphoreType.DMA((pairs, n_ctx)),
            pltpu.SemaphoreType.DMA((pairs, n_ctx)),
            pltpu.SemaphoreType.DMA((pairs, rows // tile, n_tp)),
            pltpu.SemaphoreType.DMA((pairs, rows // tile, n_tp)),
            pltpu.SemaphoreType.DMA((3,)),
            pltpu.SemaphoreType.DMA((n_fsdp * n_ctx,)),
            pltpu.SemaphoreType.DMA((n_fsdp * n_ctx,)),
        ],
        compiler_params=pltpu.CompilerParams(
            collective_id=3, has_side_effects=True, vmem_limit_bytes=60 * MIB
        ),
        cost_estimate=pl.CostEstimate(flops=100 * rows * length * cols, bytes_accessed=8 * length * cols, transcendentals=rows * length * cols // DH),
    )(query, own, lines, cross)


def remote(source, target, send, receive, where):
    return pltpu.make_async_remote_copy(
        src_ref=source,
        dst_ref=target,
        send_sem=send,
        recv_sem=receive,
        device_id=where,
        device_id_type=pl.DeviceIdType.MESH,
    )


def greet(barrier, me, peers):
    for number, where in peers:

        @pl.when(number != me)
        def _():
            pl.semaphore_signal(
                barrier, inc=1, device_id=where, device_id_type=pl.DeviceIdType.MESH
            )


class LineSum:
    def __init__(self, axis, count, size, pairs, own, left, right, stage, total, sems, lag):
        self.lag = lag
        self.axis, self.count, self.size, self.pairs = axis, count, size, pairs
        self.own, self.left, self.right, self.stage, self.total = own, left, right, stage, total
        self.part_send, self.left_got, self.right_got, self.total_got, self.down_send, self.up_send = (
            sems.at[0], sems.at[1], sems.at[2], sems.at[3], sems.at[4], sems.at[5],
        )
        self.owners = ((count - 1) // 2, count // 2)
        self.reach = [max(owner, count - 1 - owner) for owner in self.owners]
        self.steps = pairs + self.lag * 2 * max(self.reach)

    @staticmethod
    def scratch(rows, width, size):
        return [pltpu.VMEM((rows, width), jnp.bfloat16)] * 4 + [
            pltpu.SemaphoreType.DMA((6, rows // size))
        ]

    def signal_neighbours(self, barrier):
        me = lax.axis_index(self.axis)
        for offset, there in ((-1, me > 0), (1, me < self.count - 1)):

            @pl.when(there)
            def _():
                pl.semaphore_signal(
                    barrier,
                    inc=1,
                    device_id={self.axis: me + offset},
                    device_id_type=pl.DeviceIdType.MESH,
                )

    def neighbours(self):
        me = lax.axis_index(self.axis)
        return jnp.where(me > 0, 1, 0) + jnp.where(me < self.count - 1, 1, 0)

    def place(self, side, pair):
        chunk = side * self.pairs + pair
        return chunk, pl.ds(pl.multiple_of(chunk * self.size, self.size), self.size)

    def part_up(self, chunk, rows):
        me = lax.axis_index(self.axis)
        return remote(
            self.stage.at[rows], self.left.at[rows], self.part_send.at[chunk], self.left_got.at[chunk], {self.axis: me + 1}
        )

    def part_down(self, chunk, rows):
        me = lax.axis_index(self.axis)
        return remote(
            self.stage.at[rows], self.right.at[rows], self.part_send.at[chunk], self.right_got.at[chunk], {self.axis: me - 1}
        )

    def total_up(self, chunk, rows):
        me = lax.axis_index(self.axis)
        return remote(
            self.total.at[rows], self.total.at[rows], self.up_send.at[chunk], self.total_got.at[chunk], {self.axis: me + 1}
        )

    def total_down(self, chunk, rows):
        me = lax.axis_index(self.axis)
        return remote(
            self.total.at[rows], self.total.at[rows], self.down_send.at[chunk], self.total_got.at[chunk], {self.axis: me - 1}
        )

    def arrived(self, target, rows, got):
        me = lax.axis_index(self.axis)
        peer = jnp.where(me < self.count - 1, me + 1, me - 1)
        remote(target.at[rows], target.at[rows], got, got, {self.axis: peer}).wait_recv()

    def step(self, number):
        me = lax.axis_index(self.axis)
        last = self.count - 1
        wide = jnp.float32
        for side, owner in enumerate(self.owners):
            reach = self.reach[side]
            from_end = jnp.where(me < owner, me, jnp.where(me > owner, last - me, reach))
            pair = number - self.lag * from_end
            chunk, rows = self.place(side, pair)
            inside = (pair >= 0) & (pair < self.pairs)

            @pl.when(inside & (me == 0) & (me < owner))
            def _():
                self.stage[rows, :] = self.own[rows, :]
                self.part_up(chunk, rows).start()

            @pl.when(inside & (me > 0) & (me < owner))
            def _():
                self.arrived(self.left, rows, self.left_got.at[chunk])
                self.stage[rows, :] = (self.own[rows, :].astype(wide) + self.left[rows, :].astype(wide)).astype(jnp.bfloat16)
                self.part_up(chunk, rows).start()

            @pl.when(inside & (me == last) & (me > owner))
            def _():
                self.stage[rows, :] = self.own[rows, :]
                self.part_down(chunk, rows).start()

            @pl.when(inside & (me < last) & (me > owner))
            def _():
                self.arrived(self.right, rows, self.right_got.at[chunk])
                self.stage[rows, :] = (self.own[rows, :].astype(wide) + self.right[rows, :].astype(wide)).astype(jnp.bfloat16)
                self.part_down(chunk, rows).start()

            @pl.when(inside & (me == owner))
            def _():
                value = self.own[rows, :].astype(wide)
                if owner > 0:
                    self.arrived(self.left, rows, self.left_got.at[chunk])
                    value = value + self.left[rows, :].astype(wide)
                if owner < last:
                    self.arrived(self.right, rows, self.right_got.at[chunk])
                    value = value + self.right[rows, :].astype(wide)
                self.total[rows, :] = value.astype(jnp.bfloat16)
                if owner > 0:
                    self.total_down(chunk, rows).start()
                if owner < last:
                    self.total_up(chunk, rows).start()

            away = jnp.where(me < owner, owner - me, me - owner)
            pair = number - self.lag * (reach + away)
            chunk, rows = self.place(side, pair)
            inside = (pair >= 0) & (pair < self.pairs) & (me != owner)

            @pl.when(inside)
            def _():
                self.arrived(self.total, rows, self.total_got.at[chunk])

            @pl.when(inside & (me < owner) & (me > 0))
            def _():
                self.total_down(chunk, rows).start()

            @pl.when(inside & (me > owner) & (me < last))
            def _():
                self.total_up(chunk, rows).start()

    def finish(self):
        me = lax.axis_index(self.axis)
        last = self.count - 1
        for side, owner in enumerate(self.owners):

            def one(pair, carry):
                chunk, rows = self.place(side, pair)

                @pl.when(me < owner)
                def _():
                    self.part_up(chunk, rows).wait_send()

                @pl.when(me > owner)
                def _():
                    self.part_down(chunk, rows).wait_send()

                @pl.when((me <= owner) & (me > 0))
                def _():
                    self.total_down(chunk, rows).wait_send()

                @pl.when((me >= owner) & (me < last))
                def _():
                    self.total_up(chunk, rows).wait_send()

                return carry

            lax.fori_loop(0, self.pairs, one, 0)


SUM_ROWS = 16
BACK_ROWS = 32


def combine_sum_kernel(count, slots_ref, back_ref, out_ref, own, left, right, stage, total, sems):
    rows, width = own.shape
    places = back_ref.shape[0]
    line = LineSum("tp", count, SUM_ROWS, rows // SUM_ROWS // 2, own, left, right, stage, total, sems, 3)
    barrier = pltpu.get_barrier_semaphore()
    line.signal_neighbours(barrier)
    size, depth = 256, 512

    def one(number, carry):
        spot = pl.ds(pl.multiple_of(number * size, size), size)
        slots = slots_ref[spot, :]
        value = jnp.zeros((size, width), jnp.float32)
        for start in range(0, places, depth):
            lane = lax.broadcasted_iota(jnp.int32, (size, depth), 1) + start
            hit = (lane == slots[:, 0:1]) | (lane == slots[:, 1:2])
            value = value + dot_nn(
                jnp.where(hit, 1.0, 0.0).astype(jnp.bfloat16), back_ref[start : start + depth, :]
            )
        own[spot, :] = value.astype(jnp.bfloat16)
        return carry

    lax.fori_loop(0, rows // size, one, 0)
    pl.semaphore_wait(barrier, line.neighbours())

    def step(number, carry):
        line.step(number)
        return carry

    lax.fori_loop(0, line.steps, step, 0)
    out_ref[...] = total[...]
    line.finish()


def combine_sum(slots, back, rows):
    width = back.shape[1]
    vmem = pl.BlockSpec(memory_space=pltpu.VMEM)
    return pl.pallas_call(
        functools.partial(combine_sum_kernel, lax.axis_size("tp")),
        out_shape=jax.ShapeDtypeStruct((rows, width), jnp.bfloat16),
        in_specs=[vmem, vmem],
        out_specs=vmem,
        scratch_shapes=[pltpu.VMEM((rows, width), jnp.bfloat16)] + LineSum.scratch(rows, width, SUM_ROWS),
        compiler_params=pltpu.CompilerParams(
            collective_id=0, has_side_effects=True, vmem_limit_bytes=48 * MIB
        ),
        cost_estimate=pl.CostEstimate(
            flops=2 * rows * back.shape[0] * width, bytes_accessed=200 * rows * width, transcendentals=0
        ),
    )(slots, back)


def attend_back_kernel(length, rows, tile, chunk, n_pairs_all, n_ctx, n_tp, q_ref, k_ref, v_ref, g_ref, m_ref, log_ref, line_ref, part_ref, dq_ref, dkv_ref, sums_ref, total_ref, strip, gather, dk_ref, dv_ref, mine_ref, got_ref, swap_send, swap_got, left, right, stage, total, sems):
    pair = pl.program_id(0)
    step = pl.program_id(1)
    n_pairs = n_pairs_all
    steps = rows // tile
    span = line_ref.shape[2]
    last = length // LANES - 1
    here = lax.axis_index("ctx")
    turn = pair * steps + step
    line_sum = LineSum("tp", n_tp, BACK_ROWS, part_ref.shape[0] // BACK_ROWS // 2, part_ref, left, right, stage, total, sems, 2)
    barrier = pltpu.get_barrier_semaphore()

    def swap(slot, peer):
        return remote(
            mine_ref.at[peer], got_ref.at[slot, here], swap_send.at[slot, peer], swap_got.at[slot, here], {"ctx": peer}
        )

    def arrival(slot, peer):
        return remote(
            mine_ref.at[peer], got_ref.at[slot, peer], swap_send.at[slot, peer], swap_got.at[slot, peer], {"ctx": peer}
        )

    @pl.when(turn == 0)
    def _():
        line_sum.signal_neighbours(barrier)
        for peer in range(n_ctx):

            @pl.when(peer != here)
            def _():
                pl.semaphore_signal(
                    barrier, inc=1, device_id={"ctx": peer}, device_id_type=pl.DeviceIdType.MESH
                )

        pl.semaphore_wait(barrier, line_sum.neighbours() + (n_ctx - 1))

    @pl.when(step == 0)
    def _():
        for half in range(2):
            line = jnp.broadcast_to(line_ref[0, half : half + 1, :], (LANES, span))
            strip[half] = pltpu.roll(line, span - LANES, 1, stride=1, stride_axis=0).astype(strip.dtype)
        gather[...] = jnp.zeros_like(gather)
        dk_ref[...] = jnp.zeros_like(dk_ref)
        dv_ref[...] = jnp.zeros_like(dv_ref)

    chunks = length // chunk
    turns = n_pairs_all * steps * chunks

    def sum_step(number, carry):
        line_sum.step(number)
        return carry

    query = q_ref[...]
    grad = g_ref[...]
    product = grad.astype(jnp.float32) * m_ref[...].astype(jnp.float32)
    owns, grads, deltas, logs = [], [], [], []
    for half in range(2):
        mine = half_mask((tile, LANES), half)
        owns.append(jnp.where(mine, query, jnp.zeros_like(query)))
        grads.append(jnp.where(mine, grad, jnp.zeros_like(grad)))
        picks = half_mask((8, LANES), half).astype(jnp.float32)
        deltas.append(
            lax.dot_general(picks, product, (((1,), (1,)), ((), ())), precision=lax.Precision.HIGHEST, preferred_element_type=jnp.float32)[0:1, :]
        )
        logs.append(log_ref[0, half : half + 1, :])

    def one_chunk(number, carry):
        outs = []
        now = turn * chunks + number
        lax.fori_loop(now * line_sum.steps // turns, (now + 1) * line_sum.steps // turns, sum_step, 0)
        base = pl.multiple_of(number * chunk, chunk)
        keys = k_ref[pl.ds(base, chunk), :]
        values = v_ref[pl.ds(base, chunk), :]
        new_key = dk_ref[pl.ds(base, chunk), :]
        new_value = dv_ref[pl.ds(base, chunk), :]
        for half in range(2):
            logit = dot_nt(keys, owns[half])
            places = []
            bias = []
            for group in range(chunk // LANES):
                row_group = number * (chunk // LANES) + group
                start = pl.multiple_of((last - row_group) * LANES + step * tile, LANES)
                places.append(start)
                bias.append(strip[half, :, pl.ds(start, tile)].astype(jnp.float32))
            bias = jnp.concatenate(bias, 0) if len(bias) > 1 else bias[0]
            shares = jnp.exp(logit + bias - logs[half])
            grad_shares = dot_nt(values, grads[half])
            scores = shares * (grad_shares - deltas[half])
            low_shares = shares.astype(jnp.bfloat16)
            low_scores = scores.astype(jnp.bfloat16)
            new_value = new_value + dot_nn(low_shares, grads[half])
            new_key = new_key + dot_nn(low_scores, owns[half])
            outs.append(carry[half] + dot_tn(low_scores, keys))
            for group, start in enumerate(places):
                gather[half, :, pl.ds(start, tile)] += scores[group * LANES : (group + 1) * LANES]
        dk_ref[pl.ds(base, chunk), :] = new_key
        dv_ref[pl.ds(base, chunk), :] = new_value
        return tuple(outs)

    zero = jnp.zeros((tile, LANES), jnp.float32)
    first, second = lax.fori_loop(0, length // chunk, one_chunk, (zero, zero))
    both = jnp.where(half_mask((tile, LANES), 0), first, second)
    dq_ref[...] = (both * (DH**-0.5)).astype(dq_ref.dtype)

    @pl.when(step == steps - 1)
    def _():
        for peer in range(n_ctx):
            spot = slice(peer * rows, (peer + 1) * rows)

            @pl.when((peer != here) & (pair > 0))
            def _():
                swap(pair - 1, peer).wait_send()

            mine_ref[peer, :, :LANES] = dk_ref[spot, :].astype(jnp.bfloat16)
            mine_ref[peer, :, LANES:] = dv_ref[spot, :].astype(jnp.bfloat16)

            @pl.when(peer != here)
            def _():
                swap(pair, peer).start()

        got_ref[pair, here] = mine_ref[here]
        for half in range(2):
            values = gather[half]
            size = LANES // 2
            while size >= 1:
                values = values[:size] + pltpu.roll(values[size : 2 * size], span - size, 1)
                size //= 2
            sums_ref[0, half : half + 1, :] = pltpu.roll(jnp.broadcast_to(values, (8, span)), LANES, 1)[0:1]

    @pl.when((step == steps - 1) & (pair == n_pairs - 1))
    def _():
        total_ref[...] = total[...]
        for slot in range(2):
            for peer in range(n_ctx):

                @pl.when(peer != here)
                def _():
                    arrival(slot, peer).wait_recv()

            value = got_ref[slot, 0].astype(jnp.float32)
            for peer in range(1, n_ctx):
                value = value + got_ref[slot, peer].astype(jnp.float32)
            dkv_ref[slot] = value.astype(jnp.bfloat16)
        for peer in range(n_ctx):

            @pl.when(peer != here)
            def _():
                swap(1, peer).wait_send()

        line_sum.finish()


def attend_back(query, key_value, grad, mixed, logs, lines, part):
    rows, cols = query.shape
    length = key_value.shape[2]
    pairs = cols // LANES
    depth = 2 if length <= 4096 else 1
    n_ctx = lax.axis_size("ctx")
    tile = 256
    chunk = 512
    span = lines.shape[2]
    width = part.shape[1]
    return pl.pallas_call(
        functools.partial(attend_back_kernel, length, rows, tile, chunk, pairs, n_ctx, lax.axis_size("tp")),
        grid=(pairs, rows // tile),
        in_specs=[
            pl.BlockSpec((tile, LANES), lambda p, t: (t, p)),
            pl.BlockSpec((None, None, length, LANES), lambda p, t: (p, 0, 0, 0), pipeline_mode=pl.Buffered(depth)),
            pl.BlockSpec((None, None, length, LANES), lambda p, t: (p, 1, 0, 0), pipeline_mode=pl.Buffered(depth)),
            pl.BlockSpec((tile, LANES), lambda p, t: (t, p)),
            pl.BlockSpec((tile, LANES), lambda p, t: (t, p)),
            pl.BlockSpec((1, 2, tile), lambda p, t: (p, 0, t)),
            pl.BlockSpec((1, 2, span), lambda p, t: (p, 0, 0)),
            pl.BlockSpec(memory_space=pltpu.VMEM),
        ],
        out_specs=[
            pl.BlockSpec((tile, LANES), lambda p, t: (t, p)),
            pl.BlockSpec(memory_space=pltpu.VMEM),
            pl.BlockSpec((1, 2, span), lambda p, t: (p, 0, 0)),
            pl.BlockSpec(memory_space=pltpu.VMEM),
        ],
        out_shape=[
            jax.ShapeDtypeStruct((rows, cols), jnp.bfloat16),
            jax.ShapeDtypeStruct((pairs, rows, 2 * LANES), jnp.bfloat16),
            jax.ShapeDtypeStruct((pairs, 2, span), jnp.float32),
            jax.ShapeDtypeStruct((rows, width), jnp.bfloat16),
        ],
        scratch_shapes=[
            pltpu.VMEM((2, LANES, span), jnp.float32 if length <= 4096 else jnp.bfloat16),
            pltpu.VMEM((2, LANES, span), jnp.float32),
            pltpu.VMEM((length, LANES), jnp.float32),
            pltpu.VMEM((length, LANES), jnp.float32),
            pltpu.VMEM((n_ctx, rows, 2 * LANES), jnp.bfloat16),
            pltpu.VMEM((pairs, n_ctx, rows, 2 * LANES), jnp.bfloat16),
            pltpu.SemaphoreType.DMA((pairs, n_ctx)),
            pltpu.SemaphoreType.DMA((pairs, n_ctx)),
        ]
        + LineSum.scratch(rows, width, BACK_ROWS),
        compiler_params=pltpu.CompilerParams(
            collective_id=1, has_side_effects=True, vmem_limit_bytes=60 * MIB
        ),
        cost_estimate=pl.CostEstimate(flops=40 * rows * length * cols, bytes_accessed=24 * length * cols, transcendentals=rows * length * cols // DH),
    )(query, key_value, key_value, grad, mixed, logs, lines, part)


def tail_kernel(
    n_fsdp,
    n_ctx,
    n_tp,
    blocks,
    sum_rows,
    part_ref,
    small_ref,
    grad_ref,
    scale_ref,
    p_right,
    s_left,
    p_left,
    w_ref,
    new_left,
    new_w,
    total_ref,
    small_out,
    turned,
    direction,
    squares,
    plane_got,
    line_got,
    line_own,
    plane_send,
    plane_sem,
    tp_send,
    tp_sem,
    left,
    right,
    stage,
    total,
    sems,
):
    turn = pl.program_id(0)
    turns = pl.num_programs(0)
    rights, lefts = blocks
    line = LineSum("tp", n_tp, BACK_ROWS, part_ref.shape[0] // BACK_ROWS // 2, part_ref, left, right, stage, total, sems, 2)
    here = lax.axis_index("fsdp") * n_ctx + lax.axis_index("ctx")
    tp_here = lax.axis_index("tp")
    shards = n_fsdp * n_ctx
    plane = [(f * n_ctx + c, {"fsdp": f, "ctx": c}) for f in range(n_fsdp) for c in range(n_ctx)]
    column = [(t, {"tp": t}) for t in range(n_tp)]
    other = jnp.where(here == 0, 1, 0)
    other_where = {"fsdp": other // n_ctx, "ctx": other % n_ctx}
    other_tp = {"tp": jnp.where(tp_here == 0, 1, 0)}
    middle = rights + 2

    def plane_copy(number, where):
        return remote(small_ref.at[number], plane_got.at[here], plane_send.at[number], plane_sem.at[here], where)

    def tp_copy(number, where):
        return remote(line_own, line_got.at[tp_here], tp_send.at[number], tp_sem.at[tp_here], where)

    @pl.when(turn == 0)
    def _():
        barrier = pltpu.get_barrier_semaphore()
        greet(barrier, here, plane)
        greet(barrier, tp_here, column)
        squares[...] = jnp.zeros_like(squares)
        pl.semaphore_wait(barrier, shards - 1 + n_tp - 1)
        for number, where in plane:

            @pl.when(number != here)
            def _():
                plane_copy(number, where).start()

        plane_got[here] = small_ref[here]

    @pl.when(turn == middle)
    def _():
        for number, where in plane:

            @pl.when(number != here)
            def _():
                remote(plane_got.at[number], plane_got.at[number], plane_sem.at[number], plane_sem.at[number], other_where).wait_recv()

        added = plane_got[0]
        largest = plane_got[0]
        for number in range(1, shards):
            added = added + plane_got[number]
            largest = jnp.maximum(largest, plane_got[number])
        row = lax.broadcasted_iota(jnp.int32, added.shape, 0)
        line_own[...] = jnp.where(row == sum_rows + 1, largest, added)
        for number, where in column:

            @pl.when(number != tp_here)
            def _():
                tp_copy(number, where).start()

        line_got[tp_here] = line_own[...]

    def one(number, carry):
        line.step(number)
        return carry

    lax.fori_loop(turn * line.steps // turns, (turn + 1) * line.steps // turns, one, 0)

    @pl.when(turn < rights)
    def _():
        spot = pl.ds(pl.multiple_of(turn * LANES, LANES), LANES)
        turned[spot, :] = dot_nn(p_right[...].astype(jnp.bfloat16), grad_ref[...]).astype(jnp.bfloat16)

    @pl.when((turn >= rights) & (turn < rights + lefts))
    def _():
        spot = pl.ds(pl.multiple_of((turn - rights) * LANES, LANES), LANES)
        new_left[...] = decay * s_left[...] + (1.0 - decay) * dot_tn(grad_ref[:, spot], grad_ref[...])
        value = dot_nn(turned[...], p_left[...].astype(jnp.bfloat16))
        squares[...] = squares[...] + jnp.sum(value * value, 0, keepdims=True)
        direction[:, spot] = value.astype(jnp.bfloat16)

    @pl.when(turn >= rights + lefts)
    def _():
        spot = pl.ds(pl.multiple_of((turn - rights - lefts) * LANES, LANES), LANES)
        mean = jnp.sum(squares[0:1, :], 1, keepdims=True) / (grad_ref.shape[0] * grad_ref.shape[1])
        factor = scale_ref[0:1, 0:1] * lax.rsqrt(mean + step_epsilon)
        new_w[...] = w_ref[...] - factor * direction[spot, :].astype(jnp.float32)

    @pl.when(turn == turns - 1)
    def _():
        total_ref[...] = total[...]
        for number, where in column:

            @pl.when(number != tp_here)
            def _():
                remote(line_got.at[number], line_got.at[number], tp_sem.at[number], tp_sem.at[number], other_tp).wait_recv()

        added = line_got[0]
        for number in range(1, n_tp):
            added = added + line_got[number]
        row = lax.broadcasted_iota(jnp.int32, added.shape, 0)
        small_out[...] = jnp.where(row < sum_rows, added, line_own[...])
        for number, where in plane:

            @pl.when(number != here)
            def _():
                plane_copy(number, where).wait_send()

        for number, where in column:

            @pl.when(number != tp_here)
            def _():
                tp_copy(number, where).wait_send()

        line.finish()


def tail(part, small, sum_rows, grad, scale, left, right, weight):
    rows, width = part.shape
    deep, wide = grad.shape
    n_fsdp, n_ctx, n_tp = lax.axis_size("fsdp"), lax.axis_size("ctx"), lax.axis_size("tp")
    rights, lefts = deep // LANES, wide // LANES
    turns = 2 * rights + lefts
    small_rows = small.shape[1]
    vmem = pl.BlockSpec(memory_space=pltpu.VMEM)

    def at_right(turn):
        return jnp.minimum(turn, rights - 1)

    def at_left(turn):
        return jnp.clip(turn - rights, 0, lefts - 1)

    def at_weight(turn):
        return jnp.clip(turn - rights - lefts, 0, rights - 1)

    return pl.pallas_call(
        functools.partial(tail_kernel, n_fsdp, n_ctx, n_tp, (rights, lefts), sum_rows),
        grid=(turns,),
        in_specs=[
            vmem,
            vmem,
            vmem,
            vmem,
            pl.BlockSpec((None, LANES, deep), lambda t: (1, at_right(t), 0)),
            pl.BlockSpec((None, LANES, wide), lambda t: (0, at_left(t), 0)),
            pl.BlockSpec((None, wide, LANES), lambda t: (1, 0, at_left(t))),
            pl.BlockSpec((LANES, wide), lambda t: (at_weight(t), 0)),
        ],
        out_specs=[
            pl.BlockSpec((LANES, wide), lambda t: (at_left(t), 0)),
            pl.BlockSpec((LANES, wide), lambda t: (at_weight(t), 0)),
            vmem,
            vmem,
        ],
        out_shape=[
            jax.ShapeDtypeStruct((wide, wide), jnp.float32),
            jax.ShapeDtypeStruct((deep, wide), jnp.float32),
            jax.ShapeDtypeStruct((rows, width), jnp.bfloat16),
            jax.ShapeDtypeStruct((small_rows, LANES), jnp.float32),
        ],
        scratch_shapes=[
            pltpu.VMEM((deep, wide), jnp.bfloat16),
            pltpu.VMEM((deep, wide), jnp.bfloat16),
            pltpu.VMEM((1, LANES), jnp.float32),
            pltpu.VMEM((n_fsdp * n_ctx, small_rows, LANES), jnp.float32),
            pltpu.VMEM((n_tp, small_rows, LANES), jnp.float32),
            pltpu.VMEM((small_rows, LANES), jnp.float32),
            pltpu.SemaphoreType.DMA((n_fsdp * n_ctx,)),
            pltpu.SemaphoreType.DMA((n_fsdp * n_ctx,)),
            pltpu.SemaphoreType.DMA((n_tp,)),
            pltpu.SemaphoreType.DMA((n_tp,)),
        ]
        + LineSum.scratch(rows, width, BACK_ROWS),
        compiler_params=pltpu.CompilerParams(
            collective_id=2, has_side_effects=True, vmem_limit_bytes=56 * MIB
        ),
        cost_estimate=pl.CostEstimate(
            flops=8 * deep * wide * (deep + wide), bytes_accessed=240 * rows * width, transcendentals=0
        ),
    )(part, small, grad, scale, right, left, left, weight)


GELU_A = 0.7978845608028654
GELU_B = 0.044715


def expert_kernel(n_fsdp, n_ctx, slots_ref, second_ref, grad_ref, other_ref, w_ref, out_ref, router_ref, sent_ref, hidden_ref, mixed_ref, choice_ref, rows_out, stage, land, send, got, own_sem):
    experts, capacity, width = stage.shape
    half = w_ref.shape[0] // 2
    rows_all = second_ref.shape[0]
    here = lax.axis_index("fsdp") * n_ctx + lax.axis_index("ctx")
    plane = [(f * n_ctx + c, {"fsdp": f, "ctx": c}) for f in range(n_fsdp) for c in range(n_ctx)]
    other = jnp.where(here == 0, 1, 0)
    barrier = pltpu.get_barrier_semaphore()
    greet(barrier, here, plane)

    def build(expert):
        place = lax.broadcasted_iota(jnp.int32, (capacity, rows_all), 0) + expert * capacity
        hit = (place == slots_ref[0:1, :]) | (place == slots_ref[1:2, :])
        picks = jnp.where(hit, 1.0, 0.0).astype(jnp.bfloat16)
        return dot_nn(picks, second_ref[...]).astype(jnp.bfloat16)

    def copy_to(expert):
        where = {"fsdp": expert // n_ctx, "ctx": expert % n_ctx}
        return remote(stage.at[expert], land.at[here], send.at[expert], got.at[here], where)

    land[here] = build(here)
    pl.semaphore_wait(barrier, experts - 1)

    def post(turn, carry):
        expert = (here + turn) % experts
        stage[expert] = build(expert)
        copy_to(expert).start()
        return carry

    lax.fori_loop(1, experts, post, 0)

    def compute(turn, carry):
        source = (here + experts - turn) % experts

        @pl.when(turn > 0)
        def _():
            where = {"fsdp": other // n_ctx, "ctx": other % n_ctx}
            remote(land.at[source], land.at[source], got.at[source], got.at[source], where).wait_recv()

        rows = land[source]
        first = dot_nt(rows, w_ref[:half, :])
        second = dot_nt(rows, w_ref[half:, :])
        logits = dot_nn(rows, router_ref[...])
        lane = lax.broadcasted_iota(jnp.int32, logits.shape, 1)
        contrast = (lane == here).astype(jnp.float32) - (lane == other_ref[source]).astype(jnp.float32)
        gate = jax.nn.sigmoid(jnp.sum(logits * contrast, 1, keepdims=True))
        square = first * first
        bent = jnp.tanh(GELU_A * first * (1.0 + GELU_B * square))
        rise = 0.5 * (1.0 + bent)
        gelu = first * rise
        slope = rise + 0.5 * GELU_A * first * (1.0 - bent * bent) * (1.0 + 3.0 * GELU_B * square)
        hidden = gelu * second
        plain = dot_nt(grad_ref[source], out_ref[...])
        grad_gate = jnp.sum(plain * hidden, 1, keepdims=True)
        choice = (gate * (1.0 - gate) * grad_gate * contrast).astype(jnp.bfloat16)
        scaled = gate * plain
        grad_first = (scaled * second * slope).astype(jnp.bfloat16)
        grad_second = (scaled * gelu).astype(jnp.bfloat16)
        hidden_ref[source] = (gate * hidden).astype(jnp.bfloat16)
        mixed_ref[0, source] = grad_first
        mixed_ref[1, source] = grad_second
        choice_ref[source] = choice
        sent = dot_nn(grad_first, w_ref[:half, :]) + dot_nn(grad_second, w_ref[half:, :])
        sent_ref[source] = (sent + dot_nt(choice, router_ref[...])).astype(jnp.bfloat16)
        return carry

    lax.fori_loop(0, experts, compute, 0)
    keep = pltpu.make_async_copy(land, rows_out, own_sem)
    keep.start()

    def settle(turn, carry):
        copy_to((here + turn) % experts).wait_send()
        return carry

    lax.fori_loop(1, experts, settle, 0)
    keep.wait()


def expert_chain(slots, second, grads, other, weight, weight_out, router):
    experts, capacity, width = grads.shape
    half = weight.shape[0] // 2
    n_fsdp, n_ctx = lax.axis_size("fsdp"), lax.axis_size("ctx")
    vmem = pl.BlockSpec(memory_space=pltpu.VMEM)
    count = experts * capacity
    return pl.pallas_call(
        functools.partial(expert_kernel, n_fsdp, n_ctx),
        in_specs=[vmem] * 7,
        out_specs=[vmem] * 4 + [pl.BlockSpec(memory_space=pl.ANY)],
        out_shape=[
            jax.ShapeDtypeStruct((experts, capacity, width), jnp.bfloat16),
            jax.ShapeDtypeStruct((experts, capacity, half), jnp.bfloat16),
            jax.ShapeDtypeStruct((2, experts, capacity, half), jnp.bfloat16),
            jax.ShapeDtypeStruct((experts, capacity, LANES), jnp.bfloat16),
            jax.ShapeDtypeStruct((experts, capacity, width), jnp.bfloat16),
        ],
        scratch_shapes=[
            pltpu.VMEM((experts, capacity, width), jnp.bfloat16),
            pltpu.VMEM((experts, capacity, width), jnp.bfloat16),
            pltpu.SemaphoreType.DMA((experts,)),
            pltpu.SemaphoreType.DMA((experts,)),
            pltpu.SemaphoreType.DMA,
        ],
        compiler_params=pltpu.CompilerParams(
            collective_id=4, has_side_effects=True, vmem_limit_bytes=60 * MIB
        ),
        cost_estimate=pl.CostEstimate(
            flops=20 * count * width * half, bytes_accessed=80 * count * width, transcendentals=count * half
        ),
    )(slots, second, grads, other, weight, weight_out, router)


def normalize(values, gain):
    return values * lax.rsqrt(jnp.mean(values * values, -1, keepdims=True) + norm_epsilon) * gain


def gated_gelu(both):
    return jax.nn.gelu(both[..., 0, :], approximate=True) * both[..., 1, :]


def precondition(grad, master, left, right):
    low = grad.astype(jnp.bfloat16)
    new_left = decay * left[0] + (1.0 - decay) * dot_nt(low, low)
    new_right = decay * right[0] + (1.0 - decay) * dot_tn(low, low)
    turned = dot_nn(left[1].astype(jnp.bfloat16), low).astype(jnp.bfloat16)
    direction = dot_nn(turned, right[1].astype(jnp.bfloat16))
    size = jnp.sqrt(jnp.mean(master * master) + step_epsilon)
    step = (
        matrix_rate * size * direction * lax.rsqrt(jnp.mean(direction * direction) + step_epsilon)
    )
    return (new_left, new_right, master - step)


def adapt(grad, moment, master, rate):
    new_moment = decay * moment + (1.0 - decay) * grad * grad
    return (new_moment, master - rate * grad * lax.rsqrt(new_moment + moment_epsilon))


def barrier(*values):
    return lax.optimization_barrier(values)


def crossing(values):
    return lax.all_to_all(values, ("fsdp", "ctx"), split_axis=0, concat_axis=0, tiled=True)


def on_device(
    tokens,
    cotangent,
    routes,
    buckets,
    attention_in,
    attention_out,
    router,
    gains,
    bias_table,
    expert_in,
    expert_out,
    attention_in_left,
    attention_in_right,
    attention_out_left,
    attention_out_right,
    expert_in_left,
    expert_in_right,
    expert_out_left,
    expert_out_right,
    router_moment,
    gains_moment,
    table_moment,
):
    low = jnp.bfloat16
    rows = tokens.shape[0]
    width = tokens.shape[1]
    shards = lax.axis_size("fsdp") * lax.axis_size("ctx")
    n_ctx = lax.axis_size("ctx")
    n_tp = lax.axis_size("tp")
    here = lax.axis_index("fsdp") * n_ctx + lax.axis_index("ctx")
    tp_here = lax.axis_index("tp")
    length = rows * n_ctx
    depth = attention_in.shape[1]
    head_cols = attention_in.shape[2]
    local_heads = head_cols // DH
    head_pairs = head_cols // LANES
    table_size = bias_table.shape[0]
    experts = router.shape[1]
    capacity = rows * TOPK * 5 // (4 * experts)
    slots_all = experts * capacity
    span = length + rows

    sizes = (depth * experts, 2 * depth, table_size * local_heads)
    small = jnp.concatenate(
        [router.astype(low).reshape(-1), gains.astype(low).reshape(-1), bias_table.astype(low).reshape(-1)]
    )
    small = jnp.pad(small, (0, -small.shape[0] % (16 * head_cols))).reshape(-1, head_cols)
    gathered = lax.all_gather(
        jnp.concatenate(
            [
                attention_in.astype(low).reshape(3 * depth, head_cols),
                small,
            ],
            0,
        ),
        ("fsdp", "ctx"),
        axis=0,
        tiled=False,
    )
    entry_full = (
        gathered[:, : 3 * depth]
        .reshape(shards, 3, depth, head_cols)
        .transpose(1, 0, 2, 3)
        .reshape(3, width, head_cols)
    )
    small = gathered[:, 3 * depth :].reshape(shards, -1)
    router_full = small[:, : sizes[0]].reshape(width, experts)
    gains_full = (
        small[:, sizes[0] : sizes[0] + sizes[1]]
        .reshape(shards, 2, depth)
        .transpose(1, 0, 2)
        .reshape(2, width)
    )
    table_full = small[:, sizes[0] + sizes[1] : sum(sizes)].reshape(shards * table_size, local_heads)
    gain_first = gains_full[0].astype(jnp.float32)
    gain_second = gains_full[1].astype(jnp.float32)
    expand_out = expert_out[0].astype(low)

    chosen = routes.reshape(-1)
    route_hits = (chosen[:, None] == jnp.arange(experts, dtype=jnp.int32)[None, :]).astype(
        jnp.int32
    )
    slots = jnp.sum(route_hits * (jnp.cumsum(route_hits, 0) - 1), 1)
    slot_rows = (chosen * capacity + slots).reshape(rows, TOPK)
    place = jnp.arange(slots_all, dtype=jnp.int32)
    first_hit = place[:, None] == slot_rows[None, :, 0]
    second_hit = place[:, None] == slot_rows[None, :, 1]
    picks = (first_hit | second_hit).astype(low)
    other = jnp.sum(
        jnp.where(first_hit, routes[None, :, 1], 0) + jnp.where(second_hit, routes[None, :, 0], 0),
        1,
    )
    grad_buffer = dot_nn(picks, cotangent).astype(low).reshape(experts, capacity, width)
    other_arrived = crossing(other.reshape(experts, capacity)).reshape(-1)

    inputs = tokens.astype(jnp.float32)
    first = normalize(inputs, gain_first).astype(low)
    projected = jnp.einsum(
        "sd,kde->kse", first, entry_full, preferred_element_type=jnp.float32
    )
    query = (projected[0].astype(low) * (DH**-0.5)).astype(low)
    own_pairs = (
        projected[1:].astype(low).reshape(2, rows, head_pairs, LANES).transpose(2, 0, 1, 3)
    )
    low_end = length - rows - lax.axis_index("ctx") * rows
    near = lax.dynamic_slice_in_dim(jnp.pad(buckets, (0, 1)), low_end, span, 0)
    hits = (near[:, None] == jnp.arange(table_full.shape[0], dtype=jnp.int32)[None, :]).astype(low)
    lines = lax.dot_general(
        table_full, hits, (((0,), (1,)), ((), ())), preferred_element_type=jnp.float32
    ).reshape(head_pairs, 2, span)
    hits_back = (near[::-1][:, None] == jnp.arange(table_full.shape[0], dtype=jnp.int32)[None, :]).astype(low)
    back_lines = lax.dot_general(
        table_full, hits_back, (((0,), (1,)), ((), ())), preferred_element_type=jnp.float32
    ).reshape(head_pairs, 2, span)
    exit_piece = attention_out.astype(low)
    exit_rows = lax.dynamic_update_slice_in_dim(
        jnp.zeros((n_tp * head_cols, depth), low), exit_piece, tp_here * head_cols, 0
    )
    for shift in range(1, n_tp):
        piece = lax.ppermute(exit_piece, "tp", [(i, (i + shift) % n_tp) for i in range(n_tp)])
        exit_rows = lax.dynamic_update_slice_in_dim(
            exit_rows, piece, (tp_here + n_tp - shift) % n_tp * head_cols, 0
        )
    exit_all = lax.all_gather(exit_rows, ("fsdp", "ctx"), axis=1, tiled=True)
    exit_own = lax.dynamic_slice_in_dim(exit_all, tp_here * head_cols, head_cols, 0)
    mixed, logs, peak_own, key_value, mixed_all, grad_arrived = attend(
        query, own_pairs, lines, grad_buffer
    )
    value = dot_nn(mixed_all, exit_all)
    middle = inputs + value
    second = normalize(middle, gain_second).astype(low)

    columns = 2 * expert_in.shape[3]
    flat_master = expert_in[0].transpose(1, 2, 0).reshape(columns, width)
    flat_low = flat_master.astype(low)
    wide_router = jnp.pad(router_full, ((0, 0), (0, LANES - experts)))
    half = columns // 2
    sent_grads, gated_hidden, grad_mixed_up, grad_choice, arrived = expert_chain(
        slot_rows.T,
        second,
        grad_arrived,
        other_arrived.reshape(experts, capacity, 1),
        flat_low,
        expand_out,
        wide_router,
    )
    gated_hidden = gated_hidden.reshape(slots_all, half)
    grad_mixed_up = grad_mixed_up.reshape(2, slots_all, half)
    grad_choice = grad_choice.reshape(slots_all, LANES)
    arrived = arrived.reshape(slots_all, width)
    grad_arrived = grad_arrived.reshape(slots_all, width)
    back_grads = crossing(sent_grads.reshape(experts, capacity, width)).reshape(slots_all, width)

    sent_rows = dot_nn(gated_hidden, expand_out).astype(low)
    grad_router = dot_tn(arrived, grad_choice)[:, :experts]
    grad_expand_out = dot_tn(gated_hidden, grad_arrived)
    shrink_left, shrink_right, shrink_new = precondition(
        grad_expand_out, expert_out[0], expert_out_left, expert_out_right
    )
    grad_expand_in = jnp.einsum(
        "gsf,sd->gfd", grad_mixed_up, arrived, preferred_element_type=jnp.float32
    )
    flat_grad = grad_expand_in.reshape(columns, width).astype(low)
    expand_right = decay * expert_in_right[0] + (1.0 - decay) * dot_nt(flat_grad, flat_grad)
    back_grads, sent_rows, grad_router, grad_expand_out, grad_expand_in, shrink_left, shrink_right, shrink_new, expand_right, flat_grad = barrier(
        back_grads, sent_rows, grad_router, grad_expand_out, grad_expand_in, shrink_left, shrink_right, shrink_new, expand_right, flat_grad
    )
    grad_second = combine_sum(slot_rows, back_grads, rows)

    back_rows = crossing(sent_rows.reshape(experts, capacity, width)).reshape(slots_all, width)
    grad_second, back_rows = barrier(grad_second, back_rows)
    result_part = dot_tn(picks, back_rows).astype(low)

    unused, pull = jax.vjp(normalize, middle, gain_second)
    grad_middle_norm, grad_gain_second = pull(grad_second.astype(jnp.float32))
    grad_middle = cotangent.astype(jnp.float32) + grad_middle_norm
    grad_attention = grad_middle.astype(low)
    grad_mixed = dot_nt(grad_attention, exit_own).astype(low)
    grad_query, key_value_grad, sums, result_sum = attend_back(
        query, key_value, grad_mixed, mixed, logs, back_lines, result_part
    )
    result = (middle + result_sum.astype(jnp.float32)).astype(low)
    grad_projected = jnp.stack(
        [
            grad_query,
            jnp.concatenate([key_value_grad[pair, :, :LANES] for pair in range(head_pairs)], 1),
            jnp.concatenate([key_value_grad[pair, :, LANES:] for pair in range(head_pairs)], 1),
        ]
    )
    grad_exit = dot_tn(mixed, grad_attention).astype(low)
    grad_first_part = jnp.einsum(
        "kse,kde->sd", grad_projected, entry_full, preferred_element_type=jnp.float32
    )
    unused, pull = jax.vjp(normalize, inputs, gain_first)
    grad_gain_first = pull(grad_first_part)[1]
    grad_entry = jnp.einsum(
        "sd,kse->dke", first, grad_projected, preferred_element_type=jnp.float32
    ).astype(low)
    table_grad = lax.dot_general(
        hits_back.astype(jnp.float32),
        sums.reshape(local_heads, span),
        (((0,), (1,)), ((), ())),
        precision=highest,
        preferred_element_type=jnp.float32,
    )
    gain_sums = jnp.stack([grad_gain_first, jnp.where(tp_here == 0, grad_gain_second, 0.0)])
    peak_own = peak_own[:, :, 0].reshape(local_heads)
    pieces = [
        grad_router.reshape(shards, -1),
        gain_sums.reshape(2, shards, depth).transpose(1, 0, 2).reshape(shards, -1),
        table_grad.reshape(shards, -1),
        jnp.broadcast_to(peak_own[None], (shards, local_heads)),
    ]
    spots = [0]
    padded = []
    for piece in pieces:
        padded.append(jnp.pad(piece, ((0, 0), (0, -piece.shape[1] % LANES))))
        spots.append(spots[-1] + padded[-1].shape[1] // LANES)
    small = jnp.concatenate(padded, 1)
    small = jnp.pad(small, ((0, 0), (0, -small.shape[1] % (8 * LANES)))).reshape(shards, -1, LANES)
    size = jnp.sqrt(jnp.mean(flat_master * flat_master) + step_epsilon)
    weight_terms = jnp.concatenate(
        [
            grad_entry.reshape(shards, 3 * depth, head_cols),
            grad_exit.reshape(head_cols, shards, depth)
            .transpose(1, 0, 2)
            .reshape(shards, depth, head_cols),
        ],
        1,
    )
    first_part, small, weight_terms = barrier(grad_first_part.astype(low), small, weight_terms)
    weight_terms = crossing(weight_terms)
    expand_left, expand_new, grad_first, small_sum = tail(
        first_part,
        small,
        spots[2],
        flat_grad,
        jnp.full((8, LANES), matrix_rate * size, jnp.float32),
        expert_in_left,
        expert_in_right,
        flat_master,
    )
    grad_first, weight_terms = barrier(grad_first, weight_terms)
    owned = jnp.sum(weight_terms.astype(jnp.float32), 0)
    owned_in = owned[: 3 * depth].reshape(depth, 3, head_cols).transpose(1, 0, 2)
    owned_out = owned[3 * depth :].reshape(head_cols, depth)
    grad_tokens = grad_middle + pull(grad_first.astype(jnp.float32))[0]

    def small_piece(number, shape):
        count = 1
        for extent in shape:
            count *= extent
        return small_sum[spots[number] : spots[number + 1]].reshape(-1)[:count].reshape(shape)

    owned_router = small_piece(0, (depth, experts))
    owned_gains = small_piece(1, (2, depth))
    owned_table = small_piece(2, (table_size, local_heads))
    peaks = small_piece(3, (local_heads,))
    in_left, in_right, in_new = jax.vmap(precondition)(
        owned_in,
        attention_in,
        jnp.swapaxes(attention_in_left, 0, 1),
        jnp.swapaxes(attention_in_right, 0, 1),
    )
    column = jnp.sqrt(jnp.repeat(clip_level / jnp.maximum(peaks, clip_level), DH))
    in_new = in_new * jnp.stack([column, column, jnp.ones_like(column)])[:, None, :]
    out_left, out_right, out_new = precondition(
        owned_out, attention_out, attention_out_left, attention_out_right
    )
    router_moment_new, router_new = adapt(owned_router, router_moment, router, router_rate)
    gains_moment_new, gains_new = adapt(owned_gains, gains_moment, gains, gain_rate)
    table_moment_new, table_new = adapt(owned_table, table_moment, bias_table, table_rate)
    return (
        result,
        grad_tokens,
        owned_in,
        in_new,
        in_left,
        in_right,
        owned_out,
        out_new,
        out_left,
        out_right,
        grad_expand_in.transpose(2, 0, 1)[None],
        expand_new.reshape(2, -1, width).transpose(2, 0, 1)[None],
        expand_left,
        expand_right,
        grad_expand_out[None],
        shrink_new[None],
        shrink_left,
        shrink_right,
        owned_router,
        router_moment_new,
        router_new,
        owned_gains,
        gains_moment_new,
        gains_new,
        owned_table,
        table_moment_new,
        table_new,
    )


def solution(mesh):
    placed = (
        P(("fsdp", "ctx"), None),
        P(("fsdp", "ctx"), None),
        P(("fsdp", "ctx"), None),
        P(),
        P(None, ("fsdp", "ctx"), "tp"),
        P("tp", ("fsdp", "ctx")),
        P(("fsdp", "ctx"), None),
        P(None, ("fsdp", "ctx")),
        P(("fsdp", "ctx"), "tp"),
        P(("fsdp", "ctx"), None, None, "tp"),
        P(("fsdp", "ctx"), "tp", None),
        P(None, None, ("fsdp", "ctx", "tp"), None),
        P(None, None, ("fsdp", "ctx", "tp"), None),
        P(None, ("fsdp", "ctx", "tp"), None),
        P(None, ("fsdp", "ctx", "tp"), None),
        P(None, ("fsdp", "ctx", "tp"), None),
        P(None, ("fsdp", "ctx", "tp"), None),
        P(None, ("fsdp", "ctx", "tp"), None),
        P(None, ("fsdp", "ctx", "tp"), None),
        P(("fsdp", "ctx"), None),
        P(None, ("fsdp", "ctx")),
        P(("fsdp", "ctx"), "tp"),
    )
    return jax.shard_map(
        on_device,
        mesh=mesh,
        in_specs=placed,
        out_specs=(
            P(("fsdp", "ctx"), None),
            P(("fsdp", "ctx"), None),
            P(None, ("fsdp", "ctx"), "tp"),
            P(None, ("fsdp", "ctx"), "tp"),
            P(None, ("fsdp", "ctx", "tp"), None),
            P(None, ("fsdp", "ctx", "tp"), None),
            P("tp", ("fsdp", "ctx")),
            P("tp", ("fsdp", "ctx")),
            P(("fsdp", "ctx", "tp"), None),
            P(("fsdp", "ctx", "tp"), None),
            P(("fsdp", "ctx"), None, None, "tp"),
            P(("fsdp", "ctx"), None, None, "tp"),
            P(("fsdp", "ctx", "tp"), None),
            P(("fsdp", "ctx", "tp"), None),
            P(("fsdp", "ctx"), "tp", None),
            P(("fsdp", "ctx"), "tp", None),
            P(("fsdp", "ctx", "tp"), None),
            P(("fsdp", "ctx", "tp"), None),
            P(("fsdp", "ctx"), None),
            P(("fsdp", "ctx"), None),
            P(("fsdp", "ctx"), None),
            P(None, ("fsdp", "ctx")),
            P(None, ("fsdp", "ctx")),
            P(None, ("fsdp", "ctx")),
            P(("fsdp", "ctx"), "tp"),
            P(("fsdp", "ctx"), "tp"),
            P(("fsdp", "ctx"), "tp"),
        ),
        check_vma=False,
    )
```

```python
import functools

import jax
import jax.numpy as jnp
from jax import lax
from jax.experimental import pallas as pl
from jax.experimental.pallas import tpu as pltpu

from jax.sharding import PartitionSpec as P

DH = 64
LANES = 128
MIB = 1024 * 1024


TOPK = 2

highest = lax.Precision.HIGHEST
norm_epsilon = 1e-06
step_epsilon = 1e-06
moment_epsilon = 1e-08
clip_level = 4.0
decay = 0.5
matrix_rate = 0.3
gain_rate = 0.25
router_rate = 0.01
table_rate = 0.3


def dot_nt(left, right):
    return lax.dot_general(left, right, (((1,), (1,)), ((), ())), preferred_element_type=jnp.float32)


def dot_nn(left, right):
    return lax.dot_general(left, right, (((1,), (0,)), ((), ())), preferred_element_type=jnp.float32)


def dot_tn(left, right):
    return lax.dot_general(left, right, (((0,), (0,)), ((), ())), preferred_element_type=jnp.float32)


def half_mask(shape, half):
    lane = lax.broadcasted_iota(jnp.int32, shape, 1)
    return (lane // DH) == half


def attend_kernel(length, rows, tile, pairs, n_fsdp, n_ctx, n_tp, q_ref, own_ref, line_ref, cross_ref, mixed_ref, log_ref, peak_ref, kv_out, all_out, cross_out, strip, wide, kv_ref, all_ref, kv_send, kv_got, mix_send, mix_got, out_sem, cross_send, cross_got):
    pair = pl.program_id(0)
    step = pl.program_id(1)
    steps = rows // tile
    span = line_ref.shape[2]
    here = lax.axis_index("ctx")
    tp_here = lax.axis_index("tp")
    own_rows = pl.ds(pl.multiple_of(here * rows, rows), rows)
    ctx_peers = [(number, {"ctx": number}) for number in range(n_ctx)]
    tp_peers = [(number, {"tp": number}) for number in range(n_tp)]
    shard = lax.axis_index("fsdp") * n_ctx + here
    plane = [(f * n_ctx + c, {"fsdp": f, "ctx": c}) for f in range(n_fsdp) for c in range(n_ctx)]
    other = jnp.where(shard == 0, 1, 0)
    other_plane = {"fsdp": other // n_ctx, "ctx": other % n_ctx}
    other_ctx = {"ctx": jnp.where(here == 0, 1, 0)}
    other_tp = {"tp": jnp.where(tp_here == 0, 1, 0)}

    def kv_copy(slot, number, where):
        return remote(
            own_ref.at[slot], kv_ref.at[slot, :, own_rows, :], kv_send.at[slot, number], kv_got.at[slot, here], where
        )

    def kv_arrived(slot, number):
        spot = kv_ref.at[slot, :, pl.ds(number * rows, rows), :]
        remote(spot, spot, kv_got.at[slot, number], kv_got.at[slot, number], other_ctx).wait_recv()

    def cross_copy(number, where):
        return remote(
            cross_ref.at[number], cross_out.at[shard], cross_send.at[number], cross_got.at[shard], where
        )

    def cross_own():
        return pltpu.make_async_copy(cross_ref.at[shard], cross_out.at[shard], out_sem.at[2])

    def mix_spot(slot, turn, number):
        return (
            pl.ds(pl.multiple_of(turn * tile, tile), tile),
            pl.ds(pl.multiple_of((number * pairs + slot) * LANES, LANES), LANES),
        )

    def mix_copy(slot, turn, number, where):
        spot = all_ref.at[mix_spot(slot, turn, tp_here)]
        return remote(spot, spot, mix_send.at[slot, turn, number], mix_got.at[slot, turn, tp_here], where)

    @pl.when((pair == 0) & (step == 0))
    def _():
        barrier = pltpu.get_barrier_semaphore()
        greet(barrier, shard, plane)
        greet(barrier, tp_here, tp_peers)
        pl.semaphore_wait(barrier, n_fsdp * n_ctx - 1 + n_tp - 1)
        for slot in range(pairs):
            for number, where in ctx_peers:

                @pl.when(number != here)
                def _():
                    kv_copy(slot, number, where).start()

            kv_ref[slot, :, own_rows, :] = own_ref[slot]

    @pl.when(step == 0)
    def _():
        for half in range(2):
            line = jnp.broadcast_to(line_ref[0, half : half + 1, :], (LANES, span))
            strip[half] = pltpu.roll(line, span - (LANES - 1), 1, stride=1, stride_axis=0)
        wide[:, LANES:] = jnp.ones((length, LANES), jnp.bfloat16)
        peak_ref[...] = jnp.full(peak_ref.shape, -jnp.inf, jnp.float32)
        for number, where in ctx_peers:

            @pl.when(number != here)
            def _():
                kv_arrived(pair, number)

        wide[:, :LANES] = kv_ref[pair, 1]

    @pl.when((pair == 0) & (step == 2))
    def _():
        cross_own().start()
        for number, where in plane:

            @pl.when(number != shard)
            def _():
                cross_copy(number, where).start()

    query = q_ref[...]
    groups = tile // LANES
    last = rows // LANES - 1
    mixed = jnp.zeros((tile, LANES), jnp.float32)
    for half in range(2):
        mine = half_mask((tile, LANES), half)
        own = jnp.where(mine, query, jnp.zeros_like(query))
        logit = dot_nt(own, kv_ref[pair, 0])
        top = jnp.max(logit, 1, keepdims=True)
        bias = []
        for group in range(groups):
            start = pl.multiple_of((last - (step * groups + group)) * LANES, LANES)
            bias.append(strip[half, :, pl.ds(start, length)])
        bias = jnp.concatenate(bias, 0) if groups > 1 else bias[0]
        powers = jnp.exp(logit + bias - top)
        both = dot_nn(powers.astype(jnp.bfloat16), wide[...])
        total = both[:, LANES:]
        mixed = jnp.where(mine, both[:, :LANES] / total, mixed)
        log_total = top + jnp.log(total)
        log_ref[0, half : half + 1, :] = log_total.T[0:1, :]
        best = jnp.max(jnp.broadcast_to(top, (tile, LANES)), 0, keepdims=True)
        peak_ref[0, half : half + 1, :] = jnp.maximum(peak_ref[0, half : half + 1, :], best)
    low = mixed.astype(jnp.bfloat16)
    mixed_ref[...] = low
    all_ref[mix_spot(pair, step, tp_here)] = low
    for number, where in reversed(tp_peers):

        @pl.when(number != tp_here)
        def _():
            mix_copy(pair, step, number, where).start()

    @pl.when((pair == pairs - 1) & (step == steps - 1))
    def _():
        for slot in range(pairs):
            for number, where in ctx_peers:

                @pl.when(number != here)
                def _():
                    kv_copy(slot, number, where).wait_send()

        def one(index, carry):
            slot, turn = index // steps, index % steps
            for number, where in tp_peers:

                @pl.when(number != tp_here)
                def _():
                    spot = all_ref.at[mix_spot(slot, turn, number)]
                    got = mix_got.at[slot, turn, number]
                    remote(spot, spot, got, got, other_tp).wait_recv()
                    mix_copy(slot, turn, number, where).wait_send()

            return carry

        kept = pltpu.make_async_copy(kv_ref, kv_out, out_sem.at[0])
        kept.start()
        lax.fori_loop(0, pairs * steps, one, 0)
        gathered = pltpu.make_async_copy(all_ref, all_out, out_sem.at[1])
        gathered.start()
        kept.wait()
        gathered.wait()
        cross_own().wait()
        for number, where in plane:

            @pl.when(number != shard)
            def _():
                spot = cross_out.at[number]
                remote(spot, spot, cross_got.at[number], cross_got.at[number], other_plane).wait_recv()
                cross_copy(number, where).wait_send()


def attend(query, own, lines, cross):
    rows, cols = query.shape
    n_fsdp, n_ctx, n_tp = lax.axis_size("fsdp"), lax.axis_size("ctx"), lax.axis_size("tp")
    length = rows * n_ctx
    pairs = cols // LANES
    tile = 256 if length <= 4096 else 128
    span = lines.shape[2]
    vmem = pl.BlockSpec(memory_space=pltpu.VMEM)
    return pl.pallas_call(
        functools.partial(attend_kernel, length, rows, tile, pairs, n_fsdp, n_ctx, n_tp),
        grid=(pairs, rows // tile),
        in_specs=[
            pl.BlockSpec((tile, LANES), lambda p, t: (t, p)),
            vmem,
            pl.BlockSpec((1, 2, span), lambda p, t: (p, 0, 0)),
            pl.BlockSpec(memory_space=pl.ANY),
        ],
        out_specs=[
            pl.BlockSpec((tile, LANES), lambda p, t: (t, p)),
            pl.BlockSpec((1, 2, tile), lambda p, t: (p, 0, t)),
            pl.BlockSpec((1, 2, LANES), lambda p, t: (p, 0, 0)),
            pl.BlockSpec(memory_space=pl.ANY),
            pl.BlockSpec(memory_space=pl.ANY),
            pl.BlockSpec(memory_space=pl.ANY),
        ],
        out_shape=[
            jax.ShapeDtypeStruct((rows, cols), jnp.bfloat16),
            jax.ShapeDtypeStruct((pairs, 2, rows), jnp.float32),
            jax.ShapeDtypeStruct((pairs, 2, LANES), jnp.float32),
            jax.ShapeDtypeStruct((pairs, 2, length, LANES), jnp.bfloat16),
            jax.ShapeDtypeStruct((rows, n_tp * cols), jnp.bfloat16),
            jax.ShapeDtypeStruct(cross.shape, cross.dtype),
        ],
        scratch_shapes=[
            pltpu.VMEM((2, LANES, span), jnp.float32),
            pltpu.VMEM((length, 2 * LANES), jnp.bfloat16),
            pltpu.VMEM((pairs, 2, length, LANES), jnp.bfloat16),
            pltpu.VMEM((rows, n_tp * cols), jnp.bfloat16),
            pltpu.SemaphoreType.DMA((pairs, n_ctx)),
            pltpu.SemaphoreType.DMA((pairs, n_ctx)),
            pltpu.SemaphoreType.DMA((pairs, rows // tile, n_tp)),
            pltpu.SemaphoreType.DMA((pairs, rows // tile, n_tp)),
            pltpu.SemaphoreType.DMA((3,)),
            pltpu.SemaphoreType.DMA((n_fsdp * n_ctx,)),
            pltpu.SemaphoreType.DMA((n_fsdp * n_ctx,)),
        ],
        compiler_params=pltpu.CompilerParams(
            collective_id=3, has_side_effects=True, vmem_limit_bytes=60 * MIB
        ),
        cost_estimate=pl.CostEstimate(flops=100 * rows * length * cols, bytes_accessed=8 * length * cols, transcendentals=rows * length * cols // DH),
    )(query, own, lines, cross)


def remote(source, target, send, receive, where):
    return pltpu.make_async_remote_copy(
        src_ref=source,
        dst_ref=target,
        send_sem=send,
        recv_sem=receive,
        device_id=where,
        device_id_type=pl.DeviceIdType.MESH,
    )


def greet(barrier, me, peers):
    for number, where in peers:

        @pl.when(number != me)
        def _():
            pl.semaphore_signal(
                barrier, inc=1, device_id=where, device_id_type=pl.DeviceIdType.MESH
            )


class LineSum:
    def __init__(self, axis, count, size, pairs, own, left, right, stage, total, sems, lag):
        self.lag = lag
        self.axis, self.count, self.size, self.pairs = axis, count, size, pairs
        self.own, self.left, self.right, self.stage, self.total = own, left, right, stage, total
        self.part_send, self.left_got, self.right_got, self.total_got, self.down_send, self.up_send = (
            sems.at[0], sems.at[1], sems.at[2], sems.at[3], sems.at[4], sems.at[5],
        )
        self.owners = ((count - 1) // 2, count // 2)
        self.reach = [max(owner, count - 1 - owner) for owner in self.owners]
        self.steps = pairs + self.lag * 2 * max(self.reach)

    @staticmethod
    def scratch(rows, width, size):
        return [pltpu.VMEM((rows, width), jnp.bfloat16)] * 4 + [
            pltpu.SemaphoreType.DMA((6, rows // size))
        ]

    def signal_neighbours(self, barrier):
        me = lax.axis_index(self.axis)
        for offset, there in ((-1, me > 0), (1, me < self.count - 1)):

            @pl.when(there)
            def _():
                pl.semaphore_signal(
                    barrier,
                    inc=1,
                    device_id={self.axis: me + offset},
                    device_id_type=pl.DeviceIdType.MESH,
                )

    def neighbours(self):
        me = lax.axis_index(self.axis)
        return jnp.where(me > 0, 1, 0) + jnp.where(me < self.count - 1, 1, 0)

    def place(self, side, pair):
        chunk = side * self.pairs + pair
        return chunk, pl.ds(pl.multiple_of(chunk * self.size, self.size), self.size)

    def part_up(self, chunk, rows):
        me = lax.axis_index(self.axis)
        return remote(
            self.stage.at[rows], self.left.at[rows], self.part_send.at[chunk], self.left_got.at[chunk], {self.axis: me + 1}
        )

    def part_down(self, chunk, rows):
        me = lax.axis_index(self.axis)
        return remote(
            self.stage.at[rows], self.right.at[rows], self.part_send.at[chunk], self.right_got.at[chunk], {self.axis: me - 1}
        )

    def total_up(self, chunk, rows):
        me = lax.axis_index(self.axis)
        return remote(
            self.total.at[rows], self.total.at[rows], self.up_send.at[chunk], self.total_got.at[chunk], {self.axis: me + 1}
        )

    def total_down(self, chunk, rows):
        me = lax.axis_index(self.axis)
        return remote(
            self.total.at[rows], self.total.at[rows], self.down_send.at[chunk], self.total_got.at[chunk], {self.axis: me - 1}
        )

    def arrived(self, target, rows, got):
        me = lax.axis_index(self.axis)
        peer = jnp.where(me < self.count - 1, me + 1, me - 1)
        remote(target.at[rows], target.at[rows], got, got, {self.axis: peer}).wait_recv()

    def step(self, number):
        me = lax.axis_index(self.axis)
        last = self.count - 1
        wide = jnp.float32
        for side, owner in enumerate(self.owners):
            reach = self.reach[side]
            from_end = jnp.where(me < owner, me, jnp.where(me > owner, last - me, reach))
            pair = number - self.lag * from_end
            chunk, rows = self.place(side, pair)
            inside = (pair >= 0) & (pair < self.pairs)

            @pl.when(inside & (me == 0) & (me < owner))
            def _():
                self.stage[rows, :] = self.own[rows, :]
                self.part_up(chunk, rows).start()

            @pl.when(inside & (me > 0) & (me < owner))
            def _():
                self.arrived(self.left, rows, self.left_got.at[chunk])
                self.stage[rows, :] = (self.own[rows, :].astype(wide) + self.left[rows, :].astype(wide)).astype(jnp.bfloat16)
                self.part_up(chunk, rows).start()

            @pl.when(inside & (me == last) & (me > owner))
            def _():
                self.stage[rows, :] = self.own[rows, :]
                self.part_down(chunk, rows).start()

            @pl.when(inside & (me < last) & (me > owner))
            def _():
                self.arrived(self.right, rows, self.right_got.at[chunk])
                self.stage[rows, :] = (self.own[rows, :].astype(wide) + self.right[rows, :].astype(wide)).astype(jnp.bfloat16)
                self.part_down(chunk, rows).start()

            @pl.when(inside & (me == owner))
            def _():
                value = self.own[rows, :].astype(wide)
                if owner > 0:
                    self.arrived(self.left, rows, self.left_got.at[chunk])
                    value = value + self.left[rows, :].astype(wide)
                if owner < last:
                    self.arrived(self.right, rows, self.right_got.at[chunk])
                    value = value + self.right[rows, :].astype(wide)
                self.total[rows, :] = value.astype(jnp.bfloat16)
                if owner > 0:
                    self.total_down(chunk, rows).start()
                if owner < last:
                    self.total_up(chunk, rows).start()

            away = jnp.where(me < owner, owner - me, me - owner)
            pair = number - self.lag * (reach + away)
            chunk, rows = self.place(side, pair)
            inside = (pair >= 0) & (pair < self.pairs) & (me != owner)

            @pl.when(inside)
            def _():
                self.arrived(self.total, rows, self.total_got.at[chunk])

            @pl.when(inside & (me < owner) & (me > 0))
            def _():
                self.total_down(chunk, rows).start()

            @pl.when(inside & (me > owner) & (me < last))
            def _():
                self.total_up(chunk, rows).start()

    def finish(self):
        me = lax.axis_index(self.axis)
        last = self.count - 1
        for side, owner in enumerate(self.owners):

            def one(pair, carry):
                chunk, rows = self.place(side, pair)

                @pl.when(me < owner)
                def _():
                    self.part_up(chunk, rows).wait_send()

                @pl.when(me > owner)
                def _():
                    self.part_down(chunk, rows).wait_send()

                @pl.when((me <= owner) & (me > 0))
                def _():
                    self.total_down(chunk, rows).wait_send()

                @pl.when((me >= owner) & (me < last))
                def _():
                    self.total_up(chunk, rows).wait_send()

                return carry

            lax.fori_loop(0, self.pairs, one, 0)


SUM_ROWS = 16
BACK_ROWS = 32


def combine_sum_kernel(count, slots_ref, back_ref, out_ref, own, left, right, stage, total, sems):
    rows, width = own.shape
    places = back_ref.shape[0]
    line = LineSum("tp", count, SUM_ROWS, rows // SUM_ROWS // 2, own, left, right, stage, total, sems, 3)
    barrier = pltpu.get_barrier_semaphore()
    line.signal_neighbours(barrier)
    size, depth = 256, 512

    def one(number, carry):
        spot = pl.ds(pl.multiple_of(number * size, size), size)
        slots = slots_ref[spot, :]
        value = jnp.zeros((size, width), jnp.float32)
        for start in range(0, places, depth):
            lane = lax.broadcasted_iota(jnp.int32, (size, depth), 1) + start
            hit = (lane == slots[:, 0:1]) | (lane == slots[:, 1:2])
            value = value + dot_nn(
                jnp.where(hit, 1.0, 0.0).astype(jnp.bfloat16), back_ref[start : start + depth, :]
            )
        own[spot, :] = value.astype(jnp.bfloat16)
        return carry

    lax.fori_loop(0, rows // size, one, 0)
    pl.semaphore_wait(barrier, line.neighbours())

    def step(number, carry):
        line.step(number)
        return carry

    lax.fori_loop(0, line.steps, step, 0)
    out_ref[...] = total[...]
    line.finish()


def combine_sum(slots, back, rows):
    width = back.shape[1]
    vmem = pl.BlockSpec(memory_space=pltpu.VMEM)
    return pl.pallas_call(
        functools.partial(combine_sum_kernel, lax.axis_size("tp")),
        out_shape=jax.ShapeDtypeStruct((rows, width), jnp.bfloat16),
        in_specs=[vmem, vmem],
        out_specs=vmem,
        scratch_shapes=[pltpu.VMEM((rows, width), jnp.bfloat16)] + LineSum.scratch(rows, width, SUM_ROWS),
        compiler_params=pltpu.CompilerParams(
            collective_id=0, has_side_effects=True, vmem_limit_bytes=48 * MIB
        ),
        cost_estimate=pl.CostEstimate(
            flops=2 * rows * back.shape[0] * width, bytes_accessed=200 * rows * width, transcendentals=0
        ),
    )(slots, back)


def attend_back_kernel(length, rows, tile, chunk, n_pairs_all, n_ctx, n_tp, q_ref, k_ref, v_ref, g_ref, m_ref, log_ref, line_ref, part_ref, dq_ref, dkv_ref, sums_ref, total_ref, strip, gather, dk_ref, dv_ref, mine_ref, got_ref, swap_send, swap_got, left, right, stage, total, sems):
    pair = pl.program_id(0)
    step = pl.program_id(1)
    n_pairs = n_pairs_all
    steps = rows // tile
    span = line_ref.shape[2]
    last = length // LANES - 1
    here = lax.axis_index("ctx")
    turn = pair * steps + step
    line_sum = LineSum("tp", n_tp, BACK_ROWS, part_ref.shape[0] // BACK_ROWS // 2, part_ref, left, right, stage, total, sems, 2)
    barrier = pltpu.get_barrier_semaphore()

    def swap(slot, peer):
        return remote(
            mine_ref.at[peer], got_ref.at[slot, here], swap_send.at[slot, peer], swap_got.at[slot, here], {"ctx": peer}
        )

    def arrival(slot, peer):
        return remote(
            mine_ref.at[peer], got_ref.at[slot, peer], swap_send.at[slot, peer], swap_got.at[slot, peer], {"ctx": peer}
        )

    @pl.when(turn == 0)
    def _():
        line_sum.signal_neighbours(barrier)
        for peer in range(n_ctx):

            @pl.when(peer != here)
            def _():
                pl.semaphore_signal(
                    barrier, inc=1, device_id={"ctx": peer}, device_id_type=pl.DeviceIdType.MESH
                )

        pl.semaphore_wait(barrier, line_sum.neighbours() + (n_ctx - 1))

    @pl.when(step == 0)
    def _():
        for half in range(2):
            line = jnp.broadcast_to(line_ref[0, half : half + 1, :], (LANES, span))
            strip[half] = pltpu.roll(line, span - LANES, 1, stride=1, stride_axis=0).astype(strip.dtype)
        gather[...] = jnp.zeros_like(gather)
        dk_ref[...] = jnp.zeros_like(dk_ref)
        dv_ref[...] = jnp.zeros_like(dv_ref)

    chunks = length // chunk
    turns = n_pairs_all * steps * chunks

    def sum_step(number, carry):
        line_sum.step(number)
        return carry

    query = q_ref[...]
    grad = g_ref[...]
    product = grad.astype(jnp.float32) * m_ref[...].astype(jnp.float32)
    owns, grads, deltas, logs = [], [], [], []
    for half in range(2):
        mine = half_mask((tile, LANES), half)
        owns.append(jnp.where(mine, query, jnp.zeros_like(query)))
        grads.append(jnp.where(mine, grad, jnp.zeros_like(grad)))
        picks = half_mask((8, LANES), half).astype(jnp.float32)
        deltas.append(
            lax.dot_general(picks, product, (((1,), (1,)), ((), ())), precision=lax.Precision.HIGHEST, preferred_element_type=jnp.float32)[0:1, :]
        )
        logs.append(log_ref[0, half : half + 1, :])

    def one_chunk(number, carry):
        outs = []
        now = turn * chunks + number
        lax.fori_loop(now * line_sum.steps // turns, (now + 1) * line_sum.steps // turns, sum_step, 0)
        base = pl.multiple_of(number * chunk, chunk)
        keys = k_ref[pl.ds(base, chunk), :]
        values = v_ref[pl.ds(base, chunk), :]
        new_key = dk_ref[pl.ds(base, chunk), :]
        new_value = dv_ref[pl.ds(base, chunk), :]
        for half in range(2):
            logit = dot_nt(keys, owns[half])
            places = []
            bias = []
            for group in range(chunk // LANES):
                row_group = number * (chunk // LANES) + group
                start = pl.multiple_of((last - row_group) * LANES + step * tile, LANES)
                places.append(start)
                bias.append(strip[half, :, pl.ds(start, tile)].astype(jnp.float32))
            bias = jnp.concatenate(bias, 0) if len(bias) > 1 else bias[0]
            shares = jnp.exp(logit + bias - logs[half])
            grad_shares = dot_nt(values, grads[half])
            scores = shares * (grad_shares - deltas[half])
            low_shares = shares.astype(jnp.bfloat16)
            low_scores = scores.astype(jnp.bfloat16)
            new_value = new_value + dot_nn(low_shares, grads[half])
            new_key = new_key + dot_nn(low_scores, owns[half])
            outs.append(carry[half] + dot_tn(low_scores, keys))
            for group, start in enumerate(places):
                gather[half, :, pl.ds(start, tile)] += scores[group * LANES : (group + 1) * LANES]
        dk_ref[pl.ds(base, chunk), :] = new_key
        dv_ref[pl.ds(base, chunk), :] = new_value
        return tuple(outs)

    zero = jnp.zeros((tile, LANES), jnp.float32)
    first, second = lax.fori_loop(0, length // chunk, one_chunk, (zero, zero))
    both = jnp.where(half_mask((tile, LANES), 0), first, second)
    dq_ref[...] = (both * (DH**-0.5)).astype(dq_ref.dtype)

    @pl.when(step == steps - 1)
    def _():
        for peer in range(n_ctx):
            spot = slice(peer * rows, (peer + 1) * rows)

            @pl.when((peer != here) & (pair > 0))
            def _():
                swap(pair - 1, peer).wait_send()

            mine_ref[peer, :, :LANES] = dk_ref[spot, :].astype(jnp.bfloat16)
            mine_ref[peer, :, LANES:] = dv_ref[spot, :].astype(jnp.bfloat16)

            @pl.when(peer != here)
            def _():
                swap(pair, peer).start()

        got_ref[pair, here] = mine_ref[here]
        for half in range(2):
            values = gather[half]
            size = LANES // 2
            while size >= 1:
                values = values[:size] + pltpu.roll(values[size : 2 * size], span - size, 1)
                size //= 2
            sums_ref[0, half : half + 1, :] = pltpu.roll(jnp.broadcast_to(values, (8, span)), LANES, 1)[0:1]

    @pl.when((step == steps - 1) & (pair == n_pairs - 1))
    def _():
        total_ref[...] = total[...]
        for slot in range(2):
            for peer in range(n_ctx):

                @pl.when(peer != here)
                def _():
                    arrival(slot, peer).wait_recv()

            value = got_ref[slot, 0].astype(jnp.float32)
            for peer in range(1, n_ctx):
                value = value + got_ref[slot, peer].astype(jnp.float32)
            dkv_ref[slot] = value.astype(jnp.bfloat16)
        for peer in range(n_ctx):

            @pl.when(peer != here)
            def _():
                swap(1, peer).wait_send()

        line_sum.finish()


def attend_back(query, key_value, grad, mixed, logs, lines, part):
    rows, cols = query.shape
    length = key_value.shape[2]
    pairs = cols // LANES
    depth = 2 if length <= 4096 else 1
    n_ctx = lax.axis_size("ctx")
    tile = 256
    chunk = 512
    span = lines.shape[2]
    width = part.shape[1]
    return pl.pallas_call(
        functools.partial(attend_back_kernel, length, rows, tile, chunk, pairs, n_ctx, lax.axis_size("tp")),
        grid=(pairs, rows // tile),
        in_specs=[
            pl.BlockSpec((tile, LANES), lambda p, t: (t, p)),
            pl.BlockSpec((None, None, length, LANES), lambda p, t: (p, 0, 0, 0), pipeline_mode=pl.Buffered(depth)),
            pl.BlockSpec((None, None, length, LANES), lambda p, t: (p, 1, 0, 0), pipeline_mode=pl.Buffered(depth)),
            pl.BlockSpec((tile, LANES), lambda p, t: (t, p)),
            pl.BlockSpec((tile, LANES), lambda p, t: (t, p)),
            pl.BlockSpec((1, 2, tile), lambda p, t: (p, 0, t)),
            pl.BlockSpec((1, 2, span), lambda p, t: (p, 0, 0)),
            pl.BlockSpec(memory_space=pltpu.VMEM),
        ],
        out_specs=[
            pl.BlockSpec((tile, LANES), lambda p, t: (t, p)),
            pl.BlockSpec(memory_space=pltpu.VMEM),
            pl.BlockSpec((1, 2, span), lambda p, t: (p, 0, 0)),
            pl.BlockSpec(memory_space=pltpu.VMEM),
        ],
        out_shape=[
            jax.ShapeDtypeStruct((rows, cols), jnp.bfloat16),
            jax.ShapeDtypeStruct((pairs, rows, 2 * LANES), jnp.bfloat16),
            jax.ShapeDtypeStruct((pairs, 2, span), jnp.float32),
            jax.ShapeDtypeStruct((rows, width), jnp.bfloat16),
        ],
        scratch_shapes=[
            pltpu.VMEM((2, LANES, span), jnp.float32 if length <= 4096 else jnp.bfloat16),
            pltpu.VMEM((2, LANES, span), jnp.float32),
            pltpu.VMEM((length, LANES), jnp.float32),
            pltpu.VMEM((length, LANES), jnp.float32),
            pltpu.VMEM((n_ctx, rows, 2 * LANES), jnp.bfloat16),
            pltpu.VMEM((pairs, n_ctx, rows, 2 * LANES), jnp.bfloat16),
            pltpu.SemaphoreType.DMA((pairs, n_ctx)),
            pltpu.SemaphoreType.DMA((pairs, n_ctx)),
        ]
        + LineSum.scratch(rows, width, BACK_ROWS),
        compiler_params=pltpu.CompilerParams(
            collective_id=1, has_side_effects=True, vmem_limit_bytes=60 * MIB
        ),
        cost_estimate=pl.CostEstimate(flops=40 * rows * length * cols, bytes_accessed=24 * length * cols, transcendentals=rows * length * cols // DH),
    )(query, key_value, key_value, grad, mixed, logs, lines, part)


def tail_kernel(
    n_fsdp,
    n_ctx,
    n_tp,
    blocks,
    sum_rows,
    part_ref,
    small_ref,
    grad_ref,
    scale_ref,
    p_right,
    s_left,
    p_left,
    w_ref,
    new_left,
    new_w,
    total_ref,
    small_out,
    turned,
    direction,
    squares,
    plane_got,
    line_got,
    line_own,
    plane_send,
    plane_sem,
    tp_send,
    tp_sem,
    left,
    right,
    stage,
    total,
    sems,
):
    turn = pl.program_id(0)
    turns = pl.num_programs(0)
    rights, lefts = blocks
    line = LineSum("tp", n_tp, BACK_ROWS, part_ref.shape[0] // BACK_ROWS // 2, part_ref, left, right, stage, total, sems, 2)
    here = lax.axis_index("fsdp") * n_ctx + lax.axis_index("ctx")
    tp_here = lax.axis_index("tp")
    shards = n_fsdp * n_ctx
    plane = [(f * n_ctx + c, {"fsdp": f, "ctx": c}) for f in range(n_fsdp) for c in range(n_ctx)]
    column = [(t, {"tp": t}) for t in range(n_tp)]
    other = jnp.where(here == 0, 1, 0)
    other_where = {"fsdp": other // n_ctx, "ctx": other % n_ctx}
    other_tp = {"tp": jnp.where(tp_here == 0, 1, 0)}
    middle = rights + 2

    def plane_copy(number, where):
        return remote(small_ref.at[number], plane_got.at[here], plane_send.at[number], plane_sem.at[here], where)

    def tp_copy(number, where):
        return remote(line_own, line_got.at[tp_here], tp_send.at[number], tp_sem.at[tp_here], where)

    @pl.when(turn == 0)
    def _():
        barrier = pltpu.get_barrier_semaphore()
        greet(barrier, here, plane)
        greet(barrier, tp_here, column)
        squares[...] = jnp.zeros_like(squares)
        pl.semaphore_wait(barrier, shards - 1 + n_tp - 1)
        for number, where in plane:

            @pl.when(number != here)
            def _():
                plane_copy(number, where).start()

        plane_got[here] = small_ref[here]

    @pl.when(turn == middle)
    def _():
        for number, where in plane:

            @pl.when(number != here)
            def _():
                remote(plane_got.at[number], plane_got.at[number], plane_sem.at[number], plane_sem.at[number], other_where).wait_recv()

        added = plane_got[0]
        largest = plane_got[0]
        for number in range(1, shards):
            added = added + plane_got[number]
            largest = jnp.maximum(largest, plane_got[number])
        row = lax.broadcasted_iota(jnp.int32, added.shape, 0)
        line_own[...] = jnp.where(row == sum_rows + 1, largest, added)
        for number, where in column:

            @pl.when(number != tp_here)
            def _():
                tp_copy(number, where).start()

        line_got[tp_here] = line_own[...]

    def one(number, carry):
        line.step(number)
        return carry

    lax.fori_loop(turn * line.steps // turns, (turn + 1) * line.steps // turns, one, 0)

    @pl.when(turn < rights)
    def _():
        spot = pl.ds(pl.multiple_of(turn * LANES, LANES), LANES)
        turned[spot, :] = dot_nn(p_right[...].astype(jnp.bfloat16), grad_ref[...]).astype(jnp.bfloat16)

    @pl.when((turn >= rights) & (turn < rights + lefts))
    def _():
        spot = pl.ds(pl.multiple_of((turn - rights) * LANES, LANES), LANES)
        new_left[...] = decay * s_left[...] + (1.0 - decay) * dot_tn(grad_ref[:, spot], grad_ref[...])
        value = dot_nn(turned[...], p_left[...].astype(jnp.bfloat16))
        squares[...] = squares[...] + jnp.sum(value * value, 0, keepdims=True)
        direction[:, spot] = value.astype(jnp.bfloat16)

    @pl.when(turn >= rights + lefts)
    def _():
        spot = pl.ds(pl.multiple_of((turn - rights - lefts) * LANES, LANES), LANES)
        mean = jnp.sum(squares[0:1, :], 1, keepdims=True) / (grad_ref.shape[0] * grad_ref.shape[1])
        factor = scale_ref[0:1, 0:1] * lax.rsqrt(mean + step_epsilon)
        new_w[...] = w_ref[...] - factor * direction[spot, :].astype(jnp.float32)

    @pl.when(turn == turns - 1)
    def _():
        total_ref[...] = total[...]
        for number, where in column:

            @pl.when(number != tp_here)
            def _():
                remote(line_got.at[number], line_got.at[number], tp_sem.at[number], tp_sem.at[number], other_tp).wait_recv()

        added = line_got[0]
        for number in range(1, n_tp):
            added = added + line_got[number]
        row = lax.broadcasted_iota(jnp.int32, added.shape, 0)
        small_out[...] = jnp.where(row < sum_rows, added, line_own[...])
        for number, where in plane:

            @pl.when(number != here)
            def _():
                plane_copy(number, where).wait_send()

        for number, where in column:

            @pl.when(number != tp_here)
            def _():
                tp_copy(number, where).wait_send()

        line.finish()


def tail(part, small, sum_rows, grad, scale, left, right, weight):
    rows, width = part.shape
    deep, wide = grad.shape
    n_fsdp, n_ctx, n_tp = lax.axis_size("fsdp"), lax.axis_size("ctx"), lax.axis_size("tp")
    rights, lefts = deep // LANES, wide // LANES
    turns = 2 * rights + lefts
    small_rows = small.shape[1]
    vmem = pl.BlockSpec(memory_space=pltpu.VMEM)

    def at_right(turn):
        return jnp.minimum(turn, rights - 1)

    def at_left(turn):
        return jnp.clip(turn - rights, 0, lefts - 1)

    def at_weight(turn):
        return jnp.clip(turn - rights - lefts, 0, rights - 1)

    return pl.pallas_call(
        functools.partial(tail_kernel, n_fsdp, n_ctx, n_tp, (rights, lefts), sum_rows),
        grid=(turns,),
        in_specs=[
            vmem,
            vmem,
            vmem,
            vmem,
            pl.BlockSpec((None, LANES, deep), lambda t: (1, at_right(t), 0)),
            pl.BlockSpec((None, LANES, wide), lambda t: (0, at_left(t), 0)),
            pl.BlockSpec((None, wide, LANES), lambda t: (1, 0, at_left(t))),
            pl.BlockSpec((LANES, wide), lambda t: (at_weight(t), 0)),
        ],
        out_specs=[
            pl.BlockSpec((LANES, wide), lambda t: (at_left(t), 0)),
            pl.BlockSpec((LANES, wide), lambda t: (at_weight(t), 0)),
            vmem,
            vmem,
        ],
        out_shape=[
            jax.ShapeDtypeStruct((wide, wide), jnp.float32),
            jax.ShapeDtypeStruct((deep, wide), jnp.float32),
            jax.ShapeDtypeStruct((rows, width), jnp.bfloat16),
            jax.ShapeDtypeStruct((small_rows, LANES), jnp.float32),
        ],
        scratch_shapes=[
            pltpu.VMEM((deep, wide), jnp.bfloat16),
            pltpu.VMEM((deep, wide), jnp.bfloat16),
            pltpu.VMEM((1, LANES), jnp.float32),
            pltpu.VMEM((n_fsdp * n_ctx, small_rows, LANES), jnp.float32),
            pltpu.VMEM((n_tp, small_rows, LANES), jnp.float32),
            pltpu.VMEM((small_rows, LANES), jnp.float32),
            pltpu.SemaphoreType.DMA((n_fsdp * n_ctx,)),
            pltpu.SemaphoreType.DMA((n_fsdp * n_ctx,)),
            pltpu.SemaphoreType.DMA((n_tp,)),
            pltpu.SemaphoreType.DMA((n_tp,)),
        ]
        + LineSum.scratch(rows, width, BACK_ROWS),
        compiler_params=pltpu.CompilerParams(
            collective_id=2, has_side_effects=True, vmem_limit_bytes=56 * MIB
        ),
        cost_estimate=pl.CostEstimate(
            flops=8 * deep * wide * (deep + wide), bytes_accessed=240 * rows * width, transcendentals=0
        ),
    )(part, small, grad, scale, right, left, left, weight)


GELU_A = 0.7978845608028654
GELU_B = 0.044715


def expert_kernel(n_fsdp, n_ctx, slots_ref, second_ref, grad_ref, other_ref, w_ref, out_ref, router_ref, sent_ref, hidden_ref, mixed_ref, choice_ref, rows_out, stage, land, w_low, out_low, send, got, own_sem):
    experts, capacity, width = stage.shape
    half = w_ref.shape[0] // 2
    rows_all = second_ref.shape[0]
    here = lax.axis_index("fsdp") * n_ctx + lax.axis_index("ctx")
    plane = [(f * n_ctx + c, {"fsdp": f, "ctx": c}) for f in range(n_fsdp) for c in range(n_ctx)]
    other = jnp.where(here == 0, 1, 0)
    barrier = pltpu.get_barrier_semaphore()
    greet(barrier, here, plane)

    def build(expert):
        place = lax.broadcasted_iota(jnp.int32, (capacity, rows_all), 0) + expert * capacity
        hit = (place == slots_ref[0:1, :]) | (place == slots_ref[1:2, :])
        picks = jnp.where(hit, 1.0, 0.0).astype(jnp.bfloat16)
        return dot_nn(picks, second_ref[...]).astype(jnp.bfloat16)

    def copy_to(expert):
        where = {"fsdp": expert // n_ctx, "ctx": expert % n_ctx}
        return remote(stage.at[expert], land.at[here], send.at[expert], got.at[here], where)

    land[here] = build(here)
    pl.semaphore_wait(barrier, experts - 1)

    def post(turn, carry):
        expert = (here + turn) % experts
        stage[expert] = build(expert)
        copy_to(expert).start()
        return carry

    lax.fori_loop(1, experts, post, 0)

    def narrow(part, carry):
        spot = pl.ds(pl.multiple_of(part * 64, 64), 64)
        both = pl.ds(pl.multiple_of(part * 128, 128), 128)
        w_low[both, :] = w_ref[both, :].astype(jnp.bfloat16)
        out_low[spot, :] = out_ref[spot, :].astype(jnp.bfloat16)
        return carry

    lax.fori_loop(0, half // 64, narrow, 0)

    def compute(turn, carry):
        source = (here + experts - turn) % experts

        @pl.when(turn > 0)
        def _():
            where = {"fsdp": other // n_ctx, "ctx": other % n_ctx}
            remote(land.at[source], land.at[source], got.at[source], got.at[source], where).wait_recv()

        rows = land[source]
        first = dot_nt(rows, w_low[:half, :])
        second = dot_nt(rows, w_low[half:, :])
        logits = dot_nn(rows, router_ref[...])
        lane = lax.broadcasted_iota(jnp.int32, logits.shape, 1)
        contrast = (lane == here).astype(jnp.float32) - (lane == other_ref[source]).astype(jnp.float32)
        gate = jax.nn.sigmoid(jnp.sum(logits * contrast, 1, keepdims=True))
        square = first * first
        bent = jnp.tanh(GELU_A * first * (1.0 + GELU_B * square))
        rise = 0.5 * (1.0 + bent)
        gelu = first * rise
        slope = rise + 0.5 * GELU_A * first * (1.0 - bent * bent) * (1.0 + 3.0 * GELU_B * square)
        hidden = gelu * second
        plain = dot_nt(grad_ref[source], out_low[...])
        grad_gate = jnp.sum(plain * hidden, 1, keepdims=True)
        choice = (gate * (1.0 - gate) * grad_gate * contrast).astype(jnp.bfloat16)
        scaled = gate * plain
        grad_first = (scaled * second * slope).astype(jnp.bfloat16)
        grad_second = (scaled * gelu).astype(jnp.bfloat16)
        hidden_ref[source] = (gate * hidden).astype(jnp.bfloat16)
        mixed_ref[0, source] = grad_first
        mixed_ref[1, source] = grad_second
        choice_ref[source] = choice
        sent = dot_nn(grad_first, w_low[:half, :]) + dot_nn(grad_second, w_low[half:, :])
        sent_ref[source] = (sent + dot_nt(choice, router_ref[...])).astype(jnp.bfloat16)
        return carry

    lax.fori_loop(0, experts, compute, 0)
    keep = pltpu.make_async_copy(land, rows_out, own_sem)
    keep.start()

    def settle(turn, carry):
        copy_to((here + turn) % experts).wait_send()
        return carry

    lax.fori_loop(1, experts, settle, 0)
    keep.wait()


def expert_chain(slots, second, grads, other, weight, weight_out, router):
    experts, capacity, width = grads.shape
    half = weight.shape[0] // 2
    n_fsdp, n_ctx = lax.axis_size("fsdp"), lax.axis_size("ctx")
    vmem = pl.BlockSpec(memory_space=pltpu.VMEM)
    count = experts * capacity
    return pl.pallas_call(
        functools.partial(expert_kernel, n_fsdp, n_ctx),
        in_specs=[vmem] * 7,
        out_specs=[vmem] * 4 + [pl.BlockSpec(memory_space=pl.ANY)],
        out_shape=[
            jax.ShapeDtypeStruct((experts, capacity, width), jnp.bfloat16),
            jax.ShapeDtypeStruct((experts, capacity, half), jnp.bfloat16),
            jax.ShapeDtypeStruct((2, experts, capacity, half), jnp.bfloat16),
            jax.ShapeDtypeStruct((experts, capacity, LANES), jnp.bfloat16),
            jax.ShapeDtypeStruct((experts, capacity, width), jnp.bfloat16),
        ],
        scratch_shapes=[
            pltpu.VMEM((experts, capacity, width), jnp.bfloat16),
            pltpu.VMEM((experts, capacity, width), jnp.bfloat16),
            pltpu.VMEM((2 * half, width), jnp.bfloat16),
            pltpu.VMEM((half, width), jnp.bfloat16),
            pltpu.SemaphoreType.DMA((experts,)),
            pltpu.SemaphoreType.DMA((experts,)),
            pltpu.SemaphoreType.DMA,
        ],
        compiler_params=pltpu.CompilerParams(
            collective_id=4, has_side_effects=True, vmem_limit_bytes=60 * MIB
        ),
        cost_estimate=pl.CostEstimate(
            flops=20 * count * width * half, bytes_accessed=80 * count * width, transcendentals=count * half
        ),
    )(slots, second, grads, other, weight, weight_out, router)


def normalize(values, gain):
    return values * lax.rsqrt(jnp.mean(values * values, -1, keepdims=True) + norm_epsilon) * gain


def gated_gelu(both):
    return jax.nn.gelu(both[..., 0, :], approximate=True) * both[..., 1, :]


def precondition(grad, master, left, right):
    low = grad.astype(jnp.bfloat16)
    new_left = decay * left[0] + (1.0 - decay) * dot_nt(low, low)
    new_right = decay * right[0] + (1.0 - decay) * dot_tn(low, low)
    turned = dot_nn(left[1].astype(jnp.bfloat16), low).astype(jnp.bfloat16)
    direction = dot_nn(turned, right[1].astype(jnp.bfloat16))
    size = jnp.sqrt(jnp.mean(master * master) + step_epsilon)
    step = (
        matrix_rate * size * direction * lax.rsqrt(jnp.mean(direction * direction) + step_epsilon)
    )
    return (new_left, new_right, master - step)


def adapt(grad, moment, master, rate):
    new_moment = decay * moment + (1.0 - decay) * grad * grad
    return (new_moment, master - rate * grad * lax.rsqrt(new_moment + moment_epsilon))


def barrier(*values):
    return lax.optimization_barrier(values)


def crossing(values):
    return lax.all_to_all(values, ("fsdp", "ctx"), split_axis=0, concat_axis=0, tiled=True)


def on_device(
    tokens,
    cotangent,
    routes,
    buckets,
    attention_in,
    attention_out,
    router,
    gains,
    bias_table,
    expert_in,
    expert_out,
    attention_in_left,
    attention_in_right,
    attention_out_left,
    attention_out_right,
    expert_in_left,
    expert_in_right,
    expert_out_left,
    expert_out_right,
    router_moment,
    gains_moment,
    table_moment,
):
    low = jnp.bfloat16
    rows = tokens.shape[0]
    width = tokens.shape[1]
    shards = lax.axis_size("fsdp") * lax.axis_size("ctx")
    n_ctx = lax.axis_size("ctx")
    n_tp = lax.axis_size("tp")
    here = lax.axis_index("fsdp") * n_ctx + lax.axis_index("ctx")
    tp_here = lax.axis_index("tp")
    length = rows * n_ctx
    depth = attention_in.shape[1]
    head_cols = attention_in.shape[2]
    local_heads = head_cols // DH
    head_pairs = head_cols // LANES
    table_size = bias_table.shape[0]
    experts = router.shape[1]
    capacity = rows * TOPK * 5 // (4 * experts)
    slots_all = experts * capacity
    span = length + rows

    sizes = (depth * experts, 2 * depth, table_size * local_heads)
    small = jnp.concatenate(
        [router.astype(low).reshape(-1), gains.astype(low).reshape(-1), bias_table.astype(low).reshape(-1)]
    )
    small = jnp.pad(small, (0, -small.shape[0] % (16 * head_cols))).reshape(-1, head_cols)
    gathered = lax.all_gather(
        jnp.concatenate(
            [
                attention_in.astype(low).reshape(3 * depth, head_cols),
                small,
            ],
            0,
        ),
        ("fsdp", "ctx"),
        axis=0,
        tiled=False,
    )
    entry_full = (
        gathered[:, : 3 * depth]
        .reshape(shards, 3, depth, head_cols)
        .transpose(1, 0, 2, 3)
        .reshape(3, width, head_cols)
    )
    small = gathered[:, 3 * depth :].reshape(shards, -1)
    router_full = small[:, : sizes[0]].reshape(width, experts)
    gains_full = (
        small[:, sizes[0] : sizes[0] + sizes[1]]
        .reshape(shards, 2, depth)
        .transpose(1, 0, 2)
        .reshape(2, width)
    )
    table_full = small[:, sizes[0] + sizes[1] : sum(sizes)].reshape(shards * table_size, local_heads)
    gain_first = gains_full[0].astype(jnp.float32)
    gain_second = gains_full[1].astype(jnp.float32)
    expand_out = expert_out[0].astype(low)

    chosen = routes.reshape(-1)
    route_hits = (chosen[:, None] == jnp.arange(experts, dtype=jnp.int32)[None, :]).astype(
        jnp.int32
    )
    slots = jnp.sum(route_hits * (jnp.cumsum(route_hits, 0) - 1), 1)
    slot_rows = (chosen * capacity + slots).reshape(rows, TOPK)
    place = jnp.arange(slots_all, dtype=jnp.int32)
    first_hit = place[:, None] == slot_rows[None, :, 0]
    second_hit = place[:, None] == slot_rows[None, :, 1]
    picks = (first_hit | second_hit).astype(low)
    other = jnp.sum(
        jnp.where(first_hit, routes[None, :, 1], 0) + jnp.where(second_hit, routes[None, :, 0], 0),
        1,
    )
    grad_buffer = dot_nn(picks, cotangent).astype(low).reshape(experts, capacity, width)
    other_arrived = crossing(other.reshape(experts, capacity)).reshape(-1)

    inputs = tokens.astype(jnp.float32)
    first = normalize(inputs, gain_first).astype(low)
    projected = jnp.einsum(
        "sd,kde->kse", first, entry_full, preferred_element_type=jnp.float32
    )
    query = (projected[0].astype(low) * (DH**-0.5)).astype(low)
    own_pairs = (
        projected[1:].astype(low).reshape(2, rows, head_pairs, LANES).transpose(2, 0, 1, 3)
    )
    low_end = length - rows - lax.axis_index("ctx") * rows
    near = lax.dynamic_slice_in_dim(jnp.pad(buckets, (0, 1)), low_end, span, 0)
    hits = (near[:, None] == jnp.arange(table_full.shape[0], dtype=jnp.int32)[None, :]).astype(low)
    lines = lax.dot_general(
        table_full, hits, (((0,), (1,)), ((), ())), preferred_element_type=jnp.float32
    ).reshape(head_pairs, 2, span)
    hits_back = (near[::-1][:, None] == jnp.arange(table_full.shape[0], dtype=jnp.int32)[None, :]).astype(low)
    back_lines = lax.dot_general(
        table_full, hits_back, (((0,), (1,)), ((), ())), preferred_element_type=jnp.float32
    ).reshape(head_pairs, 2, span)
    exit_piece = attention_out.astype(low)
    exit_rows = lax.dynamic_update_slice_in_dim(
        jnp.zeros((n_tp * head_cols, depth), low), exit_piece, tp_here * head_cols, 0
    )
    for shift in range(1, n_tp):
        piece = lax.ppermute(exit_piece, "tp", [(i, (i + shift) % n_tp) for i in range(n_tp)])
        exit_rows = lax.dynamic_update_slice_in_dim(
            exit_rows, piece, (tp_here + n_tp - shift) % n_tp * head_cols, 0
        )
    exit_all = lax.all_gather(exit_rows, ("fsdp", "ctx"), axis=1, tiled=True)
    exit_own = lax.dynamic_slice_in_dim(exit_all, tp_here * head_cols, head_cols, 0)
    mixed, logs, peak_own, key_value, mixed_all, grad_arrived = attend(
        query, own_pairs, lines, grad_buffer
    )
    value = dot_nn(mixed_all, exit_all)
    middle = inputs + value
    second = normalize(middle, gain_second).astype(low)

    columns = 2 * expert_in.shape[3]
    flat_master = expert_in[0].transpose(1, 2, 0).reshape(columns, width)
    wide_router = jnp.pad(router_full, ((0, 0), (0, LANES - experts)))
    half = columns // 2
    sent_grads, gated_hidden, grad_mixed_up, grad_choice, arrived = expert_chain(
        slot_rows.T,
        second,
        grad_arrived,
        other_arrived.reshape(experts, capacity, 1),
        flat_master,
        expert_out[0],
        wide_router,
    )
    gated_hidden = gated_hidden.reshape(slots_all, half)
    grad_mixed_up = grad_mixed_up.reshape(2, slots_all, half)
    grad_choice = grad_choice.reshape(slots_all, LANES)
    arrived = arrived.reshape(slots_all, width)
    grad_arrived = grad_arrived.reshape(slots_all, width)
    back_grads = crossing(sent_grads.reshape(experts, capacity, width)).reshape(slots_all, width)

    sent_rows = dot_nn(gated_hidden, expand_out).astype(low)
    grad_router = dot_tn(arrived, grad_choice)[:, :experts]
    grad_expand_out = dot_tn(gated_hidden, grad_arrived)
    shrink_left, shrink_right, shrink_new = precondition(
        grad_expand_out, expert_out[0], expert_out_left, expert_out_right
    )
    grad_expand_in = jnp.einsum(
        "gsf,sd->gfd", grad_mixed_up, arrived, preferred_element_type=jnp.float32
    )
    flat_grad = grad_expand_in.reshape(columns, width).astype(low)
    expand_right = decay * expert_in_right[0] + (1.0 - decay) * dot_nt(flat_grad, flat_grad)
    back_grads, sent_rows, grad_router, grad_expand_out, grad_expand_in, shrink_left, shrink_right, shrink_new, expand_right, flat_grad = barrier(
        back_grads, sent_rows, grad_router, grad_expand_out, grad_expand_in, shrink_left, shrink_right, shrink_new, expand_right, flat_grad
    )
    grad_second = combine_sum(slot_rows, back_grads, rows)

    back_rows = crossing(sent_rows.reshape(experts, capacity, width)).reshape(slots_all, width)
    grad_second, back_rows = barrier(grad_second, back_rows)
    result_part = dot_tn(picks, back_rows).astype(low)

    unused, pull = jax.vjp(normalize, middle, gain_second)
    grad_middle_norm, grad_gain_second = pull(grad_second.astype(jnp.float32))
    grad_middle = cotangent.astype(jnp.float32) + grad_middle_norm
    grad_attention = grad_middle.astype(low)
    grad_mixed = dot_nt(grad_attention, exit_own).astype(low)
    grad_query, key_value_grad, sums, result_sum = attend_back(
        query, key_value, grad_mixed, mixed, logs, back_lines, result_part
    )
    result = (middle + result_sum.astype(jnp.float32)).astype(low)
    grad_projected = jnp.stack(
        [
            grad_query,
            jnp.concatenate([key_value_grad[pair, :, :LANES] for pair in range(head_pairs)], 1),
            jnp.concatenate([key_value_grad[pair, :, LANES:] for pair in range(head_pairs)], 1),
        ]
    )
    grad_exit = dot_tn(mixed, grad_attention).astype(low)
    grad_first_part = jnp.einsum(
        "kse,kde->sd", grad_projected, entry_full, preferred_element_type=jnp.float32
    )
    unused, pull = jax.vjp(normalize, inputs, gain_first)
    grad_gain_first = pull(grad_first_part)[1]
    grad_entry = jnp.einsum(
        "sd,kse->dke", first, grad_projected, preferred_element_type=jnp.float32
    ).astype(low)
    table_grad = lax.dot_general(
        hits_back.astype(jnp.float32),
        sums.reshape(local_heads, span),
        (((0,), (1,)), ((), ())),
        precision=highest,
        preferred_element_type=jnp.float32,
    )
    gain_sums = jnp.stack([grad_gain_first, jnp.where(tp_here == 0, grad_gain_second, 0.0)])
    peak_own = peak_own[:, :, 0].reshape(local_heads)
    pieces = [
        grad_router.reshape(shards, -1),
        gain_sums.reshape(2, shards, depth).transpose(1, 0, 2).reshape(shards, -1),
        table_grad.reshape(shards, -1),
        jnp.broadcast_to(peak_own[None], (shards, local_heads)),
    ]
    spots = [0]
    padded = []
    for piece in pieces:
        padded.append(jnp.pad(piece, ((0, 0), (0, -piece.shape[1] % LANES))))
        spots.append(spots[-1] + padded[-1].shape[1] // LANES)
    small = jnp.concatenate(padded, 1)
    small = jnp.pad(small, ((0, 0), (0, -small.shape[1] % (8 * LANES)))).reshape(shards, -1, LANES)
    size = jnp.sqrt(jnp.mean(flat_master * flat_master) + step_epsilon)
    weight_terms = jnp.concatenate(
        [
            grad_entry.reshape(shards, 3 * depth, head_cols),
            grad_exit.reshape(head_cols, shards, depth)
            .transpose(1, 0, 2)
            .reshape(shards, depth, head_cols),
        ],
        1,
    )
    first_part, small, weight_terms = barrier(grad_first_part.astype(low), small, weight_terms)
    weight_terms = crossing(weight_terms)
    expand_left, expand_new, grad_first, small_sum = tail(
        first_part,
        small,
        spots[2],
        flat_grad,
        jnp.full((8, LANES), matrix_rate * size, jnp.float32),
        expert_in_left,
        expert_in_right,
        flat_master,
    )
    grad_first, weight_terms = barrier(grad_first, weight_terms)
    owned = jnp.sum(weight_terms.astype(jnp.float32), 0)
    owned_in = owned[: 3 * depth].reshape(depth, 3, head_cols).transpose(1, 0, 2)
    owned_out = owned[3 * depth :].reshape(head_cols, depth)
    grad_tokens = grad_middle + pull(grad_first.astype(jnp.float32))[0]

    def small_piece(number, shape):
        count = 1
        for extent in shape:
            count *= extent
        return small_sum[spots[number] : spots[number + 1]].reshape(-1)[:count].reshape(shape)

    owned_router = small_piece(0, (depth, experts))
    owned_gains = small_piece(1, (2, depth))
    owned_table = small_piece(2, (table_size, local_heads))
    peaks = small_piece(3, (local_heads,))
    in_left, in_right, in_new = jax.vmap(precondition)(
        owned_in,
        attention_in,
        jnp.swapaxes(attention_in_left, 0, 1),
        jnp.swapaxes(attention_in_right, 0, 1),
    )
    column = jnp.sqrt(jnp.repeat(clip_level / jnp.maximum(peaks, clip_level), DH))
    in_new = in_new * jnp.stack([column, column, jnp.ones_like(column)])[:, None, :]
    out_left, out_right, out_new = precondition(
        owned_out, attention_out, attention_out_left, attention_out_right
    )
    router_moment_new, router_new = adapt(owned_router, router_moment, router, router_rate)
    gains_moment_new, gains_new = adapt(owned_gains, gains_moment, gains, gain_rate)
    table_moment_new, table_new = adapt(owned_table, table_moment, bias_table, table_rate)
    return (
        result,
        grad_tokens,
        owned_in,
        in_new,
        in_left,
        in_right,
        owned_out,
        out_new,
        out_left,
        out_right,
        grad_expand_in.transpose(2, 0, 1)[None],
        expand_new.reshape(2, -1, width).transpose(2, 0, 1)[None],
        expand_left,
        expand_right,
        grad_expand_out[None],
        shrink_new[None],
        shrink_left,
        shrink_right,
        owned_router,
        router_moment_new,
        router_new,
        owned_gains,
        gains_moment_new,
        gains_new,
        owned_table,
        table_moment_new,
        table_new,
    )


def solution(mesh):
    placed = (
        P(("fsdp", "ctx"), None),
        P(("fsdp", "ctx"), None),
        P(("fsdp", "ctx"), None),
        P(),
        P(None, ("fsdp", "ctx"), "tp"),
        P("tp", ("fsdp", "ctx")),
        P(("fsdp", "ctx"), None),
        P(None, ("fsdp", "ctx")),
        P(("fsdp", "ctx"), "tp"),
        P(("fsdp", "ctx"), None, None, "tp"),
        P(("fsdp", "ctx"), "tp", None),
        P(None, None, ("fsdp", "ctx", "tp"), None),
        P(None, None, ("fsdp", "ctx", "tp"), None),
        P(None, ("fsdp", "ctx", "tp"), None),
        P(None, ("fsdp", "ctx", "tp"), None),
        P(None, ("fsdp", "ctx", "tp"), None),
        P(None, ("fsdp", "ctx", "tp"), None),
        P(None, ("fsdp", "ctx", "tp"), None),
        P(None, ("fsdp", "ctx", "tp"), None),
        P(("fsdp", "ctx"), None),
        P(None, ("fsdp", "ctx")),
        P(("fsdp", "ctx"), "tp"),
    )
    return jax.shard_map(
        on_device,
        mesh=mesh,
        in_specs=placed,
        out_specs=(
            P(("fsdp", "ctx"), None),
            P(("fsdp", "ctx"), None),
            P(None, ("fsdp", "ctx"), "tp"),
            P(None, ("fsdp", "ctx"), "tp"),
            P(None, ("fsdp", "ctx", "tp"), None),
            P(None, ("fsdp", "ctx", "tp"), None),
            P("tp", ("fsdp", "ctx")),
            P("tp", ("fsdp", "ctx")),
            P(("fsdp", "ctx", "tp"), None),
            P(("fsdp", "ctx", "tp"), None),
            P(("fsdp", "ctx"), None, None, "tp"),
            P(("fsdp", "ctx"), None, None, "tp"),
            P(("fsdp", "ctx", "tp"), None),
            P(("fsdp", "ctx", "tp"), None),
            P(("fsdp", "ctx"), "tp", None),
            P(("fsdp", "ctx"), "tp", None),
            P(("fsdp", "ctx", "tp"), None),
            P(("fsdp", "ctx", "tp"), None),
            P(("fsdp", "ctx"), None),
            P(("fsdp", "ctx"), None),
            P(("fsdp", "ctx"), None),
            P(None, ("fsdp", "ctx")),
            P(None, ("fsdp", "ctx")),
            P(None, ("fsdp", "ctx")),
            P(("fsdp", "ctx"), "tp"),
            P(("fsdp", "ctx"), "tp"),
            P(("fsdp", "ctx"), "tp"),
        ),
        check_vma=False,
    )
```
